32 devices in a mesh: dp: 16 (over z, y, x), col: 2 (over core).
Axes of the slice: x: 2, y: 2, z: 4, core: 2. Of those that a mesh axis runs over, the one named last changes fastest.
Arguments:
- gradients: bfloat16 [16, 6, 512, 2048], P('dp', None, None, 'col')
- momentum: float32 [6, 512, 2048], P(None, 'dp', 'col'), may hold values from -48 to 48
- master: float32 [6, 512, 2048], P(None, 'dp', 'col'), may hold values from -0.125 to 0.125
- owners: int32 [6], replicated, may hold values from 0 to 15, as said below
Outputs:
- new_weights: bfloat16 [6, 512, 2048], P(None, None, 'col')
- new_master: float32 [6, 512, 2048], P(None, 'dp', 'col')
- new_momentum: float32 [6, 512, 2048], P(None, 'dp', 'col')
- owned_updates: bfloat16 [16, 2, 512, 2048], P('dp', None, None, 'col')
- owned_rms: float32 [16, 2], P('dp')
The draws below stay inside these ranges and needn't reach their ends.
Inputs may be any that keep to these rules, and one draw needn't show every extreme that they name: `owners`: no owner index appears more than 2 times, and exactly one appears 2 times.
All inputs are finite; a program needn't handle non-finite values.
Results may differ from the reference program's by a relative error of at most 0.04.
Values may be sent and summed in bfloat16 or wider, within the bound.
No kernel may reach another device: no remote copies, remote signals or barrier semaphores. Data moves between devices by JAX's collectives and lax.ppermute only.
A program may use at most 64 MiB of HBM per device.

```python
import math
import jax
import jax.numpy as jnp
from jax import lax

KV = 512
D = 2048
NM = 6
NS_STEPS = 3
MOST = 2
N_DP = 16
N_COL = 2


def draw_gradients(key, part):
    key = jax.random.fold_in(key, 11)
    key_base, key_rows, key_cols = jax.random.split(key, 3)
    row_scale = jnp.exp(jax.random.uniform(key_rows, (1, NM, KV, 1), jnp.float32, 0.0, math.log(10.0)))
    col_scale = jnp.exp(jax.random.uniform(key_cols, (1, NM, 1, D), jnp.float32, 0.0, math.log(10.0)))
    replica = 1.0 + 2.0 * jnp.arange(N_DP, dtype=jnp.float32).reshape(N_DP, 1, 1, 1) / max(N_DP - 1, 1)
    position = jnp.arange(D, dtype=jnp.float32).reshape(1, 1, 1, D) / max(D - 1, 1)
    ramp = 1.0 + 2.0 * position
    base = jax.random.normal(key_base, (N_DP, NM, KV, D), jnp.float32)
    return (0.1 * base * row_scale * col_scale * ramp * replica).astype(jnp.bfloat16)


def draw_owners(key, part):
    key = jax.random.fold_in(key, 23)
    key_ids, key_pick, key_order = jax.random.split(key, 3)
    middle = jax.random.permutation(key_ids, N_DP - 2)[:NM - 3].astype(jnp.int32) + 1
    ends = jnp.array([0, N_DP - 1], dtype=jnp.int32)
    distinct = jnp.concatenate([ends, middle])
    which = jax.random.randint(key_pick, (1,), 0, NM - 1)
    extra = jnp.take(distinct, which)
    listed = jnp.concatenate([extra, distinct])
    return jax.random.permutation(key_order, listed).astype(jnp.int32)


def level_of(own_key, extent, cuts, low, top_value):
    def one(axis_at, blocks):
        heights = jax.random.uniform(jax.random.fold_in(jax.random.fold_in(own_key, 6), axis_at), (blocks,), jnp.float32, low / len(cuts), top_value / len(cuts))
        return jnp.repeat(jnp.exp(heights), extent[axis_at] // blocks).reshape((-1,) + (1,) * (len(extent) - axis_at - 1))

    gain = one(*cuts[0])
    for cut in cuts[1:]:
        gain = gain * one(*cut)
    return gain


def bell_draw(own_key, dims, spread, bound, cuts=(), held_as=jnp.bfloat16):
    loudness = level_of(own_key, dims, cuts, -0.22, 0.18) if cuts else 1.0
    values = jax.random.normal(own_key, dims, jnp.float32) * spread * loudness
    return jnp.minimum(jnp.maximum(values, -bound), bound).astype(held_as)


def setup_inputs(seed: int = 0) -> dict:
    seeds = jax.random.split(jax.random.key(seed), 5)
    gradients = draw_gradients(jax.random.fold_in(seeds[4], 71), 0)
    momentum = bell_draw(seeds[1], (NM, KV, D), 8.0, 48.0, ((1, 16), (2, 2)), jnp.float32)
    master = bell_draw(seeds[2], (NM, KV, D), D ** -0.5, 0.125, ((1, 16), (2, 2)), jnp.float32)
    owners = draw_owners(jax.random.fold_in(seeds[4], 71), 0)
    return dict(gradients=gradients, momentum=momentum, master=master, owners=owners)


quintic_first = 3.4445
quintic_second = -4.775
quintic_third = 2.0315
momentum_decay = 0.95
learn_rate = 0.3
weight_decay = 0.1
epsilon = 1e-07

def orthogonalize(update):
    squares = jnp.sum(jnp.square(update.astype(jnp.float32)))
    iterate = (update.astype(jnp.float32) / (jnp.sqrt(squares) + epsilon)).astype(jnp.bfloat16)
    col_width = D // N_COL
    for iteration in range(NS_STEPS):
        blocks = iterate.astype(jnp.float32).reshape(KV, N_COL, col_width)
        partial_value = jnp.einsum('icw,jcw->cij', blocks, blocks)
        rounded = lax.optimization_barrier(partial_value.astype(jnp.bfloat16))
        gram_sum = lax.optimization_barrier(jnp.sum(rounded.astype(jnp.float32), axis=0))
        gram_half = gram_sum.astype(jnp.bfloat16)
        square = jnp.dot(gram_half, gram_half, preferred_element_type=jnp.float32)
        mixing = (quintic_second * gram_sum + quintic_third * square).astype(jnp.bfloat16)
        iterate = (quintic_first * iterate.astype(jnp.float32) + jnp.dot(mixing, iterate, preferred_element_type=jnp.float32)).astype(jnp.bfloat16)
    factor = 0.2 * math.sqrt(max(KV, D))
    return (factor * iterate.astype(jnp.float32)).astype(jnp.bfloat16)

def reference(gradients, momentum, master, owners):

    def accumulate(index, running):
        return running + lax.dynamic_index_in_dim(gradients, index, 0, keepdims=False).astype(jnp.float32)
    summed = lax.fori_loop(0, N_DP, accumulate, jnp.zeros((NM, KV, D), jnp.float32))
    new_momentum = momentum_decay * momentum + summed
    update = (summed + momentum_decay * new_momentum).astype(jnp.bfloat16)
    squares = lax.optimization_barrier(jnp.sum(jnp.square(update.astype(jnp.float32)), axis=(1, 2)))
    matrix_rms = jnp.sqrt(squares / float(KV * D))
    scaled = lax.map(orthogonalize, update)
    new_master = master * (1.0 - learn_rate * weight_decay) - learn_rate * scaled.astype(jnp.float32)
    new_weights = new_master.astype(jnp.bfloat16)
    matches = owners[:, None] == owners[None, :]
    earlier = jnp.arange(NM, dtype=jnp.int32)[None, :] < jnp.arange(NM, dtype=jnp.int32)[:, None]
    slot_index = lax.optimization_barrier(jnp.sum((matches & earlier).astype(jnp.int32), axis=1)).astype(jnp.int32)
    target = owners * MOST + slot_index
    picker = (jnp.arange(N_DP * MOST, dtype=jnp.int32)[:, None] == target[None, :]).astype(jnp.float32)
    owned_updates = jnp.einsum('sm,mkd->skd', picker, scaled.astype(jnp.float32)).astype(jnp.bfloat16)
    owned_updates = owned_updates.reshape(N_DP, MOST, KV, D)
    owned_rms = lax.optimization_barrier(jnp.sum(picker * matrix_rms[None, :], axis=1)).reshape(N_DP, MOST)
    return (new_weights, new_master, new_momentum, owned_updates, owned_rms)
```

```python
import functools
import math

import jax
import jax.numpy as jnp
from jax import lax
from jax.experimental import pallas as pl
from jax.experimental.pallas import tpu as pltpu
from jax.sharding import PartitionSpec as P

KV = 512
D = 2048
MOST = 2

quintic_first = 3.4445
quintic_second = -4.775
quintic_third = 2.0315
momentum_decay = 0.95
learn_rate = 0.3
weight_decay = 0.1
epsilon = 1e-07
factor = 0.2 * math.sqrt(max(KV, D))

VMEM_LIMIT = 56 * 1024 * 1024


def dot(left, right):
    return jnp.dot(left, right, preferred_element_type=jnp.float32)


def gram_kernel(update_ref, gram_ref):
    for index in range(update_ref.shape[0]):
        block = update_ref[index]
        gram = lax.dot_general(
            block, block, (((1,), (1,)), ((), ())), preferred_element_type=jnp.float32
        )
        gram_ref[index] = gram.astype(jnp.bfloat16)


def grams(update):
    count, rows, width = update.shape
    return pl.pallas_call(
        gram_kernel,
        grid=(count,),
        in_specs=[pl.BlockSpec((1, rows, width), lambda i: (i, 0, 0))],
        out_specs=pl.BlockSpec((1, rows, rows), lambda i: (i, 0, 0)),
        out_shape=jax.ShapeDtypeStruct((count, rows, rows), jnp.bfloat16),
        compiler_params=pltpu.CompilerParams(vmem_limit_bytes=VMEM_LIMIT),
        cost_estimate=pl.CostEstimate(
            flops=2 * count * rows * rows * width,
            bytes_accessed=2 * count * rows * (width + rows),
            transcendentals=0,
        ),
    )(update)


def half(value):
    return value.astype(jnp.bfloat16)


def mixers(grams_now):
    return [
        quintic_second * gram + quintic_third * dot(half(gram), half(gram)) for gram in grams_now
    ]


def next_grams(grams_now, mixes):
    lefts = [
        quintic_first * gram + dot(half(mix), half(gram)) for gram, mix in zip(grams_now, mixes)
    ]
    return [quintic_first * left + dot(half(left), half(mix)) for left, mix in zip(lefts, mixes)]


def newton_kernel(parts, *refs):
    gram_refs = refs[:parts]
    update_ref, master_ref, scaled_ref, weights_ref, squares_ref = refs[parts:]
    each = range(update_ref.shape[0])
    rows = update_ref.shape[1]
    on_diagonal = lax.broadcasted_iota(jnp.int32, (rows, rows), 0) == lax.broadcasted_iota(
        jnp.int32, (rows, rows), 1
    )
    grams_now = []
    inverses = []
    for index in each:
        gram = gram_refs[0][index].astype(jnp.float32)
        for ref in gram_refs[1:]:
            gram = gram + ref[index].astype(jnp.float32)
        diagonal = jnp.where(on_diagonal, gram, 0.0)
        squares = jnp.sum(jnp.sum(diagonal, axis=0, keepdims=True), axis=1, keepdims=True)
        squares_ref[index] = jnp.broadcast_to(squares, squares_ref.shape[1:])
        inverse = 1.0 / (jnp.sqrt(squares) + epsilon)
        grams_now.append(gram * inverse * inverse)
        inverses.append(inverse)
    first = mixers(grams_now)
    grams_now = next_grams(grams_now, first)
    second = mixers(grams_now)
    grams_now = next_grams(grams_now, second)
    third = mixers(grams_now)
    pairs = [
        quintic_first * (m0 + m1) + dot(half(m1), half(m0)) for m0, m1 in zip(first, second)
    ]
    wholes = [
        quintic_first * pair + quintic_first**2 * m2 + dot(half(m2), half(pair))
        for pair, m2 in zip(pairs, third)
    ]
    for index in each:
        block = update_ref[index]
        product = quintic_first**3 * block.astype(jnp.float32) + dot(half(wholes[index]), block)
        scaled = half(product * (factor * inverses[index]))
        scaled_ref[index] = scaled
        weights_ref[index] = half(
            master_ref[index].astype(jnp.float32) * (1.0 - learn_rate * weight_decay)
            - learn_rate * scaled.astype(jnp.float32)
        )


def newton(gram_parts, update, master):
    count, rows, width = update.shape
    step = 2 if count % 2 == 0 else 1

    def spec(minor):
        return pl.BlockSpec((step, rows, minor), lambda i: (i, 0, 0))

    parts = len(gram_parts)
    return pl.pallas_call(
        functools.partial(newton_kernel, parts),
        grid=(count // step,),
        in_specs=[spec(rows)] * parts + [spec(width)] * 2,
        out_specs=[
            spec(width),
            spec(width),
            pl.BlockSpec((step, 8, 128), lambda i: (i, 0, 0)),
        ],
        out_shape=[
            jax.ShapeDtypeStruct(update.shape, jnp.bfloat16),
            jax.ShapeDtypeStruct(update.shape, jnp.bfloat16),
            jax.ShapeDtypeStruct((count, 8, 128), jnp.float32),
        ],
        compiler_params=pltpu.CompilerParams(vmem_limit_bytes=VMEM_LIMIT),
        cost_estimate=pl.CostEstimate(
            flops=2 * count * rows * rows * (9 * rows + width),
            bytes_accessed=2 * count * rows * (4 * width + parts * rows),
            transcendentals=0,
        ),
    )(*gram_parts, update, master)


def per_device(gradients, momentum, master, owners):
    me = lax.axis_index("dp")
    matrices, row_count, _ = momentum.shape
    master_all = lax.all_gather(master.astype(jnp.bfloat16), "dp", axis=1, tiled=True)
    summed = lax.psum_scatter(gradients[0], "dp", scatter_dimension=1, tiled=True)
    summed = summed.astype(jnp.float32)
    new_momentum = momentum_decay * momentum + summed
    update = (summed + momentum_decay * new_momentum).astype(jnp.bfloat16)
    update = lax.all_gather(update, "dp", axis=1, tiled=True)

    partial_gram = grams(update)
    if lax.axis_size("col") == 2:
        gram_parts = [partial_gram, lax.ppermute(partial_gram, "col", [(0, 1), (1, 0)])]
    else:
        gram_parts = [lax.psum(partial_gram, "col")]
    scaled, new_weights, squares = newton(gram_parts, update, master_all)

    mine = lax.dynamic_slice_in_dim(scaled, me * row_count, row_count, axis=1)
    new_master = master * (1.0 - learn_rate * weight_decay) - learn_rate * mine.astype(jnp.float32)

    held = owners == me
    rank = jnp.cumsum(held.astype(jnp.int32)) - 1
    rms = jnp.sqrt(squares[:, 0, 0] / float(KV * D))
    owned_updates = []
    owned_rms = []
    for slot in range(MOST):
        here = held & (rank == slot)
        matrix = jnp.argmax(here).astype(jnp.int32)
        found = jnp.any(here)
        chosen = lax.dynamic_index_in_dim(scaled, matrix, axis=0, keepdims=False)
        owned_updates.append(jnp.where(found, chosen, jnp.zeros_like(chosen)))
        owned_rms.append(jnp.sum(jnp.where(here, rms, 0.0)))
    owned_updates = jnp.stack(owned_updates)[None]
    owned_rms = jnp.stack(owned_rms)[None]
    return (new_weights, new_master, new_momentum, owned_updates, owned_rms)


def solution(mesh):
    return jax.shard_map(
        per_device,
        mesh=mesh,
        in_specs=(P("dp", None, None, "col"), P(None, "dp", "col"), P(None, "dp", "col"), P()),
        out_specs=(
            P(None, None, "col"),
            P(None, "dp", "col"),
            P(None, "dp", "col"),
            P("dp", None, None, "col"),
            P("dp", None),
        ),
        check_vma=False,
    )
```

```python
import functools
import math

import jax
import jax.numpy as jnp
from jax import lax
from jax.experimental import pallas as pl
from jax.experimental.pallas import tpu as pltpu
from jax.sharding import PartitionSpec as P

KV = 512
D = 2048
MOST = 2

quintic_first = 3.4445
quintic_second = -4.775
quintic_third = 2.0315
momentum_decay = 0.95
learn_rate = 0.3
weight_decay = 0.1
epsilon = 1e-07
factor = 0.2 * math.sqrt(max(KV, D))

VMEM_LIMIT = 56 * 1024 * 1024
GROUPS = 1
LINE = 4


def dot(left, right):
    return jnp.dot(left, right, preferred_element_type=jnp.float32)


def half(value):
    return value.astype(jnp.bfloat16)


def gram_kernel(*refs):
    piece_refs, (update_ref, gram_ref) = refs[:-2], refs[-2:]
    start = 0
    for ref in piece_refs:
        rows = ref.shape[1]
        update_ref[0, start : start + rows] = ref[0]
        start += rows
    block = update_ref[0]
    gram = lax.dot_general(
        block, block, (((1,), (1,)), ((), ())), preferred_element_type=jnp.float32
    )
    gram_ref[0] = half(gram)


def grams(pieces):
    count, _, width = pieces[0].shape
    rows = sum(piece.shape[1] for piece in pieces)

    def spec(height, minor):
        return pl.BlockSpec((1, height, minor), lambda i: (i, 0, 0))

    return pl.pallas_call(
        gram_kernel,
        grid=(count,),
        in_specs=[spec(piece.shape[1], width) for piece in pieces],
        out_specs=[spec(rows, width), spec(rows, rows)],
        out_shape=[
            jax.ShapeDtypeStruct((count, rows, width), jnp.bfloat16),
            jax.ShapeDtypeStruct((count, rows, rows), jnp.bfloat16),
        ],
        compiler_params=pltpu.CompilerParams(vmem_limit_bytes=VMEM_LIMIT),
        cost_estimate=pl.CostEstimate(
            flops=2 * count * rows * rows * width,
            bytes_accessed=2 * count * rows * (2 * width + rows),
            transcendentals=0,
        ),
    )(*pieces)


def mixers(grams_now):
    return [
        quintic_second * gram + quintic_third * dot(half(gram), half(gram)) for gram in grams_now
    ]


def next_grams(grams_now, mixes):
    lefts = [
        quintic_first * gram + dot(half(mix), half(gram)) for gram, mix in zip(grams_now, mixes)
    ]
    return [quintic_first * left + dot(half(left), half(mix)) for left, mix in zip(lefts, mixes)]


def newton_kernel(parts, blocks, first_matrix, places_ref, slots_ref, *refs):
    gram_refs = refs[:parts]
    update_ref, master_ref, rows_ref, owned_in_ref, rms_in_ref = refs[parts : parts + 5]
    weights_ref, new_rows_ref, owned_ref, rms_ref = refs[-4:]
    count = update_ref.shape[0]
    each = range(count)
    rows = update_ref.shape[1]
    height = rows // blocks
    at = pl.program_id(0)

    @pl.when(at == 0)
    def _():
        owned_ref[...] = owned_in_ref[...]
        rms_ref[...] = rms_in_ref[...]

    on_diagonal = lax.broadcasted_iota(jnp.int32, (rows, rows), 0) == lax.broadcasted_iota(
        jnp.int32, (rows, rows), 1
    )
    lane = lax.broadcasted_iota(jnp.int32, rms_ref.shape, 1)
    grams_now = []
    inverses = []
    for index in each:
        slot = slots_ref[first_matrix + at * count + index]
        gram = gram_refs[0][index].astype(jnp.float32)
        for ref in gram_refs[1:]:
            gram = gram + ref[index].astype(jnp.float32)
        diagonal = jnp.where(on_diagonal, gram, 0.0)
        squares = jnp.sum(jnp.sum(diagonal, axis=0, keepdims=True), axis=1, keepdims=True)
        rms_ref[...] = jnp.where(lane == slot, jnp.sqrt(squares / float(KV * D)), rms_ref[...])
        inverse = 1.0 / (jnp.sqrt(squares) + epsilon)
        grams_now.append(gram * inverse * inverse)
        inverses.append(inverse)
    first = mixers(grams_now)
    grams_now = next_grams(grams_now, first)
    second = mixers(grams_now)
    grams_now = next_grams(grams_now, second)
    third = mixers(grams_now)
    pairs = [
        quintic_first * (m0 + m1) + dot(half(m1), half(m0)) for m0, m1 in zip(first, second)
    ]
    wholes = [
        quintic_first * pair + quintic_first**2 * m2 + dot(half(m2), half(pair))
        for pair, m2 in zip(pairs, third)
    ]
    for index in each:
        slot = slots_ref[first_matrix + at * count + index]
        block = update_ref[index]
        product = quintic_first**3 * block.astype(jnp.float32) + dot(half(wholes[index]), block)
        scaled = half(product * (factor * inverses[index]))
        decayed = rows_ref[index] * (1.0 - learn_rate * weight_decay)
        new_rows_ref[index] = decayed - learn_rate * scaled[:height].astype(jnp.float32)
        for block_at in range(blocks):
            place = pl.ds(pl.multiple_of(places_ref[block_at] * height, height), height)
            piece = scaled[block_at * height : (block_at + 1) * height]
            weights_ref[index, place] = half(
                master_ref[index, place].astype(jnp.float32) * (1.0 - learn_rate * weight_decay)
                - learn_rate * piece.astype(jnp.float32)
            )

            @pl.when(slot >= 0)
            def _():
                owned_ref[jnp.maximum(slot, 0), place] = piece


def newton(places, slots, gram_parts, update, master_all, master, state, first_matrix):
    count, rows, width = update.shape
    matrices, row_count, _ = master.shape
    blocks = places.shape[0]
    step = 2 if count % 2 == 0 else 1
    offset = first_matrix // step
    parts = len(gram_parts)

    def spec(height, minor, shift=0):
        return pl.BlockSpec((step, height, minor), lambda i, *_: (i + shift, 0, 0))

    def still(shape):
        return pl.BlockSpec(shape, lambda i, *_: (0,) * len(shape))

    weights, new_master, owned, rms = state
    inputs = [*gram_parts, update, master_all, master, owned, rms]
    in_specs = [spec(rows, rows)] * parts + [
        spec(rows, width),
        spec(rows, width, offset),
        spec(row_count, width, offset),
        still(owned.shape),
        still(rms.shape),
    ]
    aliases = {}
    if weights is not None:
        aliases = {2 + len(inputs): 0, 3 + len(inputs): 1}
        inputs += [weights, new_master]
        in_specs += [pl.BlockSpec(memory_space=pl.ANY)] * 2
    return pl.pallas_call(
        functools.partial(newton_kernel, parts, blocks, first_matrix),
        grid_spec=pltpu.PrefetchScalarGridSpec(
            num_scalar_prefetch=2,
            grid=(count // step,),
            in_specs=in_specs,
            out_specs=[
                spec(rows, width, offset),
                spec(row_count, width, offset),
                still(owned.shape),
                still(rms.shape),
            ],
        ),
        out_shape=[
            jax.ShapeDtypeStruct((matrices, rows, width), jnp.bfloat16),
            jax.ShapeDtypeStruct(master.shape, jnp.float32),
            jax.ShapeDtypeStruct(owned.shape, jnp.bfloat16),
            jax.ShapeDtypeStruct(rms.shape, jnp.float32),
        ],
        input_output_aliases=aliases,
        compiler_params=pltpu.CompilerParams(vmem_limit_bytes=VMEM_LIMIT),
        cost_estimate=pl.CostEstimate(
            flops=2 * count * rows * rows * (9 * rows + width),
            bytes_accessed=2 * count * rows * (4 * width + parts * rows),
            transcendentals=0,
        ),
    )(places, slots, *inputs)


class Grid:
    def __init__(self, count):
        self.count = count
        self.me = lax.axis_index("dp")
        self.x_pairs = [(d, d ^ 1) for d in range(count)]
        self.y_pairs = [(d, d ^ 2) for d in range(count)]

    def place(self, dx, dy, dz):
        z = (self.me // 4 + dz) % LINE
        return z * 4 + ((self.me % 4) ^ (2 * dy + dx))

    def over_x(self, value):
        return lax.ppermute(value, "dp", self.x_pairs)

    def over_y(self, value):
        return lax.ppermute(value, "dp", self.y_pairs)

    def over_z(self, value, shift):
        pairs = [(d, (d // 4 + shift) % LINE * 4 + d % 4) for d in range(self.count)]
        return lax.ppermute(value, "dp", pairs)


def reduce_scatter(grid, terms, row_count):
    def term(dx, dy, dz):
        start = grid.place(dx, dy, dz) * row_count
        return lax.dynamic_slice_in_dim(terms, start, row_count, axis=1)

    def added(*values):
        return sum(value.astype(jnp.float32) for value in values)

    far = {}
    for dz in range(LINE):
        if dz < LINE // 2:
            far[dz] = grid.over_x(term(1, 1, dz))
        else:
            far[dz] = grid.over_y(term(1, 1, dz))
    near = {}
    for dz in reversed(range(LINE)):
        along_y, along_x = term(0, 1, dz), term(1, 0, dz)
        if dz < LINE // 2:
            along_y = half(added(along_y, far[dz]))
        else:
            along_x = half(added(along_x, far[dz]))
        near[dz] = added(term(0, 0, dz), grid.over_y(along_y), grid.over_x(along_x))
    return near[0] + added(*[grid.over_z(half(near[dz]), dz) for dz in range(1, LINE)])


def all_gather(grid, own):
    line = [own] + [grid.over_z(own, LINE - dz) for dz in range(1, LINE)]
    over_x = [grid.over_x(piece) for piece in line]
    over_y = [grid.over_y(piece) for piece in line]
    far = [grid.over_x(piece) for piece in over_y[: LINE // 2]]
    far += [grid.over_y(piece) for piece in over_x[LINE // 2 :]]
    return line + over_y + over_x + far


def relative_places(grid):
    order = [(dx, dy, dz) for dx in range(2) for dy in range(2) for dz in range(LINE)]
    return jnp.stack([grid.place(*place) for place in order]).astype(jnp.int32)


def gathered_grams(pieces):
    update, partial_gram = grams(pieces)
    if lax.axis_size("col") == 2:
        return update, [partial_gram, lax.ppermute(partial_gram, "col", [(0, 1), (1, 0)])]
    return update, [lax.psum(partial_gram, "col")]


def per_device(gradients, momentum, master, owners):
    me = lax.axis_index("dp")
    dp_count = lax.axis_size("dp")
    matrices, row_count, width = momentum.shape
    terms = gradients[0]
    by_pieces = dp_count == 4 * LINE and row_count % 32 == 0
    master_all = lax.all_gather(half(master), "dp", axis=1, tiled=True)

    held = owners == me
    rank = jnp.sum(held[None, :] & (jnp.arange(matrices)[None, :] < jnp.arange(matrices)[:, None]), axis=1)
    slots = jnp.where(held, rank, -1).astype(jnp.int32)
    if by_pieces:
        grid = Grid(dp_count)
        places = relative_places(grid)
    else:
        places = jnp.zeros((1,), jnp.int32)

    size = matrices // GROUPS
    state = (
        None,
        None,
        jnp.zeros((MOST, terms.shape[1], width), jnp.bfloat16),
        jnp.zeros((8, 128), jnp.float32),
    )
    momenta = []
    for first_matrix in range(0, matrices, size):
        chosen = slice(first_matrix, first_matrix + size)
        if by_pieces:
            summed = reduce_scatter(grid, terms[chosen], row_count)
        else:
            summed = lax.psum_scatter(terms[chosen], "dp", scatter_dimension=1, tiled=True)
            summed = summed.astype(jnp.float32)
        new_momentum = momentum_decay * momentum[chosen] + summed
        momenta.append(new_momentum)
        update = half(summed + momentum_decay * new_momentum)
        if by_pieces:
            pieces = all_gather(grid, update)
        else:
            pieces = [lax.all_gather(update, "dp", axis=1, tiled=True)]
        update, gram_parts = gathered_grams(pieces)
        rows = master
        if not by_pieces:
            rows = jnp.zeros((matrices, terms.shape[1], width), jnp.float32)
            rows = lax.dynamic_update_slice_in_dim(rows, master, me * row_count, axis=1)
        state = newton(places, slots, gram_parts, update, master_all, rows, state, first_matrix)
    new_weights, new_master, owned_updates, rms = state
    if not by_pieces:
        new_master = lax.dynamic_slice_in_dim(new_master, me * row_count, row_count, axis=1)
    new_momentum = momenta[0] if len(momenta) == 1 else jnp.concatenate(momenta)
    return (new_weights, new_master, new_momentum, owned_updates[None], rms[:1, :MOST])


def solution(mesh):
    return jax.shard_map(
        per_device,
        mesh=mesh,
        in_specs=(P("dp", None, None, "col"), P(None, "dp", "col"), P(None, "dp", "col"), P()),
        out_specs=(
            P(None, None, "col"),
            P(None, "dp", "col"),
            P(None, "dp", "col"),
            P("dp", None, None, "col"),
            P("dp", None),
        ),
        check_vma=False,
    )
```

```python
import functools
import math

import jax
import jax.numpy as jnp
from jax import lax
from jax.experimental import pallas as pl
from jax.experimental.pallas import tpu as pltpu
from jax.sharding import PartitionSpec as P

KV = 512
D = 2048
MOST = 2

quintic_first = 3.4445
quintic_second = -4.775
quintic_third = 2.0315
momentum_decay = 0.95
learn_rate = 0.3
weight_decay = 0.1
epsilon = 1e-07
factor = 0.2 * math.sqrt(max(KV, D))

VMEM_LIMIT = 56 * 1024 * 1024
GROUPS = 3
LINE = 4


def dot(left, right):
    return jnp.dot(left, right, preferred_element_type=jnp.float32)


def half(value):
    return value.astype(jnp.bfloat16)


def gram_kernel(*refs):
    piece_refs, (update_ref, gram_ref) = refs[:-2], refs[-2:]
    start = 0
    for ref in piece_refs:
        rows = ref.shape[2]
        for index in range(ref.shape[0]):
            update_ref[0, start : start + rows] = ref[index, 0]
            start += rows
    block = update_ref[0]
    gram = lax.dot_general(
        block, block, (((1,), (1,)), ((), ())), preferred_element_type=jnp.float32
    )
    gram_ref[0] = half(gram)


def grams(pieces):
    _, count, _, width = pieces[0].shape
    rows = sum(piece.shape[0] * piece.shape[2] for piece in pieces)

    def spec(minor):
        return pl.BlockSpec((1, rows, minor), lambda i: (i, 0, 0))

    return pl.pallas_call(
        gram_kernel,
        grid=(count,),
        in_specs=[
            pl.BlockSpec((piece.shape[0], 1, *piece.shape[2:]), lambda i: (0, i, 0, 0))
            for piece in pieces
        ],
        out_specs=[spec(width), spec(rows)],
        out_shape=[
            jax.ShapeDtypeStruct((count, rows, width), jnp.bfloat16),
            jax.ShapeDtypeStruct((count, rows, rows), jnp.bfloat16),
        ],
        compiler_params=pltpu.CompilerParams(vmem_limit_bytes=VMEM_LIMIT),
        cost_estimate=pl.CostEstimate(
            flops=2 * count * rows * rows * width,
            bytes_accessed=2 * count * rows * (2 * width + rows),
            transcendentals=0,
        ),
    )(*pieces)


def mixers(grams_now):
    return [
        quintic_second * gram + quintic_third * dot(half(gram), half(gram)) for gram in grams_now
    ]


def next_grams(grams_now, mixes):
    lefts = [
        quintic_first * gram + dot(half(mix), half(gram)) for gram, mix in zip(grams_now, mixes)
    ]
    return [quintic_first * left + dot(half(left), half(mix)) for left, mix in zip(lefts, mixes)]


def newton_kernel(parts, blocks, first_matrix, places_ref, slots_ref, *refs):
    gram_refs = refs[:parts]
    update_ref, master_ref, rows_ref, owned_in_ref, rms_in_ref = refs[parts : parts + 5]
    weights_ref, new_rows_ref, owned_ref, rms_ref = refs[-4:]
    count = update_ref.shape[0]
    each = range(count)
    rows = update_ref.shape[1]
    height = rows // blocks
    at = pl.program_id(0)

    @pl.when(at == 0)
    def _():
        owned_ref[...] = owned_in_ref[...]
        rms_ref[...] = rms_in_ref[...]

    on_diagonal = lax.broadcasted_iota(jnp.int32, (rows, rows), 0) == lax.broadcasted_iota(
        jnp.int32, (rows, rows), 1
    )
    lane = lax.broadcasted_iota(jnp.int32, rms_ref.shape, 1)
    grams_now = []
    inverses = []
    for index in each:
        slot = slots_ref[first_matrix + at * count + index]
        gram = gram_refs[0][index].astype(jnp.float32)
        for ref in gram_refs[1:]:
            gram = gram + ref[index].astype(jnp.float32)
        diagonal = jnp.where(on_diagonal, gram, 0.0)
        squares = jnp.sum(jnp.sum(diagonal, axis=0, keepdims=True), axis=1, keepdims=True)
        rms_ref[...] = jnp.where(lane == slot, jnp.sqrt(squares / float(KV * D)), rms_ref[...])
        inverse = 1.0 / (jnp.sqrt(squares) + epsilon)
        grams_now.append(gram * inverse * inverse)
        inverses.append(inverse)
    first = mixers(grams_now)
    grams_now = next_grams(grams_now, first)
    second = mixers(grams_now)
    grams_now = next_grams(grams_now, second)
    third = mixers(grams_now)
    pairs = [
        quintic_first * (m0 + m1) + dot(half(m1), half(m0)) for m0, m1 in zip(first, second)
    ]
    wholes = [
        quintic_first * pair + quintic_first**2 * m2 + dot(half(m2), half(pair))
        for pair, m2 in zip(pairs, third)
    ]
    for index in each:
        slot = slots_ref[first_matrix + at * count + index]
        block = update_ref[index]
        product = quintic_first**3 * block.astype(jnp.float32) + dot(half(wholes[index]), block)
        scaled = half(product * (factor * inverses[index]))
        decayed = rows_ref[index] * (1.0 - learn_rate * weight_decay)
        new_rows_ref[index] = decayed - learn_rate * scaled[:height].astype(jnp.float32)
        for block_at in range(blocks):
            place = pl.ds(pl.multiple_of(places_ref[block_at] * height, height), height)
            piece = scaled[block_at * height : (block_at + 1) * height]
            weights_ref[index, place] = half(
                master_ref[index, place].astype(jnp.float32) * (1.0 - learn_rate * weight_decay)
                - learn_rate * piece.astype(jnp.float32)
            )

            @pl.when(slot >= 0)
            def _():
                owned_ref[jnp.maximum(slot, 0), place] = piece


def newton(places, slots, gram_parts, update, master_all, master, state, first_matrix):
    count, rows, width = update.shape
    matrices, row_count, _ = master.shape
    blocks = places.shape[0]
    step = 2 if count % 2 == 0 else 1
    offset = first_matrix // step
    parts = len(gram_parts)

    def spec(height, minor, shift=0):
        return pl.BlockSpec((step, height, minor), lambda i, *_: (i + shift, 0, 0))

    def still(shape):
        return pl.BlockSpec(shape, lambda i, *_: (0,) * len(shape))

    weights, new_master, owned, rms = state
    inputs = [*gram_parts, update, master_all, master, owned, rms]
    in_specs = [spec(rows, rows)] * parts + [
        spec(rows, width),
        spec(rows, width, offset),
        spec(row_count, width, offset),
        still(owned.shape),
        still(rms.shape),
    ]
    aliases = {}
    if weights is not None:
        aliases = {2 + len(inputs): 0, 3 + len(inputs): 1}
        inputs += [weights, new_master]
        in_specs += [pl.BlockSpec(memory_space=pl.ANY)] * 2
    return pl.pallas_call(
        functools.partial(newton_kernel, parts, blocks, first_matrix),
        grid_spec=pltpu.PrefetchScalarGridSpec(
            num_scalar_prefetch=2,
            grid=(count // step,),
            in_specs=in_specs,
            out_specs=[
                spec(rows, width, offset),
                spec(row_count, width, offset),
                still(owned.shape),
                still(rms.shape),
            ],
        ),
        out_shape=[
            jax.ShapeDtypeStruct((matrices, rows, width), jnp.bfloat16),
            jax.ShapeDtypeStruct(master.shape, jnp.float32),
            jax.ShapeDtypeStruct(owned.shape, jnp.bfloat16),
            jax.ShapeDtypeStruct(rms.shape, jnp.float32),
        ],
        input_output_aliases=aliases,
        compiler_params=pltpu.CompilerParams(vmem_limit_bytes=VMEM_LIMIT),
        cost_estimate=pl.CostEstimate(
            flops=2 * count * rows * rows * (9 * rows + width),
            bytes_accessed=2 * count * rows * (4 * width + parts * rows),
            transcendentals=0,
        ),
    )(places, slots, *inputs)


class Grid:
    def __init__(self, count):
        self.count = count
        self.me = lax.axis_index("dp")
        self.x_pairs = [(d, d ^ 1) for d in range(count)]
        self.y_pairs = [(d, d ^ 2) for d in range(count)]

    def over_x(self, value):
        return lax.ppermute(value, "dp", self.x_pairs)

    def over_y(self, value):
        return lax.ppermute(value, "dp", self.y_pairs)

    def over_z(self, value, shift):
        pairs = [(d, (d // 4 + shift) % LINE * 4 + d % 4) for d in range(self.count)]
        return lax.ppermute(value, "dp", pairs)


def place(me, dx, dy, dz):
    z = ((me >> 2) + dz) & (LINE - 1)
    return z * 4 + ((me & 3) ^ (2 * dy + dx))


def after(value, *others):
    return lax.optimization_barrier((value, *others))[0]


def added(*values):
    return sum(value.astype(jnp.float32) for value in values)


class Stages:
    def __init__(self, grid, terms, part, row_count):
        self.grid = grid
        self.me = grid.me
        self.terms = terms
        self.part = part
        self.row_count = row_count

    def piece(self, dx, dy, dz):
        first, size = self.part.start, self.part.stop - self.part.start
        start = place(self.me, dx, dy, dz) * self.row_count
        shape = (size, self.row_count, self.terms.shape[2])
        return lax.dynamic_slice(self.terms, (first, start, 0), shape)

    def pieces(self, dx, dy, dzs):
        return jnp.stack([self.piece(dx, dy, dz) for dz in dzs])

    def sum_far(self, *ties):
        first, last = range(LINE // 2), range(LINE // 2, LINE)
        self.me = after(self.me, *ties)
        self.far_x = self.grid.over_x(self.pieces(1, 1, first))
        self.far_y = self.grid.over_y(self.pieces(1, 1, last))

    def sum_near(self, *ties):
        first, last = range(LINE // 2), range(LINE // 2, LINE)
        far_x = after(self.far_x, *ties)
        along_y = [half(added(self.pieces(0, 1, first), far_x)), self.pieces(0, 1, last)]
        along_x = [self.pieces(1, 0, first), half(added(self.pieces(1, 0, last), self.far_y))]
        self.near_y = self.grid.over_y(jnp.concatenate(along_y))
        self.near_x = self.grid.over_x(jnp.concatenate(along_x))

    def sum_line(self, *ties):
        near_x = after(self.near_x, *ties)
        near = [
            added(self.piece(0, 0, dz), near_x[dz], self.near_y[dz]) for dz in range(LINE)
        ]
        self.line_sums = [near[0]]
        self.line_sums += [self.grid.over_z(half(near[dz]), dz) for dz in range(1, LINE)]

    def summed(self):
        return added(*self.line_sums)

    def gather_line(self, own, *ties):
        own = after(own, *ties)
        self.line = [own] + [self.grid.over_z(own, LINE - dz) for dz in range(1, LINE)]

    def gather_near(self, *ties):
        self.stacked = after(jnp.stack(self.line), *ties)
        self.all_x = self.grid.over_x(self.stacked)
        self.all_y = self.grid.over_y(self.stacked)

    def gather_far(self, *ties):
        all_x = after(self.all_x, *ties)
        self.corner_x = self.grid.over_x(self.all_y[: LINE // 2])
        self.corner_y = self.grid.over_y(all_x[LINE // 2 :])

    def gathered(self):
        line = [piece[None] for piece in self.line]
        return [*line, self.all_y, self.all_x, self.corner_x, self.corner_y]


def relative_places(grid):
    order = [(dx, dy, dz) for dx in range(2) for dy in range(2) for dz in range(LINE)]
    return jnp.stack([place(grid.me, *where) for where in order]).astype(jnp.int32)


def gathered_grams(pieces):
    update, partial_gram = grams(pieces)
    if lax.axis_size("col") == 2:
        return update, [partial_gram, lax.ppermute(partial_gram, "col", [(0, 1), (1, 0)])]
    return update, [lax.psum(partial_gram, "col")]


def updated(summed, momentum):
    new_momentum = momentum_decay * momentum + summed
    return new_momentum, half(summed + momentum_decay * new_momentum)


def by_pieces(terms, momentum, chosen, newton_step):
    grid = Grid(lax.axis_size("dp"))
    row_count = momentum.shape[1]
    groups = [Stages(grid, terms, part, row_count) for part in chosen]
    momenta = []

    def finish_sum(at):
        new_momentum, own = updated(groups[at].summed(), momentum[chosen[at]])
        momenta.append(new_momentum)
        groups[at].gather_line(own)

    for at, group in enumerate(groups):
        before = groups[at - 1] if at else None
        group.sum_far(*([before.near_x, before.near_y] if at else []))
        group.sum_near()
        group.sum_line(*(before.line[1:] if at else []))
        finish_sum(at)
    parts = []
    done = []
    for at, group in enumerate(groups):
        before = groups[at - 1] if at else None
        group.gather_near(
            *([before.corner_x, before.corner_y] if at else [groups[-1].near_x, groups[-1].near_y]),
            *(groups[-1].line_sums[1:] if at == 1 else []),
        )
        if at >= 2:
            done.append(newton_step(at - 2, *parts[at - 2], group.stacked))
        group.gather_far(*done[-1:])
        pieces = group.gathered()
        if at == len(groups) - 1 and at >= 1:
            done.append(newton_step(at - 1, *parts[at - 1]))
            pieces[0] = after(pieces[0], done[-1])
        parts.append(gathered_grams(pieces))
    newton_step(len(groups) - 1, *parts[-1])
    return momenta


def per_device(gradients, momentum, master, owners):
    me = lax.axis_index("dp")
    dp_count = lax.axis_size("dp")
    matrices, row_count, width = momentum.shape
    terms = gradients[0]
    master_all = lax.all_gather(half(master), "dp", axis=1, tiled=True)

    held = owners == me
    order = jnp.arange(matrices)
    rank = jnp.sum(held[None, :] & (order[None, :] < order[:, None]), axis=1)
    slots = jnp.where(held, rank, -1).astype(jnp.int32)

    size = matrices // GROUPS
    chosen = [slice(first, first + size) for first in range(0, matrices, size)]
    in_pieces = dp_count == 4 * LINE and row_count % 32 == 0
    if in_pieces:
        places = relative_places(Grid(dp_count))
        rows = master
    else:
        places = jnp.zeros((1,), jnp.int32)
        rows = jnp.zeros((matrices, terms.shape[1], width), jnp.float32)
        rows = lax.dynamic_update_slice_in_dim(rows, master, me * row_count, axis=1)
    state = [
        None,
        None,
        jnp.zeros((MOST, terms.shape[1], width), jnp.bfloat16),
        jnp.zeros((8, 128), jnp.float32),
    ]

    def newton_step(at, update, gram_parts, *ties):
        tied = after(slots, *ties) if ties else slots
        state[:] = newton(
            places, tied, gram_parts, update, master_all, rows, state, chosen[at].start
        )
        return state[3]

    if in_pieces:
        momenta = by_pieces(terms, momentum, chosen, newton_step)
    else:
        summed = lax.psum_scatter(terms, "dp", scatter_dimension=1, tiled=True)
        new_momentum, update = updated(summed.astype(jnp.float32), momentum)
        update = lax.all_gather(update, "dp", axis=1, tiled=True)
        momenta = [new_momentum]
        for at, part in enumerate(chosen):
            newton_step(at, *gathered_grams([update[None, part]]))
    new_weights, new_master, owned_updates, rms = state
    if not in_pieces:
        new_master = lax.dynamic_slice_in_dim(new_master, me * row_count, row_count, axis=1)
    new_momentum = momenta[0] if len(momenta) == 1 else jnp.concatenate(momenta)
    return (new_weights, new_master, new_momentum, owned_updates[None], rms[:1, :MOST])


def solution(mesh):
    return jax.shard_map(
        per_device,
        mesh=mesh,
        in_specs=(P("dp", None, None, "col"), P(None, "dp", "col"), P(None, "dp", "col"), P()),
        out_specs=(
            P(None, None, "col"),
            P(None, "dp", "col"),
            P(None, "dp", "col"),
            P("dp", None, None, "col"),
            P("dp", None),
        ),
        check_vma=False,
    )
```

```python
import functools
import math

import jax
import jax.numpy as jnp
from jax import lax
from jax.experimental import pallas as pl
from jax.experimental.pallas import tpu as pltpu
from jax.sharding import PartitionSpec as P

KV = 512
D = 2048
MOST = 2

quintic_first = 3.4445
quintic_second = -4.775
quintic_third = 2.0315
momentum_decay = 0.95
learn_rate = 0.3
weight_decay = 0.1
epsilon = 1e-07
factor = 0.2 * math.sqrt(max(KV, D))

VMEM_LIMIT = 56 * 1024 * 1024
LINE = 4


def dot(left, right):
    return jnp.dot(left, right, preferred_element_type=jnp.float32)


def half(value):
    return value.astype(jnp.bfloat16)


def gram_kernel(*refs):
    piece_refs, (update_ref, gram_ref) = refs[:-2], refs[-2:]
    start = 0
    for ref in piece_refs:
        rows = ref.shape[2]
        for index in range(ref.shape[0]):
            update_ref[0, start : start + rows] = ref[index, 0]
            start += rows
    block = update_ref[0]
    gram = lax.dot_general(
        block, block, (((1,), (1,)), ((), ())), preferred_element_type=jnp.float32
    )
    gram_ref[0] = half(gram)


def grams(pieces):
    _, count, _, width = pieces[0].shape
    rows = sum(piece.shape[0] * piece.shape[2] for piece in pieces)

    def spec(minor):
        return pl.BlockSpec((1, rows, minor), lambda i: (i, 0, 0))

    return pl.pallas_call(
        gram_kernel,
        grid=(count,),
        in_specs=[
            pl.BlockSpec((piece.shape[0], 1, *piece.shape[2:]), lambda i: (0, i, 0, 0))
            for piece in pieces
        ],
        out_specs=[spec(width), spec(rows)],
        out_shape=[
            jax.ShapeDtypeStruct((count, rows, width), jnp.bfloat16),
            jax.ShapeDtypeStruct((count, rows, rows), jnp.bfloat16),
        ],
        compiler_params=pltpu.CompilerParams(vmem_limit_bytes=VMEM_LIMIT),
        cost_estimate=pl.CostEstimate(
            flops=2 * count * rows * rows * width,
            bytes_accessed=2 * count * rows * (2 * width + rows),
            transcendentals=0,
        ),
    )(*pieces)


def mixers(grams_now):
    return [
        quintic_second * gram + quintic_third * dot(half(gram), half(gram)) for gram in grams_now
    ]


def next_grams(grams_now, mixes):
    lefts = [
        quintic_first * gram + dot(half(mix), half(gram)) for gram, mix in zip(grams_now, mixes)
    ]
    return [quintic_first * left + dot(half(left), half(mix)) for left, mix in zip(lefts, mixes)]


def chain_kernel(parts, *refs):
    gram_refs = refs[:parts]
    chain_ref, squares_ref = refs[parts:]
    count, rows, _ = chain_ref.shape
    on_diagonal = lax.broadcasted_iota(jnp.int32, (rows, rows), 0) == lax.broadcasted_iota(
        jnp.int32, (rows, rows), 1
    )
    grams_now = []
    for index in range(count):
        gram = gram_refs[0][index].astype(jnp.float32)
        for ref in gram_refs[1:]:
            gram = gram + ref[index].astype(jnp.float32)
        diagonal = jnp.where(on_diagonal, gram, 0.0)
        squares = jnp.sum(jnp.sum(diagonal, axis=0, keepdims=True), axis=1, keepdims=True)
        squares_ref[index] = jnp.broadcast_to(squares, squares_ref.shape[1:])
        inverse = 1.0 / (jnp.sqrt(squares) + epsilon)
        grams_now.append(gram * inverse * inverse)
    first = mixers(grams_now)
    grams_now = next_grams(grams_now, first)
    second = mixers(grams_now)
    grams_now = next_grams(grams_now, second)
    third = mixers(grams_now)
    pairs = [
        quintic_first * (m0 + m1) + dot(half(m1), half(m0)) for m0, m1 in zip(first, second)
    ]
    for index, (pair, m2) in enumerate(zip(pairs, third)):
        whole = quintic_first * pair + quintic_first**2 * m2 + dot(half(m2), half(pair))
        chain_ref[index] = half(whole)


def chains(gram_parts):
    count, rows, _ = gram_parts[0].shape
    step = 2 if count % 2 == 0 else 1
    parts = len(gram_parts)
    spec = pl.BlockSpec((step, rows, rows), lambda i: (i, 0, 0))
    return pl.pallas_call(
        functools.partial(chain_kernel, parts),
        grid=(count // step,),
        in_specs=[spec] * parts,
        out_specs=[spec, pl.BlockSpec((step, 8, 128), lambda i: (i, 0, 0))],
        out_shape=[
            jax.ShapeDtypeStruct((count, rows, rows), jnp.bfloat16),
            jax.ShapeDtypeStruct((count, 8, 128), jnp.float32),
        ],
        compiler_params=pltpu.CompilerParams(vmem_limit_bytes=VMEM_LIMIT),
        cost_estimate=pl.CostEstimate(
            flops=18 * count * rows * rows * rows,
            bytes_accessed=2 * count * rows * rows * (parts + 1),
            transcendentals=0,
        ),
    )(*gram_parts)


def apply_kernel(places_ref, slots_ref, *refs):
    chain_ref, squares_ref, update_ref, master_ref, rows_ref = refs[:5]
    weights_ref, new_rows_ref, owned_ref, rms_ref = refs[5:]
    blocks = places_ref.shape[0]
    height = update_ref.shape[1] // blocks
    at = pl.program_id(0)
    slot = slots_ref[at]

    @pl.when(at == 0)
    def _():
        owned_ref[...] = jnp.zeros_like(owned_ref)
        rms_ref[...] = jnp.zeros_like(rms_ref)

    squares = squares_ref[0, :1, :1]
    lane = lax.broadcasted_iota(jnp.int32, rms_ref.shape, 1)
    rms_ref[...] = jnp.where(lane == slot, jnp.sqrt(squares / float(KV * D)), rms_ref[...])
    block = update_ref[0]
    product = quintic_first**3 * block.astype(jnp.float32) + dot(chain_ref[0], block)
    scaled = half(product * (factor / (jnp.sqrt(squares) + epsilon)))
    decayed = rows_ref[0] * (1.0 - learn_rate * weight_decay)
    new_rows_ref[0] = decayed - learn_rate * scaled[:height].astype(jnp.float32)
    for block_at in range(blocks):
        place = pl.ds(pl.multiple_of(places_ref[block_at] * height, height), height)
        piece = scaled[block_at * height : (block_at + 1) * height]
        weights_ref[0, place] = half(
            master_ref[0, place].astype(jnp.float32) * (1.0 - learn_rate * weight_decay)
            - learn_rate * piece.astype(jnp.float32)
        )

        @pl.when(slot >= 0)
        def _():
            owned_ref[jnp.maximum(slot, 0), place] = piece


def applied(places, slots, chain, squares, update, master_all, master):
    count, rows, width = update.shape
    row_count = master.shape[1]

    def spec(height, minor):
        return pl.BlockSpec((1, height, minor), lambda i, *_: (i, 0, 0))

    owned = (MOST, rows, width)
    return pl.pallas_call(
        apply_kernel,
        grid_spec=pltpu.PrefetchScalarGridSpec(
            num_scalar_prefetch=2,
            grid=(count,),
            in_specs=[
                spec(rows, rows),
                spec(8, 128),
                spec(rows, width),
                spec(rows, width),
                spec(row_count, width),
            ],
            out_specs=[
                spec(rows, width),
                spec(row_count, width),
                pl.BlockSpec(owned, lambda i, *_: (0, 0, 0)),
                pl.BlockSpec((8, 128), lambda i, *_: (0, 0)),
            ],
        ),
        out_shape=[
            jax.ShapeDtypeStruct((count, rows, width), jnp.bfloat16),
            jax.ShapeDtypeStruct(master.shape, jnp.float32),
            jax.ShapeDtypeStruct(owned, jnp.bfloat16),
            jax.ShapeDtypeStruct((8, 128), jnp.float32),
        ],
        compiler_params=pltpu.CompilerParams(vmem_limit_bytes=VMEM_LIMIT),
        cost_estimate=pl.CostEstimate(
            flops=2 * count * rows * rows * width,
            bytes_accessed=2 * count * rows * (4 * width + rows),
            transcendentals=0,
        ),
    )(places, slots, chain, squares, update, master_all, master)


class Grid:
    def __init__(self, count):
        self.count = count
        self.me = lax.axis_index("dp")
        self.x_pairs = [(d, d ^ 1) for d in range(count)]
        self.y_pairs = [(d, d ^ 2) for d in range(count)]

    def over_x(self, value):
        return lax.ppermute(value, "dp", self.x_pairs)

    def over_y(self, value):
        return lax.ppermute(value, "dp", self.y_pairs)

    def over_z(self, value, shift):
        pairs = [(d, (d // 4 + shift) % LINE * 4 + d % 4) for d in range(self.count)]
        return lax.ppermute(value, "dp", pairs)


def place(me, dx, dy, dz):
    z = ((me >> 2) + dz) & (LINE - 1)
    return z * 4 + ((me & 3) ^ (2 * dy + dx))


def after(value, *others):
    return lax.optimization_barrier((value, *others))[0]


def added(*values):
    return sum(value.astype(jnp.float32) for value in values)


def reduce_scatter(grid, terms, row_count):
    def term(me, dx, dy, dz):
        start = place(me, dx, dy, dz) * row_count
        return lax.dynamic_slice_in_dim(terms, start, row_count, axis=1)

    me = grid.me
    far1 = grid.over_x(term(me, 1, 1, 1))
    far2 = grid.over_y(term(me, 1, 1, 2))
    along_y2 = grid.over_y(term(me, 0, 1, 2))
    me = after(grid.me, far1, far2)
    along_x2 = grid.over_x(half(added(term(me, 1, 0, 2), far2)))
    along_y1 = grid.over_y(half(added(term(me, 0, 1, 1), far1)))

    me = after(grid.me, along_x2, along_y2)
    near2 = half(added(term(me, 0, 0, 2), along_x2, along_y2))
    line2 = grid.over_z(near2, 2)

    me = after(grid.me, near2)
    along_x1 = grid.over_x(term(me, 1, 0, 1))
    far3 = grid.over_y(term(me, 1, 1, 3))
    far0 = grid.over_x(term(me, 1, 1, 0))

    me = after(grid.me, near2, along_x1, along_y1)
    near1 = half(added(term(me, 0, 0, 1), along_x1, along_y1))
    line1 = grid.over_z(near1, 1)

    me = after(grid.me, near1)
    along_y3 = grid.over_y(term(me, 0, 1, 3))
    along_x3 = half(added(term(me, 1, 0, 3), far3))
    me = after(grid.me, along_x3)
    along_x3 = grid.over_x(along_x3)
    along_x0 = grid.over_x(term(me, 1, 0, 0))
    along_y0 = grid.over_y(half(added(term(me, 0, 1, 0), far0)))

    me = after(grid.me, along_x3, along_y3, line2)
    near3 = half(added(term(me, 0, 0, 3), along_x3, along_y3))
    line3 = grid.over_z(near3, 3)
    me = after(grid.me, near3)
    return added(term(me, 0, 0, 0), along_x0, along_y0, line1, line2, line3)


def all_gather(grid, own):
    line = [own] + [grid.over_z(own, LINE - dz) for dz in range(1, LINE)]
    over_x = [grid.over_x(piece) for piece in line]
    over_y = [grid.over_y(piece) for piece in line]
    far = [grid.over_x(piece) for piece in over_y[: LINE // 2]]
    far += [grid.over_y(piece) for piece in over_x[LINE // 2 :]]
    return line + over_y + over_x + far


def relative_places(grid):
    order = [(dx, dy, dz) for dx in range(2) for dy in range(2) for dz in range(LINE)]
    return jnp.stack([place(grid.me, *where) for where in order]).astype(jnp.int32)


def gathered_grams(pieces):
    update, partial_gram = grams(pieces)
    if lax.axis_size("col") == 2:
        return update, [partial_gram, lax.ppermute(partial_gram, "col", [(0, 1), (1, 0)])]
    return update, [lax.psum(partial_gram, "col")]


def updated(summed, momentum):
    new_momentum = momentum_decay * momentum + summed
    return new_momentum, half(summed + momentum_decay * new_momentum)


def per_device(gradients, momentum, master, owners):
    me = lax.axis_index("dp")
    dp_count = lax.axis_size("dp")
    matrices, row_count, width = momentum.shape
    terms = gradients[0]
    held = owners == me
    order = jnp.arange(matrices)
    rank = jnp.sum(held[None, :] & (order[None, :] < order[:, None]), axis=1)
    slots = jnp.where(held, rank, -1).astype(jnp.int32)

    in_pieces = dp_count == 4 * LINE and row_count % 32 == 0
    if in_pieces:
        grid = Grid(dp_count)
        places = relative_places(grid)
        rows = master
        summed = reduce_scatter(grid, terms, row_count)
        new_momentum, own = updated(summed, momentum)
        master_half = half(after(master, own))
        master_all = lax.all_gather(master_half, "dp", axis=1, tiled=True)
        pieces = [piece[None] for piece in all_gather(grid, own)]
    else:
        places = jnp.zeros((1,), jnp.int32)
        rows = jnp.zeros((matrices, terms.shape[1], width), jnp.float32)
        rows = lax.dynamic_update_slice_in_dim(rows, master, me * row_count, axis=1)
        summed = lax.psum_scatter(terms, "dp", scatter_dimension=1, tiled=True)
        new_momentum, own = updated(summed.astype(jnp.float32), momentum)
        master_all = lax.all_gather(half(master), "dp", axis=1, tiled=True)
        pieces = [lax.all_gather(own, "dp", axis=1, tiled=True)[None]]
    update, gram_parts = gathered_grams(pieces)
    chain, squares = chains(gram_parts)
    new_weights, new_master, owned_updates, rms = applied(
        places, slots, chain, squares, update, master_all, rows
    )
    if not in_pieces:
        new_master = lax.dynamic_slice_in_dim(new_master, me * row_count, row_count, axis=1)
    return (new_weights, new_master, new_momentum, owned_updates[None], rms[:1, :MOST])


def solution(mesh):
    return jax.shard_map(
        per_device,
        mesh=mesh,
        in_specs=(P("dp", None, None, "col"), P(None, "dp", "col"), P(None, "dp", "col"), P()),
        out_specs=(
            P(None, None, "col"),
            P(None, "dp", "col"),
            P(None, "dp", "col"),
            P("dp", None, None, "col"),
            P("dp", None),
        ),
        check_vma=False,
    )
```

```python
import functools
import math

import jax
import jax.numpy as jnp
from jax import lax
from jax.experimental import pallas as pl
from jax.experimental.pallas import tpu as pltpu
from jax.sharding import PartitionSpec as P

KV = 512
D = 2048
MOST = 2

quintic_first = 3.4445
quintic_second = -4.775
quintic_third = 2.0315
momentum_decay = 0.95
learn_rate = 0.3
weight_decay = 0.1
epsilon = 1e-07
factor = 0.2 * math.sqrt(max(KV, D))

VMEM_LIMIT = 56 * 1024 * 1024
LINE = 4


def dot(left, right):
    return jnp.dot(left, right, preferred_element_type=jnp.float32)


def half(value):
    return value.astype(jnp.bfloat16)


def gram_kernel(*refs):
    piece_refs, (update_ref, gram_ref) = refs[:-2], refs[-2:]
    start = 0
    for ref in piece_refs:
        rows = ref.shape[2]
        for index in range(ref.shape[0]):
            update_ref[0, start : start + rows] = ref[index, 0]
            start += rows
    block = update_ref[0]
    gram = lax.dot_general(
        block, block, (((1,), (1,)), ((), ())), preferred_element_type=jnp.float32
    )
    gram_ref[0] = half(gram)


def grams(pieces):
    _, count, _, width = pieces[0].shape
    rows = sum(piece.shape[0] * piece.shape[2] for piece in pieces)

    def spec(minor):
        return pl.BlockSpec((1, rows, minor), lambda i: (i, 0, 0))

    return pl.pallas_call(
        gram_kernel,
        grid=(count,),
        in_specs=[
            pl.BlockSpec((piece.shape[0], 1, *piece.shape[2:]), lambda i: (0, i, 0, 0))
            for piece in pieces
        ],
        out_specs=[spec(width), spec(rows)],
        out_shape=[
            jax.ShapeDtypeStruct((count, rows, width), jnp.bfloat16),
            jax.ShapeDtypeStruct((count, rows, rows), jnp.bfloat16),
        ],
        compiler_params=pltpu.CompilerParams(vmem_limit_bytes=VMEM_LIMIT),
        cost_estimate=pl.CostEstimate(
            flops=2 * count * rows * rows * width,
            bytes_accessed=2 * count * rows * (2 * width + rows),
            transcendentals=0,
        ),
    )(*pieces)


def mixers(grams_now):
    return [
        quintic_second * gram + quintic_third * dot(half(gram), half(gram)) for gram in grams_now
    ]


def next_grams(grams_now, mixes):
    lefts = [
        quintic_first * gram + dot(half(mix), half(gram)) for gram, mix in zip(grams_now, mixes)
    ]
    return [quintic_first * left + dot(half(left), half(mix)) for left, mix in zip(lefts, mixes)]


def chain_kernel(parts, *refs):
    gram_refs = refs[:parts]
    chain_ref, squares_ref = refs[parts:]
    count, rows, _ = chain_ref.shape
    on_diagonal = lax.broadcasted_iota(jnp.int32, (rows, rows), 0) == lax.broadcasted_iota(
        jnp.int32, (rows, rows), 1
    )
    grams_now = []
    for index in range(count):
        gram = gram_refs[0][index].astype(jnp.float32)
        for ref in gram_refs[1:]:
            gram = gram + ref[index].astype(jnp.float32)
        diagonal = jnp.where(on_diagonal, gram, 0.0)
        squares = jnp.sum(jnp.sum(diagonal, axis=0, keepdims=True), axis=1, keepdims=True)
        squares_ref[index] = jnp.broadcast_to(squares, squares_ref.shape[1:])
        inverse = 1.0 / (jnp.sqrt(squares) + epsilon)
        grams_now.append(gram * inverse * inverse)
    first = mixers(grams_now)
    grams_now = next_grams(grams_now, first)
    second = mixers(grams_now)
    grams_now = next_grams(grams_now, second)
    third = mixers(grams_now)
    pairs = [
        quintic_first * (m0 + m1) + dot(half(m1), half(m0)) for m0, m1 in zip(first, second)
    ]
    for index, (pair, m2) in enumerate(zip(pairs, third)):
        whole = quintic_first * pair + quintic_first**2 * m2 + dot(half(m2), half(pair))
        chain_ref[index] = half(whole)


def chains(gram_parts):
    count, rows, _ = gram_parts[0].shape
    step = 2 if count % 2 == 0 else 1
    parts = len(gram_parts)
    spec = pl.BlockSpec((step, rows, rows), lambda i: (i, 0, 0))
    return pl.pallas_call(
        functools.partial(chain_kernel, parts),
        grid=(count // step,),
        in_specs=[spec] * parts,
        out_specs=[spec, pl.BlockSpec((step, 8, 128), lambda i: (i, 0, 0))],
        out_shape=[
            jax.ShapeDtypeStruct((count, rows, rows), jnp.bfloat16),
            jax.ShapeDtypeStruct((count, 8, 128), jnp.float32),
        ],
        compiler_params=pltpu.CompilerParams(vmem_limit_bytes=VMEM_LIMIT),
        cost_estimate=pl.CostEstimate(
            flops=18 * count * rows * rows * rows,
            bytes_accessed=2 * count * rows * rows * (parts + 1),
            transcendentals=0,
        ),
    )(*gram_parts)


def apply_kernel(places_ref, slots_ref, *refs):
    chain_ref, squares_ref, update_ref, master_ref, rows_ref = refs[:5]
    weights_ref, new_rows_ref, owned_ref, rms_ref = refs[5:]
    blocks = places_ref.shape[0]
    height = update_ref.shape[1] // blocks
    at = pl.program_id(1)
    slot = slots_ref[at]

    @pl.when(at == 0)
    def _():
        owned_ref[...] = jnp.zeros_like(owned_ref)
        rms_ref[...] = jnp.zeros_like(rms_ref)

    squares = squares_ref[0, :1, :1]
    lane = lax.broadcasted_iota(jnp.int32, rms_ref.shape, 1)
    rms_ref[...] = jnp.where(lane == slot, jnp.sqrt(squares / float(KV * D)), rms_ref[...])
    block = update_ref[0]
    product = quintic_first**3 * block.astype(jnp.float32) + dot(chain_ref[0], block)
    scaled = half(product * (factor / (jnp.sqrt(squares) + epsilon)))
    decayed = rows_ref[0] * (1.0 - learn_rate * weight_decay)
    new_rows_ref[0] = decayed - learn_rate * scaled[:height].astype(jnp.float32)
    for block_at in range(blocks):
        place = pl.ds(pl.multiple_of(places_ref[block_at] * height, height), height)
        piece = scaled[block_at * height : (block_at + 1) * height]
        weights_ref[0, place] = half(
            master_ref[0, place].astype(jnp.float32) * (1.0 - learn_rate * weight_decay)
            - learn_rate * piece.astype(jnp.float32)
        )

        @pl.when(slot >= 0)
        def _():
            owned_ref[jnp.maximum(slot, 0), place] = piece


def applied(places, slots, chain, squares, update, master_all, master):
    count, rows, width = update.shape
    row_count = master.shape[1]

    cuts = 2 if width % 256 == 0 else 1
    part = width // cuts

    def spec(height):
        return pl.BlockSpec((1, height, part), lambda j, i, *_: (i, 0, j))

    def whole(height, minor):
        return pl.BlockSpec((1, height, minor), lambda j, i, *_: (i, 0, 0))

    owned = (MOST, rows, width)
    return pl.pallas_call(
        apply_kernel,
        grid_spec=pltpu.PrefetchScalarGridSpec(
            num_scalar_prefetch=2,
            grid=(cuts, count),
            in_specs=[
                whole(rows, rows),
                whole(8, 128),
                spec(rows),
                spec(rows),
                spec(row_count),
            ],
            out_specs=[
                spec(rows),
                spec(row_count),
                pl.BlockSpec((MOST, rows, part), lambda j, i, *_: (0, 0, j)),
                pl.BlockSpec((1, MOST), lambda j, i, *_: (0, 0)),
            ],
        ),
        out_shape=[
            jax.ShapeDtypeStruct((count, rows, width), jnp.bfloat16),
            jax.ShapeDtypeStruct(master.shape, jnp.float32),
            jax.ShapeDtypeStruct(owned, jnp.bfloat16),
            jax.ShapeDtypeStruct((1, MOST), jnp.float32),
        ],
        compiler_params=pltpu.CompilerParams(vmem_limit_bytes=VMEM_LIMIT),
        cost_estimate=pl.CostEstimate(
            flops=2 * count * rows * rows * width,
            bytes_accessed=2 * count * rows * (4 * width + rows),
            transcendentals=0,
        ),
    )(places, slots, chain, squares, update, master_all, master)


class Grid:
    def __init__(self, count):
        self.count = count
        self.me = lax.axis_index("dp")
        self.x_pairs = [(d, d ^ 1) for d in range(count)]
        self.y_pairs = [(d, d ^ 2) for d in range(count)]

    def over_x(self, value):
        return lax.ppermute(value, "dp", self.x_pairs)

    def over_y(self, value):
        return lax.ppermute(value, "dp", self.y_pairs)

    def over_z(self, value, shift):
        pairs = [(d, (d // 4 + shift) % LINE * 4 + d % 4) for d in range(self.count)]
        return lax.ppermute(value, "dp", pairs)


def place(me, dx, dy, dz):
    z = ((me >> 2) + dz) & (LINE - 1)
    return z * 4 + ((me & 3) ^ (2 * dy + dx))


def after(value, *others):
    return lax.optimization_barrier((value, *others))[0]


def added(*values):
    return sum(value.astype(jnp.float32) for value in values)


def reduce_scatter(grid, terms, row_count, master):
    def term(me, dx, dy, dz):
        start = place(me, dx, dy, dz) * row_count
        return lax.dynamic_slice_in_dim(terms, start, row_count, axis=1)

    me = grid.me
    raw_far1, raw_far2 = term(me, 1, 1, 1), term(me, 1, 1, 2)
    me = after(grid.me, raw_far1, raw_far2)
    raw_x1, raw_far3, raw_y2 = term(me, 1, 0, 1), term(me, 1, 1, 3), term(me, 0, 1, 2)
    raw_y3, raw_far0, raw_x0 = term(me, 0, 1, 3), term(me, 1, 1, 0), term(me, 1, 0, 0)
    far1 = grid.over_x(raw_far1)
    far2 = grid.over_y(raw_far2)
    along_x1 = grid.over_x(raw_x1)
    far3 = grid.over_y(raw_far3)
    along_y2 = grid.over_y(raw_y2)

    me = after(grid.me, far1, far2, raw_y3)
    sent_x2 = half(added(term(me, 1, 0, 2), far2))
    sent_y1 = half(added(term(me, 0, 1, 1), far1))
    along_x2 = grid.over_x(sent_x2)
    along_y1 = grid.over_y(sent_y1)

    me = after(grid.me, far3, along_x1, sent_x2, sent_y1)
    sent_x3 = half(added(term(me, 1, 0, 3), far3))
    along_x3 = grid.over_x(sent_x3)
    along_y3 = grid.over_y(after(raw_y3, far3, along_x1))

    me = after(grid.me, along_y2, along_x2, sent_x3)
    near2 = half(added(term(me, 0, 0, 2), along_x2, along_y2))
    line2 = grid.over_z(near2, 2)
    master_half = half(after(master, near2))
    far0 = grid.over_x(after(raw_far0, along_x2))

    me = after(grid.me, along_x1, along_y1, along_x3, near2, master_half)
    near1 = half(added(term(me, 0, 0, 1), along_x1, along_y1))
    line1 = grid.over_z(near1, 1)
    along_x0 = grid.over_x(after(raw_x0, along_x3))

    me = after(grid.me, along_x3, along_y3, far0, near1)
    near3 = half(added(term(me, 0, 0, 3), along_x3, along_y3))
    sent_y0 = half(added(term(me, 0, 1, 0), far0))
    line3 = grid.over_z(near3, 3)
    along_y0 = grid.over_y(sent_y0)
    me = after(grid.me, near3, sent_y0, line2)
    return added(term(me, 0, 0, 0), along_x0, along_y0, line1, line2, line3), master_half


def all_gather(grid, own):
    line = [own] + [grid.over_z(own, LINE - dz) for dz in range(1, LINE)]
    over_x = [grid.over_x(piece) for piece in line]
    over_y = [grid.over_y(piece) for piece in line]
    far = [grid.over_x(piece) for piece in over_y[: LINE // 2]]
    far += [grid.over_y(piece) for piece in over_x[LINE // 2 :]]
    return line + over_y + over_x + far


def relative_places(grid):
    order = [(dx, dy, dz) for dx in range(2) for dy in range(2) for dz in range(LINE)]
    return jnp.stack([place(grid.me, *where) for where in order]).astype(jnp.int32)


def gathered_grams(pieces):
    update, partial_gram = grams(pieces)
    if lax.axis_size("col") == 2:
        return update, [partial_gram, lax.ppermute(partial_gram, "col", [(0, 1), (1, 0)])]
    return update, [lax.psum(partial_gram, "col")]


def updated(summed, momentum):
    new_momentum = momentum_decay * momentum + summed
    return new_momentum, half(summed + momentum_decay * new_momentum)


def per_device(gradients, momentum, master, owners):
    me = lax.axis_index("dp")
    dp_count = lax.axis_size("dp")
    matrices, row_count, width = momentum.shape
    terms = gradients[0]
    held = owners == me
    order = jnp.arange(matrices)
    rank = jnp.sum(held[None, :] & (order[None, :] < order[:, None]), axis=1)
    slots = jnp.where(held, rank, -1).astype(jnp.int32)

    in_pieces = dp_count == 4 * LINE and row_count % 32 == 0
    if in_pieces:
        grid = Grid(dp_count)
        places = relative_places(grid)
        rows = master
        summed, master_half = reduce_scatter(grid, terms, row_count, master)
        new_momentum, own = updated(summed, momentum)
        master_all = lax.all_gather(master_half, "dp", axis=1, tiled=True)
        pieces = [piece[None] for piece in all_gather(grid, own)]
    else:
        places = jnp.zeros((1,), jnp.int32)
        rows = jnp.zeros((matrices, terms.shape[1], width), jnp.float32)
        rows = lax.dynamic_update_slice_in_dim(rows, master, me * row_count, axis=1)
        summed = lax.psum_scatter(terms, "dp", scatter_dimension=1, tiled=True)
        new_momentum, own = updated(summed.astype(jnp.float32), momentum)
        master_all = lax.all_gather(half(master), "dp", axis=1, tiled=True)
        pieces = [lax.all_gather(own, "dp", axis=1, tiled=True)[None]]
    update, gram_parts = gathered_grams(pieces)
    chain, squares = chains(gram_parts)
    new_weights, new_master, owned_updates, rms = applied(
        places, slots, chain, squares, update, master_all, rows
    )
    if not in_pieces:
        new_master = lax.dynamic_slice_in_dim(new_master, me * row_count, row_count, axis=1)
    return (new_weights, new_master, new_momentum, owned_updates[None], rms)


def solution(mesh):
    return jax.shard_map(
        per_device,
        mesh=mesh,
        in_specs=(P("dp", None, None, "col"), P(None, "dp", "col"), P(None, "dp", "col"), P()),
        out_specs=(
            P(None, None, "col"),
            P(None, "dp", "col"),
            P(None, "dp", "col"),
            P("dp", None, None, "col"),
            P("dp", None),
        ),
        check_vma=False,
    )
```

```python
import functools
import math

import jax
import jax.numpy as jnp
from jax import lax
from jax.experimental import pallas as pl
from jax.experimental.pallas import tpu as pltpu
from jax.sharding import PartitionSpec as P

KV = 512
D = 2048
MOST = 2

quintic_first = 3.4445
quintic_second = -4.775
quintic_third = 2.0315
momentum_decay = 0.95
learn_rate = 0.3
weight_decay = 0.1
epsilon = 1e-07
factor = 0.2 * math.sqrt(max(KV, D))

VMEM_LIMIT = 56 * 1024 * 1024
LINE = 4


def dot(left, right):
    return jnp.dot(left, right, preferred_element_type=jnp.float32)


def half(value):
    return value.astype(jnp.bfloat16)


def gram_kernel(*refs):
    piece_refs, (update_ref, low_ref, high_ref) = refs[:-3], refs[-3:]
    start = 0
    for ref in piece_refs:
        rows = ref.shape[2]
        for index in range(ref.shape[0]):
            update_ref[0, start : start + rows] = ref[index, 0]
            start += rows
    block = update_ref[0]
    gram = half(
        lax.dot_general(
            block, block, (((1,), (1,)), ((), ())), preferred_element_type=jnp.float32
        )
    )
    at = pl.program_id(0)
    middle = pl.num_programs(0) // 2

    @pl.when(at < middle)
    def _():
        low_ref[0] = gram

    @pl.when(at >= middle)
    def _():
        high_ref[0] = gram


def grams(pieces):
    _, count, _, width = pieces[0].shape
    rows = sum(piece.shape[0] * piece.shape[2] for piece in pieces)
    middle = count // 2

    return pl.pallas_call(
        gram_kernel,
        grid=(count,),
        in_specs=[
            pl.BlockSpec((piece.shape[0], 1, *piece.shape[2:]), lambda i: (0, i, 0, 0))
            for piece in pieces
        ],
        out_specs=[
            pl.BlockSpec((1, rows, width), lambda i: (i, 0, 0)),
            pl.BlockSpec((1, rows, rows), lambda i: (jnp.minimum(i, middle - 1), 0, 0)),
            pl.BlockSpec((1, rows, rows), lambda i: (jnp.maximum(i - middle, 0), 0, 0)),
        ],
        out_shape=[
            jax.ShapeDtypeStruct((count, rows, width), jnp.bfloat16),
            jax.ShapeDtypeStruct((middle, rows, rows), jnp.bfloat16),
            jax.ShapeDtypeStruct((count - middle, rows, rows), jnp.bfloat16),
        ],
        compiler_params=pltpu.CompilerParams(vmem_limit_bytes=VMEM_LIMIT),
        cost_estimate=pl.CostEstimate(
            flops=2 * count * rows * rows * width,
            bytes_accessed=2 * count * rows * (2 * width + rows),
            transcendentals=0,
        ),
    )(*pieces)


def mixers(grams_now):
    return [
        quintic_second * gram + quintic_third * dot(half(gram), half(gram)) for gram in grams_now
    ]


def next_grams(grams_now, mixes):
    lefts = [
        quintic_first * gram + dot(half(mix), half(gram)) for gram, mix in zip(grams_now, mixes)
    ]
    return [quintic_first * left + dot(half(left), half(mix)) for left, mix in zip(lefts, mixes)]


def chain_kernel(*refs):
    halves = refs[: len(refs) - 2]
    chain_ref, squares_ref = refs[-2:]
    count, _, rows, _ = chain_ref.shape
    parts = len(halves) // count
    on_diagonal = lax.broadcasted_iota(jnp.int32, (rows, rows), 0) == lax.broadcasted_iota(
        jnp.int32, (rows, rows), 1
    )
    grams_now = []
    for index in range(count):
        gram = sum(
            ref[0].astype(jnp.float32) for ref in halves[index * parts : (index + 1) * parts]
        )
        diagonal = jnp.where(on_diagonal, gram, 0.0)
        squares = jnp.sum(jnp.sum(diagonal, axis=0, keepdims=True), axis=1, keepdims=True)
        squares_ref[index, 0] = jnp.broadcast_to(squares, squares_ref.shape[2:])
        inverse = 1.0 / (jnp.sqrt(squares) + epsilon)
        grams_now.append(gram * inverse * inverse)
    first = mixers(grams_now)
    grams_now = next_grams(grams_now, first)
    second = mixers(grams_now)
    grams_now = next_grams(grams_now, second)
    third = mixers(grams_now)
    pairs = [
        quintic_first * (m0 + m1) + dot(half(m1), half(m0)) for m0, m1 in zip(first, second)
    ]
    for index, (pair, m2) in enumerate(zip(pairs, third)):
        whole = quintic_first * pair + quintic_first**2 * m2 + dot(half(m2), half(pair))
        chain_ref[index, 0] = half(whole)


def chains(low_parts, high_parts):
    count, rows, _ = low_parts[0].shape
    inputs = [*low_parts, *high_parts]

    def both(*minor):
        return pl.BlockSpec((2, 1, *minor), lambda i: (0, i, 0, 0))

    return pl.pallas_call(
        chain_kernel,
        grid=(count,),
        in_specs=[pl.BlockSpec((1, rows, rows), lambda i: (i, 0, 0))] * len(inputs),
        out_specs=[both(rows, rows), both(8, 128)],
        out_shape=[
            jax.ShapeDtypeStruct((2, count, rows, rows), jnp.bfloat16),
            jax.ShapeDtypeStruct((2, count, 8, 128), jnp.float32),
        ],
        compiler_params=pltpu.CompilerParams(vmem_limit_bytes=VMEM_LIMIT),
        cost_estimate=pl.CostEstimate(
            flops=36 * count * rows * rows * rows,
            bytes_accessed=2 * count * rows * rows * (len(inputs) + 2),
            transcendentals=0,
        ),
    )(*inputs)


def apply_kernel(lies, places_ref, slots_ref, *refs):
    chain_ref, squares_ref, update_ref, rows_ref = refs[:4]
    master_refs = refs[4:-5]
    weights_ref, new_rows_ref, owned_ref, rms_ref, scaled_ref = refs[-5:]
    blocks = len(lies)
    height = update_ref.shape[1] // blocks
    at = pl.program_id(0)
    slot = slots_ref[at]

    @pl.when(at == 0)
    def _():
        owned_ref[...] = jnp.zeros_like(owned_ref)
        rms_ref[...] = jnp.zeros_like(rms_ref)

    def span(block_at):
        return pl.ds(block_at * height, height)

    def target(block_at):
        return pl.ds(pl.multiple_of(places_ref[block_at] * height, height), height)

    squares = squares_ref[0, :1, :1]
    lane = lax.broadcasted_iota(jnp.int32, rms_ref.shape, 1)
    rms_ref[...] = jnp.where(lane == slot, jnp.sqrt(squares / float(KV * D)), rms_ref[...])
    block = update_ref[0]
    product = quintic_first**3 * block.astype(jnp.float32) + dot(chain_ref[0], block)
    scaled_ref[...] = half(product * (factor / (jnp.sqrt(squares) + epsilon)))
    decayed = rows_ref[0] * (1.0 - learn_rate * weight_decay)
    new_rows_ref[0] = decayed - learn_rate * scaled_ref[span(0)].astype(jnp.float32)
    for block_at, (piece, where) in enumerate(lies):
        decayed = master_refs[piece][where, 0].astype(jnp.float32) * (
            1.0 - learn_rate * weight_decay
        )
        weights_ref[0, target(block_at)] = half(
            decayed - learn_rate * scaled_ref[span(block_at)].astype(jnp.float32)
        )

    @pl.when(slot >= 0)
    def _():
        for block_at in range(blocks):
            owned_ref[jnp.maximum(slot, 0), target(block_at)] = scaled_ref[span(block_at)]


def applied(places, slots, chain, squares, update, master_pieces, lies, master):
    count, rows, width = update.shape
    row_count = master.shape[1]

    def spec(height, minor):
        return pl.BlockSpec((1, height, minor), lambda i, *_: (i, 0, 0))

    owned = (MOST, rows, width)
    return pl.pallas_call(
        functools.partial(apply_kernel, lies),
        grid_spec=pltpu.PrefetchScalarGridSpec(
            num_scalar_prefetch=2,
            grid=(count,),
            in_specs=[
                spec(rows, rows),
                spec(8, 128),
                spec(rows, width),
                spec(row_count, width),
            ]
            + [
                pl.BlockSpec((piece.shape[0], 1, *piece.shape[2:]), lambda i, *_: (0, i, 0, 0))
                for piece in master_pieces
            ],
            out_specs=[
                spec(rows, width),
                spec(row_count, width),
                pl.BlockSpec(owned, lambda i, *_: (0, 0, 0)),
                pl.BlockSpec((1, MOST), lambda i, *_: (0, 0)),
            ],
            scratch_shapes=[pltpu.VMEM((rows, width), jnp.bfloat16)],
        ),
        out_shape=[
            jax.ShapeDtypeStruct((count, rows, width), jnp.bfloat16),
            jax.ShapeDtypeStruct(master.shape, jnp.float32),
            jax.ShapeDtypeStruct(owned, jnp.bfloat16),
            jax.ShapeDtypeStruct((1, MOST), jnp.float32),
        ],
        compiler_params=pltpu.CompilerParams(vmem_limit_bytes=VMEM_LIMIT),
        cost_estimate=pl.CostEstimate(
            flops=2 * count * rows * rows * width,
            bytes_accessed=2 * count * rows * (4 * width + rows),
            transcendentals=0,
        ),
    )(places, slots, chain, squares, update, master, *master_pieces)


class Grid:
    def __init__(self, count):
        self.count = count
        self.me = lax.axis_index("dp")
        self.x_pairs = [(d, d ^ 1) for d in range(count)]
        self.y_pairs = [(d, d ^ 2) for d in range(count)]

    def over_x(self, value):
        return lax.ppermute(value, "dp", self.x_pairs)

    def over_y(self, value):
        return lax.ppermute(value, "dp", self.y_pairs)

    def over_z(self, value, shift):
        pairs = [(d, (d // 4 + shift) % LINE * 4 + d % 4) for d in range(self.count)]
        return lax.ppermute(value, "dp", pairs)


def place(me, dx, dy, dz):
    z = ((me >> 2) + dz) & (LINE - 1)
    return z * 4 + ((me & 3) ^ (2 * dy + dx))


def after(value, *others):
    return lax.optimization_barrier((value, *others))[0]


def added(*values):
    return sum(value.astype(jnp.float32) for value in values)


class MasterGather:
    lies = [(0, 0), (1, 0), (2, 0), (3, 0)]
    lies += [(4, 0), (5, 0), (5, 1), (4, 1)]
    lies += [(6, 0), (7, 0), (7, 1), (6, 1)]
    lies += [(8, 0), (9, 0), (9, 1), (8, 1)]

    def __init__(self, grid, master):
        self.grid = grid
        self.line = [half(master)]

    def step_line(self, *ties):
        self.line.append(self.grid.over_z(after(self.line[-1], *ties), 1))

    def near_ends(self, *ties):
        own = after(self.line[0], *ties)
        ends = jnp.stack([own, self.line[1]])
        self.y_ends = self.grid.over_y(ends)
        self.x_ends = self.grid.over_x(ends)

    def near_middle(self, *ties):
        middle = after(jnp.stack([self.line[3], self.line[2]]), *ties)
        self.y_middle = self.grid.over_y(middle)
        self.x_middle = self.grid.over_x(middle)

    def far(self):
        self.far_ends = self.grid.over_x(after(self.y_ends, self.x_middle, self.y_middle))
        self.far_middle = self.grid.over_y(after(self.x_middle, self.y_middle))

    def pieces(self):
        own, last, middle, first = self.line
        line = [piece[None] for piece in (own, first, middle, last)]
        near = [self.y_ends, self.y_middle, self.x_ends, self.x_middle]
        return line + near + [self.far_ends, self.far_middle]


def reduce_scatter(grid, terms, row_count, master_gather):
    def term(me, dx, dy, dz):
        start = place(me, dx, dy, dz) * row_count
        return lax.dynamic_slice_in_dim(terms, start, row_count, axis=1)

    me = grid.me
    raw_far1, raw_far2 = term(me, 1, 1, 1), term(me, 1, 1, 2)
    me = after(grid.me, raw_far1, raw_far2)
    raw_x1, raw_far3, raw_y2 = term(me, 1, 0, 1), term(me, 1, 1, 3), term(me, 0, 1, 2)
    raw_y3, raw_far0, raw_x0 = term(me, 0, 1, 3), term(me, 1, 1, 0), term(me, 1, 0, 0)
    far1 = grid.over_x(raw_far1)
    far2 = grid.over_y(raw_far2)
    along_y2 = grid.over_y(raw_y2)
    along_x1 = grid.over_x(raw_x1)
    master_gather.step_line(raw_far1)

    me = after(grid.me, far1, far2, raw_y3)
    sent_x2 = half(added(term(me, 1, 0, 2), far2))
    sent_y1 = half(added(term(me, 0, 1, 1), far1))
    along_x2 = grid.over_x(sent_x2)
    along_y1 = grid.over_y(sent_y1)
    master_gather.step_line(sent_x2)

    me = after(grid.me, along_y2, along_x2, *master_gather.line[1:2])
    near2 = half(added(term(me, 0, 0, 2), along_x2, along_y2))
    line2 = grid.over_z(near2, 2)
    far3 = grid.over_y(after(raw_far3, along_y2))
    far0 = grid.over_x(after(raw_far0, along_x1))

    me = after(grid.me, along_x1, along_y1, near2)
    near1 = half(added(term(me, 0, 0, 1), along_x1, along_y1))
    line1 = grid.over_z(near1, 1)
    along_y3 = grid.over_y(after(raw_y3, along_y1))
    along_x0 = grid.over_x(after(raw_x0, along_y1))

    me = after(grid.me, far3, far0, near1, *master_gather.line[2:3])
    sent_x3 = half(added(term(me, 1, 0, 3), far3))
    sent_y0 = half(added(term(me, 0, 1, 0), far0))
    along_x3 = grid.over_x(sent_x3)
    along_y0 = grid.over_y(sent_y0)
    master_gather.step_line(sent_x3)

    me = after(grid.me, along_x3, along_y3, line2)
    near3 = half(added(term(me, 0, 0, 3), along_x3, along_y3))
    line3 = grid.over_z(near3, 3)
    master_gather.near_ends(near3)
    me = after(grid.me, near3, sent_y0, *master_gather.line[3:])
    return added(term(me, 0, 0, 0), along_x0, along_y0, line1, line2, line3)


def all_gather(grid, own, *ties):
    line = [own] + [grid.over_z(own, LINE - dz) for dz in range(1, LINE)]
    line[1] = after(line[1], *ties)
    over_x = [grid.over_x(piece) for piece in line]
    over_y = [grid.over_y(piece) for piece in line]
    far = [grid.over_x(piece) for piece in over_y[: LINE // 2]]
    far += [grid.over_y(piece) for piece in over_x[LINE // 2 :]]
    return line + over_y + over_x + far


def relative_places(grid):
    order = [(dx, dy, dz) for dx in range(2) for dy in range(2) for dz in range(LINE)]
    return jnp.stack([place(grid.me, *where) for where in order]).astype(jnp.int32)


def whole_grams(halves):
    if lax.axis_size("col") == 2:
        return [[own, lax.ppermute(own, "col", [(0, 1), (1, 0)])] for own in halves]
    return [[lax.psum(own, "col")] for own in halves]


def updated(summed, momentum):
    new_momentum = momentum_decay * momentum + summed
    return new_momentum, half(summed + momentum_decay * new_momentum)


def per_device(gradients, momentum, master, owners):
    me = lax.axis_index("dp")
    dp_count = lax.axis_size("dp")
    matrices, row_count, width = momentum.shape
    terms = gradients[0]
    held = owners == me
    order = jnp.arange(matrices)
    rank = jnp.sum(held[None, :] & (order[None, :] < order[:, None]), axis=1)
    slots = jnp.where(held, rank, -1).astype(jnp.int32)

    in_pieces = dp_count == 4 * LINE and row_count % 32 == 0
    if in_pieces:
        grid = Grid(dp_count)
        places = relative_places(grid)
        rows = master
        master_gather = MasterGather(grid, master)
        summed = reduce_scatter(grid, terms, row_count, master_gather)
        new_momentum, own = updated(summed, momentum)
        pieces = all_gather(grid, own, master_gather.x_ends, master_gather.y_ends)
        master_gather.near_middle(*pieces[1:4])
        pieces = [piece[None] for piece in pieces]
        pieces[0] = after(pieces[0], master_gather.x_middle, master_gather.y_middle)
    else:
        places = jnp.zeros((1,), jnp.int32)
        rows = jnp.zeros((matrices, terms.shape[1], width), jnp.float32)
        rows = lax.dynamic_update_slice_in_dim(rows, master, me * row_count, axis=1)
        summed = lax.psum_scatter(terms, "dp", scatter_dimension=1, tiled=True)
        new_momentum, own = updated(summed.astype(jnp.float32), momentum)
        master_pieces = [lax.all_gather(half(master), "dp", axis=1, tiled=True)[None]]
        lies = [(0, 0)]
        pieces = [lax.all_gather(own, "dp", axis=1, tiled=True)[None]]
    update, *halves = grams(pieces)
    low, high = whole_grams(halves)
    if in_pieces:
        master_gather.far()
        master_pieces, lies = master_gather.pieces(), master_gather.lies
    chain, squares = chains(low, high)
    chain = chain.reshape(matrices, *chain.shape[2:])
    squares = squares.reshape(matrices, *squares.shape[2:])
    new_weights, new_master, owned_updates, rms = applied(
        places, slots, chain, squares, update, master_pieces, lies, rows
    )
    if not in_pieces:
        new_master = lax.dynamic_slice_in_dim(new_master, me * row_count, row_count, axis=1)
    return (new_weights, new_master, new_momentum, owned_updates[None], rms)


def solution(mesh):
    return jax.shard_map(
        per_device,
        mesh=mesh,
        in_specs=(P("dp", None, None, "col"), P(None, "dp", "col"), P(None, "dp", "col"), P()),
        out_specs=(
            P(None, None, "col"),
            P(None, "dp", "col"),
            P(None, "dp", "col"),
            P("dp", None, None, "col"),
            P("dp", None),
        ),
        check_vma=False,
    )
```

```python
import functools
import math

import jax
import jax.numpy as jnp
from jax import lax
from jax.experimental import pallas as pl
from jax.experimental.pallas import tpu as pltpu
from jax.sharding import PartitionSpec as P

KV = 512
D = 2048
MOST = 2

quintic_first = 3.4445
quintic_second = -4.775
quintic_third = 2.0315
momentum_decay = 0.95
learn_rate = 0.3
weight_decay = 0.1
epsilon = 1e-07
factor = 0.2 * math.sqrt(max(KV, D))

VMEM_LIMIT = 56 * 1024 * 1024
LINE = 4
EARLY = 2


def dot(left, right):
    return jnp.dot(left, right, preferred_element_type=jnp.float32)


def half(value):
    return value.astype(jnp.bfloat16)


def gram_kernel(order_ref, *refs):
    piece_refs, (update_ref, gram_ref) = refs[:-2], refs[-2:]
    start = 0
    for ref in piece_refs:
        rows = ref.shape[1]
        update_ref[0, start : start + rows] = ref[0]
        start += rows
    block = update_ref[0]
    gram = lax.dot_general(
        block, block, (((1,), (1,)), ((), ())), preferred_element_type=jnp.float32
    )
    gram_ref[0] = half(gram)


def grams(pieces, order):
    width = pieces[0].shape[2]
    count = order.shape[0]
    rows = sum(piece.shape[1] for piece in pieces)

    def spec(minor):
        return pl.BlockSpec((1, rows, minor), lambda i, order: (i, 0, 0))

    return pl.pallas_call(
        gram_kernel,
        grid_spec=pltpu.PrefetchScalarGridSpec(
            num_scalar_prefetch=1,
            grid=(count,),
            in_specs=[
                pl.BlockSpec((1, *piece.shape[1:]), lambda i, order: (order[i], 0, 0))
                for piece in pieces
            ],
            out_specs=[spec(width), spec(rows)],
        ),
        out_shape=[
            jax.ShapeDtypeStruct((count, rows, width), jnp.bfloat16),
            jax.ShapeDtypeStruct((count, rows, rows), jnp.bfloat16),
        ],
        compiler_params=pltpu.CompilerParams(vmem_limit_bytes=VMEM_LIMIT),
        cost_estimate=pl.CostEstimate(
            flops=2 * count * rows * rows * width,
            bytes_accessed=2 * count * rows * (2 * width + rows),
            transcendentals=0,
        ),
    )(order, *pieces)


def mixers(grams_now):
    return [
        quintic_second * gram + quintic_third * dot(half(gram), half(gram)) for gram in grams_now
    ]


def next_grams(grams_now, mixes):
    lefts = [
        quintic_first * gram + dot(half(mix), half(gram)) for gram, mix in zip(grams_now, mixes)
    ]
    return [quintic_first * left + dot(half(left), half(mix)) for left, mix in zip(lefts, mixes)]


def chain_kernel(parts, *refs):
    gram_refs = refs[:parts]
    chain_ref, squares_ref = refs[parts:]
    count, rows, _ = chain_ref.shape
    on_diagonal = lax.broadcasted_iota(jnp.int32, (rows, rows), 0) == lax.broadcasted_iota(
        jnp.int32, (rows, rows), 1
    )
    grams_now = []
    inverses = []
    for index in range(count):
        gram = gram_refs[0][index].astype(jnp.float32)
        for ref in gram_refs[1:]:
            gram = gram + ref[index].astype(jnp.float32)
        diagonal = jnp.where(on_diagonal, gram, 0.0)
        squares = jnp.sum(jnp.sum(diagonal, axis=0, keepdims=True), axis=1, keepdims=True)
        squares_ref[index] = jnp.broadcast_to(squares, squares_ref.shape[1:])
        inverse = 1.0 / (jnp.sqrt(squares) + epsilon)
        grams_now.append(gram * inverse * inverse)
        inverses.append(inverse)
    first = mixers(grams_now)
    grams_now = next_grams(grams_now, first)
    second = mixers(grams_now)
    grams_now = next_grams(grams_now, second)
    third = mixers(grams_now)
    pairs = [
        quintic_first * (m0 + m1) + dot(half(m1), half(m0)) for m0, m1 in zip(first, second)
    ]
    cubed = jnp.where(on_diagonal, quintic_first**3, 0.0)
    for index, (pair, m2) in enumerate(zip(pairs, third)):
        whole = quintic_first * pair + quintic_first**2 * m2 + dot(half(m2), half(pair))
        chain_ref[index] = half((cubed + whole) * (factor * inverses[index]))


def chains(gram_parts):
    count, rows, _ = gram_parts[0].shape
    step = 3 if count % 3 == 0 else 1
    parts = len(gram_parts)
    spec = pl.BlockSpec((step, rows, rows), lambda i: (i, 0, 0))
    return pl.pallas_call(
        functools.partial(chain_kernel, parts),
        grid=(count // step,),
        in_specs=[spec] * parts,
        out_specs=[spec, pl.BlockSpec((step, 8, 128), lambda i: (i, 0, 0))],
        out_shape=[
            jax.ShapeDtypeStruct((count, rows, rows), jnp.bfloat16),
            jax.ShapeDtypeStruct((count, 8, 128), jnp.float32),
        ],
        compiler_params=pltpu.CompilerParams(vmem_limit_bytes=VMEM_LIMIT),
        cost_estimate=pl.CostEstimate(
            flops=18 * count * rows * rows * rows,
            bytes_accessed=2 * count * rows * rows * (parts + 1),
            transcendentals=0,
        ),
    )(*gram_parts)


def apply_kernel(sets, first_count, masters, places_ref, slots_ref, order_ref, *refs):
    set_refs = [refs[3 * at : 3 * at + 3] for at in range(sets)]
    master_refs = refs[3 * sets : 3 * sets + len(masters)]
    rows_ref, weights_ref, new_rows_ref, owned_ref, rms_ref, scaled_ref = refs[-6:]
    blocks = places_ref.shape[0]
    height = scaled_ref.shape[0] // blocks
    at = pl.program_id(0)
    matrix = order_ref[at]
    slot = slots_ref[matrix]

    @pl.when(at == 0)
    def _():
        owned_ref[...] = jnp.zeros_like(owned_ref)
        rms_ref[...] = jnp.zeros_like(rms_ref)

    def span(block_at):
        return pl.ds(block_at * height, height)

    def target(block_at):
        return pl.ds(pl.multiple_of(places_ref[block_at] * height, height), height)

    lane = lax.broadcasted_iota(jnp.int32, rms_ref.shape, 1)

    def make(chain_ref, squares_ref, update_ref):
        rms = jnp.sqrt(squares_ref[0, :1, :1] / float(KV * D))
        rms_ref[...] = jnp.where(lane == slot, rms, rms_ref[...])
        scaled_ref[...] = half(dot(chain_ref[0], update_ref[0]))

    for index, chosen in enumerate(set_refs):
        pl.when((at >= first_count) == (index == 1))(functools.partial(make, *chosen))

    decayed = rows_ref[0] * (1.0 - learn_rate * weight_decay)
    new_rows_ref[0] = decayed - learn_rate * scaled_ref[span(0)].astype(jnp.float32)

    def write(master_ref):
        for block_at in range(blocks):
            place = target(block_at)
            decayed = master_ref[0, place].astype(jnp.float32) * (1.0 - learn_rate * weight_decay)
            weights_ref[0, place] = half(
                decayed - learn_rate * scaled_ref[span(block_at)].astype(jnp.float32)
            )

    for (start, stop), master_ref in zip(masters, master_refs):
        pl.when((matrix >= start) & (matrix < stop))(functools.partial(write, master_ref))

    @pl.when(slot >= 0)
    def _():
        for block_at in range(blocks):
            owned_ref[jnp.maximum(slot, 0), target(block_at)] = scaled_ref[span(block_at)]


def applied(places, slots, order, sets, master_parts, master):
    _, rows, width = sets[0][2].shape
    count, row_count, _ = master.shape
    first_count = sets[0][0].shape[0]

    def by_matrix(height, minor, start=0, stop=count):
        def index(i, places, slots, order):
            return (jnp.clip(order[i] - start, 0, stop - start - 1), 0, 0)

        return pl.BlockSpec((1, height, minor), index)

    def by_step(array, start):
        last = array.shape[0] - 1

        def index(i, *_):
            return (jnp.clip(i - start, 0, last), 0, 0)

        return pl.BlockSpec((1, *array.shape[1:]), index)

    masters = []
    for part in master_parts:
        start = masters[-1][1] if masters else 0
        masters.append((start, start + part.shape[0]))
    owned = (MOST, rows, width)
    return pl.pallas_call(
        functools.partial(apply_kernel, len(sets), first_count, masters),
        grid_spec=pltpu.PrefetchScalarGridSpec(
            num_scalar_prefetch=3,
            grid=(count,),
            in_specs=[
                by_step(array, at * first_count) for at, arrays in enumerate(sets) for array in arrays
            ]
            + [by_matrix(rows, width, *bounds) for bounds in masters]
            + [by_matrix(row_count, width)],
            out_specs=[
                by_matrix(rows, width),
                by_matrix(row_count, width),
                pl.BlockSpec(owned, lambda i, *_: (0, 0, 0)),
                pl.BlockSpec((1, MOST), lambda i, *_: (0, 0)),
            ],
            scratch_shapes=[pltpu.VMEM((rows, width), jnp.bfloat16)],
        ),
        out_shape=[
            jax.ShapeDtypeStruct((count, rows, width), jnp.bfloat16),
            jax.ShapeDtypeStruct(master.shape, jnp.float32),
            jax.ShapeDtypeStruct(owned, jnp.bfloat16),
            jax.ShapeDtypeStruct((1, MOST), jnp.float32),
        ],
        compiler_params=pltpu.CompilerParams(vmem_limit_bytes=VMEM_LIMIT),
        cost_estimate=pl.CostEstimate(
            flops=2 * count * rows * rows * width,
            bytes_accessed=2 * count * rows * (4 * width + rows),
            transcendentals=0,
        ),
    )(places, slots, order, *[array for arrays in sets for array in arrays], *master_parts, master)


class Grid:
    def __init__(self, count):
        self.count = count
        self.me = lax.axis_index("dp")
        self.x_pairs = [(d, d ^ 1) for d in range(count)]
        self.y_pairs = [(d, d ^ 2) for d in range(count)]

    def over_x(self, value):
        return lax.ppermute(value, "dp", self.x_pairs)

    def over_y(self, value):
        return lax.ppermute(value, "dp", self.y_pairs)

    def over_z(self, value, shift):
        pairs = [(d, (d // 4 + shift) % LINE * 4 + d % 4) for d in range(self.count)]
        return lax.ppermute(value, "dp", pairs)


def place(me, dx, dy, dz):
    z = ((me >> 2) + dz) & (LINE - 1)
    return z * 4 + ((me & 3) ^ (2 * dy + dx))


def after(value, *others):
    return lax.optimization_barrier((value, *others))[0]


def added(*values):
    return sum(value.astype(jnp.float32) for value in values)


def reduce_scatter(grid, terms, row_count, *ties):
    def term(me, dx, dy, dz):
        start = place(me, dx, dy, dz) * row_count
        return lax.dynamic_slice_in_dim(terms, start, row_count, axis=1)

    me = grid.me
    raw_far1, raw_far2 = term(me, 1, 1, 1), term(me, 1, 1, 2)
    me = after(grid.me, raw_far1, raw_far2, *ties)
    raw_x1, raw_far3, raw_y2 = term(me, 1, 0, 1), term(me, 1, 1, 3), term(me, 0, 1, 2)
    raw_y3, raw_far0, raw_x0 = term(me, 0, 1, 3), term(me, 1, 1, 0), term(me, 1, 0, 0)
    far1 = grid.over_x(raw_far1)
    far2 = grid.over_y(raw_far2)
    along_x1 = grid.over_x(raw_x1)
    far3 = grid.over_y(raw_far3)
    along_y2 = grid.over_y(raw_y2)

    me = after(grid.me, far1, far2, raw_y3)
    sent_x2 = half(added(term(me, 1, 0, 2), far2))
    sent_y1 = half(added(term(me, 0, 1, 1), far1))
    along_x2 = grid.over_x(sent_x2)
    along_y1 = grid.over_y(sent_y1)

    me = after(grid.me, far3, along_x1, sent_x2, sent_y1)
    sent_x3 = half(added(term(me, 1, 0, 3), far3))
    along_x3 = grid.over_x(sent_x3)
    along_y3 = grid.over_y(after(raw_y3, far3, along_x1))

    me = after(grid.me, along_y2, along_x2, sent_x3)
    near2 = half(added(term(me, 0, 0, 2), along_x2, along_y2))
    line2 = grid.over_z(near2, 2)
    far0 = grid.over_x(after(raw_far0, along_x2))

    me = after(grid.me, along_x1, along_y1, along_x3, near2)
    near1 = half(added(term(me, 0, 0, 1), along_x1, along_y1))
    line1 = grid.over_z(near1, 1)
    along_x0 = grid.over_x(after(raw_x0, along_x3))

    me = after(grid.me, along_x3, along_y3, far0, near1)
    near3 = half(added(term(me, 0, 0, 3), along_x3, along_y3))
    sent_y0 = half(added(term(me, 0, 1, 0), far0))
    line3 = grid.over_z(near3, 3)
    along_y0 = grid.over_y(sent_y0)
    me = after(grid.me, near3, sent_y0, line2)
    return added(term(me, 0, 0, 0), along_x0, along_y0, line1, line2, line3)


def all_gather(grid, own, *ties):
    line = [own] + [grid.over_z(own, LINE - dz) for dz in range(1, LINE)]
    line[1] = after(line[1], *ties)
    over_x = [grid.over_x(piece) for piece in line]
    over_y = [grid.over_y(piece) for piece in line]
    far = [grid.over_x(piece) for piece in over_y[: LINE // 2]]
    far += [grid.over_y(piece) for piece in over_x[LINE // 2 :]]
    return line + over_y + over_x + far


def relative_places(grid):
    order = [(dx, dy, dz) for dx in range(2) for dy in range(2) for dz in range(LINE)]
    return jnp.stack([place(grid.me, *where) for where in order]).astype(jnp.int32)


def updated(summed, momentum):
    new_momentum = momentum_decay * momentum + summed
    return new_momentum, half(summed + momentum_decay * new_momentum)


def per_device(gradients, momentum, master, owners):
    me = lax.axis_index("dp")
    dp_count = lax.axis_size("dp")
    matrices, row_count, width = momentum.shape
    terms = gradients[0]
    held = owners == me
    index = jnp.arange(matrices)
    rank = jnp.sum(held[None, :] & (index[None, :] < index[:, None]), axis=1)
    slots = jnp.where(held, rank, -1).astype(jnp.int32)

    in_pieces = dp_count == 4 * LINE and row_count % 32 == 0
    if in_pieces:
        grid = Grid(dp_count)
        places = relative_places(grid)
        rows = master
        early = half(master[:EARLY])
        master_parts = [lax.all_gather(early, "dp", axis=1, tiled=True)]
        summed = reduce_scatter(grid, terms, row_count, early)
        new_momentum, own = updated(summed, momentum)
        late = half(after(master[EARLY:], own))
        master_parts.append(lax.all_gather(late, "dp", axis=1, tiled=True))
        pieces = all_gather(grid, own, late)
    else:
        places = jnp.zeros((1,), jnp.int32)
        rows = jnp.zeros((matrices, terms.shape[1], width), jnp.float32)
        rows = lax.dynamic_update_slice_in_dim(rows, master, me * row_count, axis=1)
        summed = lax.psum_scatter(terms, "dp", scatter_dimension=1, tiled=True)
        new_momentum, own = updated(summed.astype(jnp.float32), momentum)
        master_parts = [lax.all_gather(half(master), "dp", axis=1, tiled=True)]
        pieces = [lax.all_gather(own, "dp", axis=1, tiled=True)]

    order = jnp.arange(matrices, dtype=jnp.int32)
    if lax.axis_size("col") == 2 and matrices % 2 == 0:
        size = matrices // 2
        order = (order + lax.axis_index("col") * size) % matrices
        mine, theirs = order[:size], order[size:]
        their_update, their_gram = grams(pieces, theirs)
        swap = [(0, 1), (1, 0)]
        other_part = lax.ppermute(their_gram, "col", swap)
        my_update, my_gram = grams(pieces, mine)
        chain, squares = chains([my_gram, other_part])
        other = [lax.ppermute(chain, "col", swap), lax.ppermute(squares, "col", swap)]
        sets = [[chain, squares, my_update], [*other, their_update]]
    else:
        update, gram = grams(pieces, order)
        sets = [[*chains([lax.psum(gram, "col")]), update]]
    new_weights, new_master, owned_updates, rms = applied(
        places, slots, order, sets, master_parts, rows
    )
    if not in_pieces:
        new_master = lax.dynamic_slice_in_dim(new_master, me * row_count, row_count, axis=1)
    return (new_weights, new_master, new_momentum, owned_updates[None], rms)


def solution(mesh):
    return jax.shard_map(
        per_device,
        mesh=mesh,
        in_specs=(P("dp", None, None, "col"), P(None, "dp", "col"), P(None, "dp", "col"), P()),
        out_specs=(
            P(None, None, "col"),
            P(None, "dp", "col"),
            P(None, "dp", "col"),
            P("dp", None, None, "col"),
            P("dp", None),
        ),
        check_vma=False,
    )
```

```python
import functools
import math

import jax
import jax.numpy as jnp
from jax import lax
from jax.experimental import pallas as pl
from jax.experimental.pallas import tpu as pltpu
from jax.sharding import PartitionSpec as P

KV = 512
D = 2048
MOST = 2

quintic_first = 3.4445
quintic_second = -4.775
quintic_third = 2.0315
momentum_decay = 0.95
learn_rate = 0.3
weight_decay = 0.1
epsilon = 1e-07
factor = 0.2 * math.sqrt(max(KV, D))

VMEM_LIMIT = 56 * 1024 * 1024
LINE = 4


def dot(left, right):
    return jnp.dot(left, right, preferred_element_type=jnp.float32)


def half(value):
    return value.astype(jnp.bfloat16)


def gram_kernel(order_ref, *refs):
    piece_refs, (update_ref, gram_ref) = refs[:-2], refs[-2:]
    start = 0
    for ref in piece_refs:
        rows = ref.shape[1]
        update_ref[0, start : start + rows] = ref[0]
        start += rows
    block = update_ref[0]
    gram = lax.dot_general(
        block, block, (((1,), (1,)), ((), ())), preferred_element_type=jnp.float32
    )
    gram_ref[0] = half(gram)


def grams(pieces, order):
    width = pieces[0].shape[2]
    count = order.shape[0]
    rows = sum(piece.shape[1] for piece in pieces)

    def spec(minor):
        return pl.BlockSpec((1, rows, minor), lambda i, order: (i, 0, 0))

    return pl.pallas_call(
        gram_kernel,
        grid_spec=pltpu.PrefetchScalarGridSpec(
            num_scalar_prefetch=1,
            grid=(count,),
            in_specs=[
                pl.BlockSpec((1, *piece.shape[1:]), lambda i, order: (order[i], 0, 0))
                for piece in pieces
            ],
            out_specs=[spec(width), spec(rows)],
        ),
        out_shape=[
            jax.ShapeDtypeStruct((count, rows, width), jnp.bfloat16),
            jax.ShapeDtypeStruct((count, rows, rows), jnp.bfloat16),
        ],
        compiler_params=pltpu.CompilerParams(vmem_limit_bytes=VMEM_LIMIT),
        cost_estimate=pl.CostEstimate(
            flops=2 * count * rows * rows * width,
            bytes_accessed=2 * count * rows * (2 * width + rows),
            transcendentals=0,
        ),
    )(order, *pieces)


def mixers(grams_now):
    return [
        quintic_second * gram + quintic_third * dot(half(gram), half(gram)) for gram in grams_now
    ]


def next_grams(grams_now, mixes):
    lefts = [
        quintic_first * gram + dot(half(mix), half(gram)) for gram, mix in zip(grams_now, mixes)
    ]
    return [quintic_first * left + dot(half(left), half(mix)) for left, mix in zip(lefts, mixes)]


def chain_kernel(parts, *refs):
    gram_refs = refs[:parts]
    chain_ref, squares_ref = refs[parts:]
    count, rows, _ = chain_ref.shape
    on_diagonal = lax.broadcasted_iota(jnp.int32, (rows, rows), 0) == lax.broadcasted_iota(
        jnp.int32, (rows, rows), 1
    )
    grams_now = []
    inverses = []
    for index in range(count):
        gram = gram_refs[0][index].astype(jnp.float32)
        for ref in gram_refs[1:]:
            gram = gram + ref[index].astype(jnp.float32)
        diagonal = jnp.where(on_diagonal, gram, 0.0)
        squares = jnp.sum(jnp.sum(diagonal, axis=0, keepdims=True), axis=1, keepdims=True)
        squares_ref[index] = jnp.broadcast_to(squares, squares_ref.shape[1:])
        inverse = 1.0 / (jnp.sqrt(squares) + epsilon)
        grams_now.append(gram * inverse * inverse)
        inverses.append(inverse)
    first = mixers(grams_now)
    grams_now = next_grams(grams_now, first)
    second = mixers(grams_now)
    grams_now = next_grams(grams_now, second)
    third = mixers(grams_now)
    pairs = [
        quintic_first * (m0 + m1) + dot(half(m1), half(m0)) for m0, m1 in zip(first, second)
    ]
    cubed = jnp.where(on_diagonal, quintic_first**3, 0.0)
    for index, (pair, m2) in enumerate(zip(pairs, third)):
        whole = quintic_first * pair + quintic_first**2 * m2 + dot(half(m2), half(pair))
        chain_ref[index] = half((cubed + whole) * (factor * inverses[index]))


def chains(gram_parts):
    count, rows, _ = gram_parts[0].shape
    step = 3 if count % 3 == 0 else 1
    parts = len(gram_parts)
    spec = pl.BlockSpec((step, rows, rows), lambda i: (i, 0, 0))
    return pl.pallas_call(
        functools.partial(chain_kernel, parts),
        grid=(count // step,),
        in_specs=[spec] * parts,
        out_specs=[spec, pl.BlockSpec((step, 8, 128), lambda i: (i, 0, 0))],
        out_shape=[
            jax.ShapeDtypeStruct((count, rows, rows), jnp.bfloat16),
            jax.ShapeDtypeStruct((count, 8, 128), jnp.float32),
        ],
        compiler_params=pltpu.CompilerParams(vmem_limit_bytes=VMEM_LIMIT),
        cost_estimate=pl.CostEstimate(
            flops=18 * count * rows * rows * rows,
            bytes_accessed=2 * count * rows * rows * (parts + 1),
            transcendentals=0,
        ),
    )(*gram_parts)


def apply_kernel(sets, first_count, lies, places_ref, spans_ref, slots_ref, order_ref, *refs):
    set_refs = [refs[3 * at : 3 * at + 3] for at in range(sets)]
    master_refs = refs[3 * sets : -6]
    rows_ref, weights_ref, new_rows_ref, owned_ref, rms_ref, scaled_ref = refs[-6:]
    blocks = len(lies)
    height = scaled_ref.shape[0] // blocks
    at = pl.program_id(0)
    slot = slots_ref[order_ref[at]]

    @pl.when(at == 0)
    def _():
        owned_ref[...] = jnp.zeros_like(owned_ref)
        rms_ref[...] = jnp.zeros_like(rms_ref)

    def block_of(ref, block_at):
        return pl.ds(pl.multiple_of(ref[block_at] * height, height), height)

    lane = lax.broadcasted_iota(jnp.int32, rms_ref.shape, 1)

    def make(chain_ref, squares_ref, update_ref):
        rms = jnp.sqrt(squares_ref[0, :1, :1] / float(KV * D))
        rms_ref[...] = jnp.where(lane == slot, rms, rms_ref[...])
        scaled_ref[...] = half(dot(chain_ref[0], update_ref[0]))

    for index, chosen in enumerate(set_refs):
        pl.when((at >= first_count) == (index == 1))(functools.partial(make, *chosen))

    decayed = rows_ref[0] * (1.0 - learn_rate * weight_decay)
    new_rows_ref[0] = decayed - learn_rate * scaled_ref[:height].astype(jnp.float32)
    for block_at, (piece, where) in enumerate(lies):
        decayed = master_refs[piece][where, 0].astype(jnp.float32) * (
            1.0 - learn_rate * weight_decay
        )
        scaled = scaled_ref[block_of(spans_ref, block_at)]
        weights_ref[0, block_of(places_ref, block_at)] = half(
            decayed - learn_rate * scaled.astype(jnp.float32)
        )

    @pl.when(slot >= 0)
    def _():
        for block_at in range(blocks):
            owned_ref[jnp.maximum(slot, 0), block_of(places_ref, block_at)] = scaled_ref[
                block_of(spans_ref, block_at)
            ]


def applied(places, spans, slots, order, sets, master_pieces, lies, master):
    _, rows, width = sets[0][2].shape
    count, row_count, _ = master.shape
    first_count = sets[0][0].shape[0]

    def by_matrix(height, minor):
        def index(i, places, spans, slots, order):
            return (order[i], 0, 0)

        return pl.BlockSpec((1, height, minor), index)

    def by_piece(piece):
        def index(i, places, spans, slots, order):
            return (0, order[i], 0, 0)

        return pl.BlockSpec((piece.shape[0], 1, *piece.shape[2:]), index)

    def by_step(array, start):
        last = array.shape[0] - 1

        def index(i, *_):
            return (jnp.clip(i - start, 0, last), 0, 0)

        return pl.BlockSpec((1, *array.shape[1:]), index)

    owned = (MOST, rows, width)
    return pl.pallas_call(
        functools.partial(apply_kernel, len(sets), first_count, lies),
        grid_spec=pltpu.PrefetchScalarGridSpec(
            num_scalar_prefetch=4,
            grid=(count,),
            in_specs=[
                by_step(array, at * first_count) for at, arrays in enumerate(sets) for array in arrays
            ]
            + [by_piece(piece) for piece in master_pieces]
            + [by_matrix(row_count, width)],
            out_specs=[
                by_matrix(rows, width),
                by_matrix(row_count, width),
                pl.BlockSpec(owned, lambda i, *_: (0, 0, 0)),
                pl.BlockSpec((1, MOST), lambda i, *_: (0, 0)),
            ],
            scratch_shapes=[pltpu.VMEM((rows, width), jnp.bfloat16)],
        ),
        out_shape=[
            jax.ShapeDtypeStruct((count, rows, width), jnp.bfloat16),
            jax.ShapeDtypeStruct(master.shape, jnp.float32),
            jax.ShapeDtypeStruct(owned, jnp.bfloat16),
            jax.ShapeDtypeStruct((1, MOST), jnp.float32),
        ],
        compiler_params=pltpu.CompilerParams(vmem_limit_bytes=VMEM_LIMIT),
        cost_estimate=pl.CostEstimate(
            flops=2 * count * rows * rows * width,
            bytes_accessed=2 * count * rows * (4 * width + rows),
            transcendentals=0,
        ),
    )(
        places,
        spans,
        slots,
        order,
        *[array for arrays in sets for array in arrays],
        *master_pieces,
        master,
    )


class Grid:
    def __init__(self, count):
        self.count = count
        self.me = lax.axis_index("dp")
        self.x_pairs = [(d, d ^ 1) for d in range(count)]
        self.y_pairs = [(d, d ^ 2) for d in range(count)]

    def over_x(self, value):
        return lax.ppermute(value, "dp", self.x_pairs)

    def over_y(self, value):
        return lax.ppermute(value, "dp", self.y_pairs)

    def over_z(self, value, shift):
        pairs = [(d, (d // 4 + shift) % LINE * 4 + d % 4) for d in range(self.count)]
        return lax.ppermute(value, "dp", pairs)


def place(me, dx, dy, dz):
    z = ((me >> 2) + dz) & (LINE - 1)
    return z * 4 + ((me & 3) ^ (2 * dy + dx))


def after(value, *others):
    return lax.optimization_barrier((value, *others))[0]


def added(*values):
    return sum(value.astype(jnp.float32) for value in values)


class MasterGather:
    lies = [(0, z) for z in range(LINE)]
    lies += [(1 + 3 * (z // 2), z % 2) for z in range(LINE)]
    lies += [(2 + 3 * (z // 2), z % 2) for z in range(LINE)]
    lies += [(3 + 3 * (z // 2), z % 2) for z in range(LINE)]

    def __init__(self, grid, master):
        self.grid = grid
        lines = [[z * 4 + corner for z in range(LINE)] for corner in range(4)]
        self.own = half(master)
        self.line = lax.all_gather(self.own, "dp", axis_index_groups=lines)

    def low(self, *ties):
        line = after(self.line, *ties)
        self.low_y = self.grid.over_y(line[: LINE // 2])
        self.low_x = self.grid.over_x(line[: LINE // 2])

    def high(self, *ties):
        line = after(self.line, *ties)
        self.high_y = self.grid.over_y(line[LINE // 2 :])
        self.high_x = self.grid.over_x(line[LINE // 2 :])

    def far(self):
        self.low_far = self.grid.over_x(after(self.low_y, self.high_x))
        self.high_far = self.grid.over_y(self.high_x)

    def pieces(self):
        low = [self.low_y, self.low_x, self.low_far]
        return [self.line, *low, self.high_y, self.high_x, self.high_far]

    def places(self):
        corner, z_mine = self.grid.me & 3, self.grid.me >> 2
        places = [z * 4 + (corner ^ (2 * dy + dx)) for dx in range(2) for dy in range(2) for z in range(LINE)]
        spans = [at * 4 + ((z - z_mine) & (LINE - 1)) for at in range(4) for z in range(LINE)]
        return jnp.stack(places).astype(jnp.int32), jnp.stack(spans).astype(jnp.int32)


def reduce_scatter(grid, terms, row_count, master_gather):
    def term(me, dx, dy, dz):
        start = place(me, dx, dy, dz) * row_count
        return lax.dynamic_slice_in_dim(terms, start, row_count, axis=1)

    me = grid.me
    raw_far1, raw_far2 = term(me, 1, 1, 1), term(me, 1, 1, 2)
    me = after(grid.me, raw_far1, raw_far2, master_gather.own)
    raw_x1, raw_far3, raw_y2 = term(me, 1, 0, 1), term(me, 1, 1, 3), term(me, 0, 1, 2)
    raw_y3, raw_far0, raw_x0 = term(me, 0, 1, 3), term(me, 1, 1, 0), term(me, 1, 0, 0)
    far1 = grid.over_x(raw_far1)
    far2 = grid.over_y(raw_far2)
    along_x1 = grid.over_x(raw_x1)
    far3 = grid.over_y(raw_far3)
    along_y2 = grid.over_y(raw_y2)

    me = after(grid.me, far1, far2, raw_y3)
    sent_x2 = half(added(term(me, 1, 0, 2), far2))
    sent_y1 = half(added(term(me, 0, 1, 1), far1))
    along_x2 = grid.over_x(sent_x2)
    along_y1 = grid.over_y(sent_y1)

    me = after(grid.me, far3, along_x1, sent_x2, sent_y1)
    sent_x3 = half(added(term(me, 1, 0, 3), far3))
    along_x3 = grid.over_x(sent_x3)
    along_y3 = grid.over_y(after(raw_y3, far3, along_x1))

    me = after(grid.me, along_y2, along_x2, sent_x3)
    near2 = half(added(term(me, 0, 0, 2), along_x2, along_y2))
    line2 = grid.over_z(near2, 2)
    far0 = grid.over_x(after(raw_far0, along_x2))

    me = after(grid.me, along_x1, along_y1, along_x3, near2)
    near1 = half(added(term(me, 0, 0, 1), along_x1, along_y1))
    line1 = grid.over_z(near1, 1)
    along_x0 = grid.over_x(after(raw_x0, along_x3))

    me = after(grid.me, along_x3, along_y3, far0, near1)
    near3 = half(added(term(me, 0, 0, 3), along_x3, along_y3))
    sent_y0 = half(added(term(me, 0, 1, 0), far0))
    line3 = grid.over_z(near3, 3)
    master_gather.low(sent_y0, near3)
    along_y0 = grid.over_y(sent_y0)
    me = after(grid.me, near3, sent_y0, line2)
    return added(term(me, 0, 0, 0), along_x0, along_y0, line1, line2, line3)


def all_gather(grid, own, *ties):
    x0, y0 = grid.over_x(own), grid.over_y(own)
    z1, z3 = grid.over_z(own, LINE - 1), grid.over_z(own, 1)
    far0 = grid.over_x(y0)
    x1, y1 = grid.over_x(z1), grid.over_y(z1)
    x3, y3 = grid.over_x(z3), grid.over_y(z3)
    z2 = grid.over_z(after(own, z1, z3, *ties), 2)
    far3 = grid.over_y(x3)
    x2, y2 = grid.over_x(z2), grid.over_y(z2)
    far1 = grid.over_x(y1)
    far2 = grid.over_y(x2)
    return [own, z1, z2, z3, y0, y1, y2, y3, x0, x1, x2, x3, far0, far1, far2, far3]


def updated(summed, momentum):
    new_momentum = momentum_decay * momentum + summed
    return new_momentum, half(summed + momentum_decay * new_momentum)


def per_device(gradients, momentum, master, owners):
    me = lax.axis_index("dp")
    dp_count = lax.axis_size("dp")
    matrices, row_count, width = momentum.shape
    terms = gradients[0]
    held = owners == me
    index = jnp.arange(matrices)
    rank = jnp.sum(held[None, :] & (index[None, :] < index[:, None]), axis=1)
    slots = jnp.where(held, rank, -1).astype(jnp.int32)

    in_pieces = dp_count == 4 * LINE and row_count % 32 == 0
    if in_pieces:
        grid = Grid(dp_count)
        rows = master
        master_gather = MasterGather(grid, master)
        places, spans = master_gather.places()
        summed = reduce_scatter(grid, terms, row_count, master_gather)
        new_momentum, own = updated(summed, momentum)
        pieces = all_gather(grid, own, master_gather.low_x, master_gather.low_y)
        master_gather.high(pieces[1], pieces[2], pieces[3])
        master_gather.far()
        master_pieces, lies = master_gather.pieces(), master_gather.lies
    else:
        places = spans = jnp.zeros((1,), jnp.int32)
        rows = jnp.zeros((matrices, terms.shape[1], width), jnp.float32)
        rows = lax.dynamic_update_slice_in_dim(rows, master, me * row_count, axis=1)
        summed = lax.psum_scatter(terms, "dp", scatter_dimension=1, tiled=True)
        new_momentum, own = updated(summed.astype(jnp.float32), momentum)
        master_pieces = [lax.all_gather(half(master), "dp", axis=1, tiled=True)[None]]
        lies = [(0, 0)]
        pieces = [lax.all_gather(own, "dp", axis=1, tiled=True)]

    order = jnp.arange(matrices, dtype=jnp.int32)
    if lax.axis_size("col") == 2 and matrices % 2 == 0:
        size = matrices // 2
        order = (order + lax.axis_index("col") * size) % matrices
        mine, theirs = order[:size], order[size:]
        their_update, their_gram = grams(pieces, theirs)
        swap = [(0, 1), (1, 0)]
        other_part = lax.ppermute(their_gram, "col", swap)
        my_update, my_gram = grams(pieces, mine)
        if in_pieces:
            other_part = after(other_part, master_gather.high_x, master_gather.high_y)
        chain, squares = chains([my_gram, other_part])
        sent = chain
        if in_pieces:
            sent = after(chain, master_gather.low_far, master_gather.high_far)
        other = [lax.ppermute(sent, "col", swap), lax.ppermute(squares, "col", swap)]
        sets = [[chain, squares, my_update], [*other, their_update]]
    else:
        update, gram = grams(pieces, order)
        sets = [[*chains([lax.psum(gram, "col")]), update]]
    new_weights, new_master, owned_updates, rms = applied(
        places, spans, slots, order, sets, master_pieces, lies, rows
    )
    if not in_pieces:
        new_master = lax.dynamic_slice_in_dim(new_master, me * row_count, row_count, axis=1)
    return (new_weights, new_master, new_momentum, owned_updates[None], rms)


def solution(mesh):
    return jax.shard_map(
        per_device,
        mesh=mesh,
        in_specs=(P("dp", None, None, "col"), P(None, "dp", "col"), P(None, "dp", "col"), P()),
        out_specs=(
            P(None, None, "col"),
            P(None, "dp", "col"),
            P(None, "dp", "col"),
            P("dp", None, None, "col"),
            P("dp", None),
        ),
        check_vma=False,
    )
```

```python
import functools
import math

import jax
import jax.numpy as jnp
from jax import lax
from jax.experimental import pallas as pl
from jax.experimental.pallas import tpu as pltpu
from jax.sharding import PartitionSpec as P

KV = 512
D = 2048
MOST = 2

quintic_first = 3.4445
quintic_second = -4.775
quintic_third = 2.0315
momentum_decay = 0.95
learn_rate = 0.3
weight_decay = 0.1
epsilon = 1e-07
factor = 0.2 * math.sqrt(max(KV, D))

VMEM_LIMIT = 56 * 1024 * 1024
LINE = 4


def dot(left, right):
    return jnp.dot(left, right, preferred_element_type=jnp.float32)


def half(value):
    return value.astype(jnp.bfloat16)


def gram_kernel(order_ref, *refs):
    piece_refs, (update_ref, gram_ref) = refs[:-2], refs[-2:]
    start = 0
    for ref in piece_refs:
        rows = ref.shape[1]
        update_ref[0, start : start + rows] = ref[0]
        start += rows
    block = update_ref[0]
    gram = lax.dot_general(
        block, block, (((1,), (1,)), ((), ())), preferred_element_type=jnp.float32
    )
    gram_ref[0] = half(gram)


def grams(pieces, order):
    width = pieces[0].shape[2]
    count = order.shape[0]
    rows = sum(piece.shape[1] for piece in pieces)

    def spec(minor):
        return pl.BlockSpec((1, rows, minor), lambda i, order: (i, 0, 0))

    return pl.pallas_call(
        gram_kernel,
        grid_spec=pltpu.PrefetchScalarGridSpec(
            num_scalar_prefetch=1,
            grid=(count,),
            in_specs=[
                pl.BlockSpec((1, *piece.shape[1:]), lambda i, order: (order[i], 0, 0))
                for piece in pieces
            ],
            out_specs=[spec(width), spec(rows)],
        ),
        out_shape=[
            jax.ShapeDtypeStruct((count, rows, width), jnp.bfloat16),
            jax.ShapeDtypeStruct((count, rows, rows), jnp.bfloat16),
        ],
        compiler_params=pltpu.CompilerParams(vmem_limit_bytes=VMEM_LIMIT),
        cost_estimate=pl.CostEstimate(
            flops=2 * count * rows * rows * width,
            bytes_accessed=2 * count * rows * (2 * width + rows),
            transcendentals=0,
        ),
    )(order, *pieces)


def mixers(grams_now):
    return [
        quintic_second * gram + quintic_third * dot(half(gram), half(gram)) for gram in grams_now
    ]


def next_grams(grams_now, mixes):
    lefts = [
        quintic_first * gram + dot(half(mix), half(gram)) for gram, mix in zip(grams_now, mixes)
    ]
    return [quintic_first * left + dot(half(left), half(mix)) for left, mix in zip(lefts, mixes)]


def chain_kernel(parts, *refs):
    gram_refs = refs[:parts]
    chain_ref, squares_ref = refs[parts:]
    count, rows, _ = chain_ref.shape
    on_diagonal = lax.broadcasted_iota(jnp.int32, (rows, rows), 0) == lax.broadcasted_iota(
        jnp.int32, (rows, rows), 1
    )
    grams_now = []
    inverses = []
    for index in range(count):
        gram = gram_refs[0][index].astype(jnp.float32)
        for ref in gram_refs[1:]:
            gram = gram + ref[index].astype(jnp.float32)
        diagonal = jnp.where(on_diagonal, gram, 0.0)
        squares = jnp.sum(jnp.sum(diagonal, axis=0, keepdims=True), axis=1, keepdims=True)
        squares_ref[index] = jnp.broadcast_to(squares, squares_ref.shape[1:])
        inverse = 1.0 / (jnp.sqrt(squares) + epsilon)
        grams_now.append(gram * inverse * inverse)
        inverses.append(inverse)
    first = mixers(grams_now)
    grams_now = next_grams(grams_now, first)
    second = mixers(grams_now)
    grams_now = next_grams(grams_now, second)
    third = mixers(grams_now)
    pairs = [
        quintic_first * (m0 + m1) + dot(half(m1), half(m0)) for m0, m1 in zip(first, second)
    ]
    cubed = jnp.where(on_diagonal, quintic_first**3, 0.0)
    for index, (pair, m2) in enumerate(zip(pairs, third)):
        whole = quintic_first * pair + quintic_first**2 * m2 + dot(half(m2), half(pair))
        chain_ref[index] = half((cubed + whole) * (factor * inverses[index]))


def chains(gram_parts):
    count, rows, _ = gram_parts[0].shape
    step = 3 if count % 3 == 0 else 1
    parts = len(gram_parts)
    spec = pl.BlockSpec((step, rows, rows), lambda i: (i, 0, 0))
    return pl.pallas_call(
        functools.partial(chain_kernel, parts),
        grid=(count // step,),
        in_specs=[spec] * parts,
        out_specs=[spec, pl.BlockSpec((step, 8, 128), lambda i: (i, 0, 0))],
        out_shape=[
            jax.ShapeDtypeStruct((count, rows, rows), jnp.bfloat16),
            jax.ShapeDtypeStruct((count, 8, 128), jnp.float32),
        ],
        compiler_params=pltpu.CompilerParams(vmem_limit_bytes=VMEM_LIMIT),
        cost_estimate=pl.CostEstimate(
            flops=18 * count * rows * rows * rows,
            bytes_accessed=2 * count * rows * rows * (parts + 1),
            transcendentals=0,
        ),
    )(*gram_parts)


def apply_kernel(sets, first_count, lies, places_ref, spans_ref, slots_ref, order_ref, *refs):
    set_refs = [refs[3 * at : 3 * at + 3] for at in range(sets)]
    master_refs = refs[3 * sets : -6]
    rows_ref, weights_ref, new_rows_ref, owned_ref, rms_ref, scaled_ref = refs[-6:]
    blocks = len(lies)
    height = scaled_ref.shape[0] // blocks
    at = pl.program_id(0)
    slot = slots_ref[order_ref[at]]

    @pl.when(at == 0)
    def _():
        owned_ref[...] = jnp.zeros_like(owned_ref)
        rms_ref[...] = jnp.zeros_like(rms_ref)

    def block_of(ref, block_at):
        return pl.ds(pl.multiple_of(ref[block_at] * height, height), height)

    lane = lax.broadcasted_iota(jnp.int32, rms_ref.shape, 1)

    def make(chain_ref, squares_ref, update_ref):
        rms = jnp.sqrt(squares_ref[0, :1, :1] / float(KV * D))
        rms_ref[...] = jnp.where(lane == slot, rms, rms_ref[...])
        scaled_ref[...] = half(dot(chain_ref[0], update_ref[0]))

    for index, chosen in enumerate(set_refs):
        pl.when((at >= first_count) == (index == 1))(functools.partial(make, *chosen))

    decayed = rows_ref[0] * (1.0 - learn_rate * weight_decay)
    new_rows_ref[0] = decayed - learn_rate * scaled_ref[:height].astype(jnp.float32)
    for block_at, (piece, where) in enumerate(lies):
        decayed = master_refs[piece][where, 0].astype(jnp.float32) * (
            1.0 - learn_rate * weight_decay
        )
        scaled = scaled_ref[block_of(spans_ref, block_at)]
        weights_ref[0, block_of(places_ref, block_at)] = half(
            decayed - learn_rate * scaled.astype(jnp.float32)
        )

    @pl.when(slot >= 0)
    def _():
        for block_at in range(blocks):
            owned_ref[jnp.maximum(slot, 0), block_of(places_ref, block_at)] = scaled_ref[
                block_of(spans_ref, block_at)
            ]


def applied(places, spans, slots, order, sets, master_pieces, lies, master):
    _, rows, width = sets[0][2].shape
    count, row_count, _ = master.shape
    first_count = sets[0][0].shape[0]

    def by_matrix(height, minor):
        def index(i, places, spans, slots, order):
            return (order[i], 0, 0)

        return pl.BlockSpec((1, height, minor), index)

    def by_piece(piece):
        def index(i, places, spans, slots, order):
            return (0, order[i], 0, 0)

        return pl.BlockSpec((piece.shape[0], 1, *piece.shape[2:]), index)

    def by_step(array, start):
        last = array.shape[0] - 1

        def index(i, *_):
            return (jnp.clip(i - start, 0, last), 0, 0)

        return pl.BlockSpec((1, *array.shape[1:]), index)

    owned = (MOST, rows, width)
    return pl.pallas_call(
        functools.partial(apply_kernel, len(sets), first_count, lies),
        grid_spec=pltpu.PrefetchScalarGridSpec(
            num_scalar_prefetch=4,
            grid=(count,),
            in_specs=[
                by_step(array, at * first_count) for at, arrays in enumerate(sets) for array in arrays
            ]
            + [by_piece(piece) for piece in master_pieces]
            + [by_matrix(row_count, width)],
            out_specs=[
                by_matrix(rows, width),
                by_matrix(row_count, width),
                pl.BlockSpec(owned, lambda i, *_: (0, 0, 0)),
                pl.BlockSpec((1, MOST), lambda i, *_: (0, 0)),
            ],
            scratch_shapes=[pltpu.VMEM((rows, width), jnp.bfloat16)],
        ),
        out_shape=[
            jax.ShapeDtypeStruct((count, rows, width), jnp.bfloat16),
            jax.ShapeDtypeStruct(master.shape, jnp.float32),
            jax.ShapeDtypeStruct(owned, jnp.bfloat16),
            jax.ShapeDtypeStruct((1, MOST), jnp.float32),
        ],
        compiler_params=pltpu.CompilerParams(vmem_limit_bytes=VMEM_LIMIT),
        cost_estimate=pl.CostEstimate(
            flops=2 * count * rows * rows * width,
            bytes_accessed=2 * count * rows * (4 * width + rows),
            transcendentals=0,
        ),
    )(
        places,
        spans,
        slots,
        order,
        *[array for arrays in sets for array in arrays],
        *master_pieces,
        master,
    )


class Grid:
    def __init__(self, count):
        self.count = count
        self.me = lax.axis_index("dp")
        self.x_pairs = [(d, d ^ 1) for d in range(count)]
        self.y_pairs = [(d, d ^ 2) for d in range(count)]

    def over_x(self, value):
        return lax.ppermute(value, "dp", self.x_pairs)

    def over_y(self, value):
        return lax.ppermute(value, "dp", self.y_pairs)

    def over_z(self, value, shift):
        pairs = [(d, (d // 4 + shift) % LINE * 4 + d % 4) for d in range(self.count)]
        return lax.ppermute(value, "dp", pairs)


def place(me, dx, dy, dz):
    z = ((me >> 2) + dz) & (LINE - 1)
    return z * 4 + ((me & 3) ^ (2 * dy + dx))


def after(value, *others):
    return lax.optimization_barrier((value, *others))[0]


def added(*values):
    return sum(value.astype(jnp.float32) for value in values)


class MasterGather:
    lies = [(0, at) for at in range(4 * LINE)]

    def __init__(self, grid, master):
        self.grid = grid
        lines = [[z * 4 + corner for z in range(LINE)] for corner in range(4)]
        self.own = half(master)
        self.line = lax.all_gather(self.own, "dp", axis_index_groups=lines)

    def plane(self, *ties):
        planes = [[z * 4 + corner for corner in range(4)] for z in range(LINE)]
        line = after(self.line, *ties)
        gathered = lax.all_gather(line, "dp", axis_index_groups=planes)
        return gathered.reshape(4 * LINE, *self.own.shape)

    def places(self):
        places = [z * 4 + corner for corner in range(4) for z in range(LINE)]
        corner_mine, z_mine = self.grid.me & 3, self.grid.me >> 2
        spans = []
        for corner in range(4):
            apart = corner ^ corner_mine
            dx, dy = apart & 1, apart >> 1
            spans += [(dx * 2 + dy) * 4 + ((z - z_mine) & (LINE - 1)) for z in range(LINE)]
        return jnp.array(places, jnp.int32), jnp.stack(spans).astype(jnp.int32)


def reduce_scatter(grid, terms, row_count, master_gather):
    def term(me, dx, dy, dz):
        start = place(me, dx, dy, dz) * row_count
        return lax.dynamic_slice_in_dim(terms, start, row_count, axis=1)

    me = grid.me
    raw_far1, raw_far2 = term(me, 1, 1, 1), term(me, 1, 1, 2)
    me = after(grid.me, raw_far1, raw_far2, master_gather.own)
    raw_x1, raw_far3, raw_y2 = term(me, 1, 0, 1), term(me, 1, 1, 3), term(me, 0, 1, 2)
    raw_y3, raw_far0, raw_x0 = term(me, 0, 1, 3), term(me, 1, 1, 0), term(me, 1, 0, 0)
    far1 = grid.over_x(raw_far1)
    far2 = grid.over_y(raw_far2)
    along_x1 = grid.over_x(raw_x1)
    far3 = grid.over_y(raw_far3)
    along_y2 = grid.over_y(raw_y2)

    me = after(grid.me, far1, far2, raw_y3)
    sent_x2 = half(added(term(me, 1, 0, 2), far2))
    sent_y1 = half(added(term(me, 0, 1, 1), far1))
    along_x2 = grid.over_x(sent_x2)
    along_y1 = grid.over_y(sent_y1)

    me = after(grid.me, far3, along_x1, sent_x2, sent_y1)
    sent_x3 = half(added(term(me, 1, 0, 3), far3))
    along_x3 = grid.over_x(sent_x3)
    along_y3 = grid.over_y(after(raw_y3, far3, along_x1))

    me = after(grid.me, along_y2, along_x2, sent_x3)
    near2 = half(added(term(me, 0, 0, 2), along_x2, along_y2))
    line2 = grid.over_z(near2, 2)
    far0 = grid.over_x(after(raw_far0, along_x2))

    me = after(grid.me, along_x1, along_y1, along_x3, near2)
    near1 = half(added(term(me, 0, 0, 1), along_x1, along_y1))
    line1 = grid.over_z(near1, 1)
    along_x0 = grid.over_x(after(raw_x0, along_x3))

    me = after(grid.me, along_x3, along_y3, far0, near1)
    near3 = half(added(term(me, 0, 0, 3), along_x3, along_y3))
    sent_y0 = half(added(term(me, 0, 1, 0), far0))
    line3 = grid.over_z(near3, 3)
    along_y0 = grid.over_y(sent_y0)
    me = after(grid.me, near3, sent_y0, line2)
    return added(term(me, 0, 0, 0), along_x0, along_y0, line1, line2, line3)


def all_gather(grid, own):
    x0, y0 = grid.over_x(own), grid.over_y(own)
    z1, z3 = grid.over_z(own, LINE - 1), grid.over_z(own, 1)
    far0 = grid.over_x(y0)
    x1, y1 = grid.over_x(z1), grid.over_y(z1)
    x3, y3 = grid.over_x(z3), grid.over_y(z3)
    z2 = grid.over_z(after(own, z1, z3), 2)
    far3 = grid.over_y(x3)
    x2, y2 = grid.over_x(z2), grid.over_y(z2)
    far1 = grid.over_x(y1)
    far2 = grid.over_y(x2)
    return [own, z1, z2, z3, y0, y1, y2, y3, x0, x1, x2, x3, far0, far1, far2, far3]


def updated(summed, momentum):
    new_momentum = momentum_decay * momentum + summed
    return new_momentum, half(summed + momentum_decay * new_momentum)


def per_device(gradients, momentum, master, owners):
    me = lax.axis_index("dp")
    dp_count = lax.axis_size("dp")
    matrices, row_count, width = momentum.shape
    terms = gradients[0]
    held = owners == me
    index = jnp.arange(matrices)
    rank = jnp.sum(held[None, :] & (index[None, :] < index[:, None]), axis=1)
    slots = jnp.where(held, rank, -1).astype(jnp.int32)

    in_pieces = dp_count == 4 * LINE and row_count % 32 == 0
    if in_pieces:
        grid = Grid(dp_count)
        rows = master
        master_gather = MasterGather(grid, master)
        places, spans = master_gather.places()
        summed = reduce_scatter(grid, terms, row_count, master_gather)
        new_momentum, own = updated(summed, momentum)
        master_pieces, lies = [master_gather.plane(own)], master_gather.lies
        pieces = all_gather(grid, own)
    else:
        places = spans = jnp.zeros((1,), jnp.int32)
        rows = jnp.zeros((matrices, terms.shape[1], width), jnp.float32)
        rows = lax.dynamic_update_slice_in_dim(rows, master, me * row_count, axis=1)
        summed = lax.psum_scatter(terms, "dp", scatter_dimension=1, tiled=True)
        new_momentum, own = updated(summed.astype(jnp.float32), momentum)
        master_pieces = [lax.all_gather(half(master), "dp", axis=1, tiled=True)[None]]
        lies = [(0, 0)]
        pieces = [lax.all_gather(own, "dp", axis=1, tiled=True)]

    order = jnp.arange(matrices, dtype=jnp.int32)
    if lax.axis_size("col") == 2 and matrices % 2 == 0:
        size = matrices // 2
        order = (order + lax.axis_index("col") * size) % matrices
        mine, theirs = order[:size], order[size:]
        their_update, their_gram = grams(pieces, theirs)
        swap = [(0, 1), (1, 0)]
        other_part = lax.ppermute(their_gram, "col", swap)
        my_update, my_gram = grams(pieces, mine)
        chain, squares = chains([my_gram, other_part])
        other = [lax.ppermute(chain, "col", swap), lax.ppermute(squares, "col", swap)]
        sets = [[chain, squares, my_update], [*other, their_update]]
    else:
        update, gram = grams(pieces, order)
        sets = [[*chains([lax.psum(gram, "col")]), update]]
    new_weights, new_master, owned_updates, rms = applied(
        places, spans, slots, order, sets, master_pieces, lies, rows
    )
    if not in_pieces:
        new_master = lax.dynamic_slice_in_dim(new_master, me * row_count, row_count, axis=1)
    return (new_weights, new_master, new_momentum, owned_updates[None], rms)


def solution(mesh):
    return jax.shard_map(
        per_device,
        mesh=mesh,
        in_specs=(P("dp", None, None, "col"), P(None, "dp", "col"), P(None, "dp", "col"), P()),
        out_specs=(
            P(None, None, "col"),
            P(None, "dp", "col"),
            P(None, "dp", "col"),
            P("dp", None, None, "col"),
            P("dp", None),
        ),
        check_vma=False,
    )
```

```python
import functools
import math

import jax
import jax.numpy as jnp
from jax import lax
from jax.experimental import pallas as pl
from jax.experimental.pallas import tpu as pltpu
from jax.sharding import PartitionSpec as P

KV = 512
D = 2048
MOST = 2

quintic_first = 3.4445
quintic_second = -4.775
quintic_third = 2.0315
momentum_decay = 0.95
learn_rate = 0.3
weight_decay = 0.1
epsilon = 1e-07
factor = 0.2 * math.sqrt(max(KV, D))

VMEM_LIMIT = 56 * 1024 * 1024
LINE = 4


def dot(left, right):
    return jnp.dot(left, right, preferred_element_type=jnp.float32)


def half(value):
    return value.astype(jnp.bfloat16)


def gram_kernel(order_ref, *refs):
    piece_refs, (update_ref, gram_ref) = refs[:-2], refs[-2:]
    start = 0
    for ref in piece_refs:
        rows = ref.shape[1]
        update_ref[0, start : start + rows] = ref[0]
        start += rows
    block = update_ref[0]
    gram = lax.dot_general(
        block, block, (((1,), (1,)), ((), ())), preferred_element_type=jnp.float32
    )
    gram_ref[0] = half(gram)


def grams(pieces, order):
    width = pieces[0].shape[2]
    count = order.shape[0]
    rows = sum(piece.shape[1] for piece in pieces)

    def spec(minor):
        return pl.BlockSpec((1, rows, minor), lambda i, order: (i, 0, 0))

    return pl.pallas_call(
        gram_kernel,
        grid_spec=pltpu.PrefetchScalarGridSpec(
            num_scalar_prefetch=1,
            grid=(count,),
            in_specs=[
                pl.BlockSpec((1, *piece.shape[1:]), lambda i, order: (order[i], 0, 0))
                for piece in pieces
            ],
            out_specs=[spec(width), spec(rows)],
        ),
        out_shape=[
            jax.ShapeDtypeStruct((count, rows, width), jnp.bfloat16),
            jax.ShapeDtypeStruct((count, rows, rows), jnp.bfloat16),
        ],
        compiler_params=pltpu.CompilerParams(vmem_limit_bytes=VMEM_LIMIT),
        cost_estimate=pl.CostEstimate(
            flops=2 * count * rows * rows * width,
            bytes_accessed=2 * count * rows * (2 * width + rows),
            transcendentals=0,
        ),
    )(order, *pieces)


def mixers(grams_now):
    return [
        quintic_second * gram + quintic_third * dot(half(gram), half(gram)) for gram in grams_now
    ]


def next_grams(grams_now, mixes):
    lefts = [
        quintic_first * gram + dot(half(mix), half(gram)) for gram, mix in zip(grams_now, mixes)
    ]
    return [quintic_first * left + dot(half(left), half(mix)) for left, mix in zip(lefts, mixes)]


def chain_kernel(parts, *refs):
    gram_refs = refs[:parts]
    chain_ref, squares_ref = refs[parts:]
    count, rows, _ = chain_ref.shape
    on_diagonal = lax.broadcasted_iota(jnp.int32, (rows, rows), 0) == lax.broadcasted_iota(
        jnp.int32, (rows, rows), 1
    )
    grams_now = []
    inverses = []
    for index in range(count):
        gram = gram_refs[0][index].astype(jnp.float32)
        for ref in gram_refs[1:]:
            gram = gram + ref[index].astype(jnp.float32)
        diagonal = jnp.where(on_diagonal, gram, 0.0)
        squares = jnp.sum(jnp.sum(diagonal, axis=0, keepdims=True), axis=1, keepdims=True)
        squares_ref[index] = jnp.broadcast_to(squares, squares_ref.shape[1:])
        inverse = 1.0 / (jnp.sqrt(squares) + epsilon)
        grams_now.append(gram * inverse * inverse)
        inverses.append(inverse)
    first = mixers(grams_now)
    grams_now = next_grams(grams_now, first)
    second = mixers(grams_now)
    grams_now = next_grams(grams_now, second)
    third = mixers(grams_now)
    pairs = [
        quintic_first * (m0 + m1) + dot(half(m1), half(m0)) for m0, m1 in zip(first, second)
    ]
    cubed = jnp.where(on_diagonal, quintic_first**3, 0.0)
    for index, (pair, m2) in enumerate(zip(pairs, third)):
        whole = quintic_first * pair + quintic_first**2 * m2 + dot(half(m2), half(pair))
        chain_ref[index] = half((cubed + whole) * (factor * inverses[index]))


def chains(gram_parts):
    count, rows, _ = gram_parts[0].shape
    step = 3 if count % 3 == 0 else 1
    parts = len(gram_parts)
    spec = pl.BlockSpec((step, rows, rows), lambda i: (i, 0, 0))
    return pl.pallas_call(
        functools.partial(chain_kernel, parts),
        grid=(count // step,),
        in_specs=[spec] * parts,
        out_specs=[spec, pl.BlockSpec((step, 8, 128), lambda i: (i, 0, 0))],
        out_shape=[
            jax.ShapeDtypeStruct((count, rows, rows), jnp.bfloat16),
            jax.ShapeDtypeStruct((count, 8, 128), jnp.float32),
        ],
        compiler_params=pltpu.CompilerParams(vmem_limit_bytes=VMEM_LIMIT),
        cost_estimate=pl.CostEstimate(
            flops=18 * count * rows * rows * rows,
            bytes_accessed=2 * count * rows * rows * (parts + 1),
            transcendentals=0,
        ),
    )(*gram_parts)


def apply_kernel(sets, first_count, masters, spans_ref, slots_ref, order_ref, *refs):
    set_refs = [refs[3 * at : 3 * at + 3] for at in range(sets)]
    master_refs = refs[3 * sets : -6]
    rows_ref, weights_ref, new_rows_ref, owned_ref, rms_ref, scaled_ref = refs[-6:]
    blocks = spans_ref.shape[0]
    height = scaled_ref.shape[0] // blocks
    at = pl.program_id(0)
    matrix = order_ref[at]
    slot = slots_ref[matrix]

    @pl.when(at == 0)
    def _():
        owned_ref[...] = jnp.zeros_like(owned_ref)
        rms_ref[...] = jnp.zeros_like(rms_ref)

    def target(block_at):
        return pl.ds(block_at * height, height)

    def span(block_at):
        return pl.ds(pl.multiple_of(spans_ref[block_at] * height, height), height)

    lane = lax.broadcasted_iota(jnp.int32, rms_ref.shape, 1)

    def make(chain_ref, squares_ref, update_ref):
        rms = jnp.sqrt(squares_ref[0, :1, :1] / float(KV * D))
        rms_ref[...] = jnp.where(lane == slot, rms, rms_ref[...])
        scaled_ref[...] = half(dot(chain_ref[0], update_ref[0]))

    for index, chosen in enumerate(set_refs):
        pl.when((at >= first_count) == (index == 1))(functools.partial(make, *chosen))

    decayed = rows_ref[0] * (1.0 - learn_rate * weight_decay)
    new_rows_ref[0] = decayed - learn_rate * scaled_ref[:height].astype(jnp.float32)
    def write(master_ref, wheres):
        for block_at, where in enumerate(wheres):
            decayed = master_ref[where, 0].astype(jnp.float32) * (1.0 - learn_rate * weight_decay)
            weights_ref[0, target(block_at)] = half(
                decayed - learn_rate * scaled_ref[span(block_at)].astype(jnp.float32)
            )

    for (start, stop, wheres), master_ref in zip(masters, master_refs):
        here = (matrix >= start) & (matrix < stop)
        pl.when(here)(functools.partial(write, master_ref, wheres))

    @pl.when(slot >= 0)
    def _():
        for block_at in range(blocks):
            owned_ref[jnp.maximum(slot, 0), target(block_at)] = scaled_ref[span(block_at)]


def applied(spans, slots, order, sets, master_pieces, masters, master):
    _, rows, width = sets[0][2].shape
    count, row_count, _ = master.shape
    first_count = sets[0][0].shape[0]

    def by_matrix(height, minor):
        def index(i, spans, slots, order):
            return (order[i], 0, 0)

        return pl.BlockSpec((1, height, minor), index)

    def by_piece(piece, start, stop):
        def index(i, spans, slots, order):
            return (0, jnp.clip(order[i] - start, 0, stop - start - 1), 0, 0)

        return pl.BlockSpec((piece.shape[0], 1, *piece.shape[2:]), index)

    def by_step(array, start):
        last = array.shape[0] - 1

        def index(i, *_):
            return (jnp.clip(i - start, 0, last), 0, 0)

        return pl.BlockSpec((1, *array.shape[1:]), index)

    owned = (MOST, rows, width)
    return pl.pallas_call(
        functools.partial(apply_kernel, len(sets), first_count, masters),
        grid_spec=pltpu.PrefetchScalarGridSpec(
            num_scalar_prefetch=3,
            grid=(count,),
            in_specs=[
                by_step(array, at * first_count) for at, arrays in enumerate(sets) for array in arrays
            ]
            + [by_piece(piece, *bounds[:2]) for piece, bounds in zip(master_pieces, masters)]
            + [by_matrix(row_count, width)],
            out_specs=[
                by_matrix(rows, width),
                by_matrix(row_count, width),
                pl.BlockSpec(owned, lambda i, *_: (0, 0, 0)),
                pl.BlockSpec((1, MOST), lambda i, *_: (0, 0)),
            ],
            scratch_shapes=[pltpu.VMEM((rows, width), jnp.bfloat16)],
        ),
        out_shape=[
            jax.ShapeDtypeStruct((count, rows, width), jnp.bfloat16),
            jax.ShapeDtypeStruct(master.shape, jnp.float32),
            jax.ShapeDtypeStruct(owned, jnp.bfloat16),
            jax.ShapeDtypeStruct((1, MOST), jnp.float32),
        ],
        compiler_params=pltpu.CompilerParams(vmem_limit_bytes=VMEM_LIMIT),
        cost_estimate=pl.CostEstimate(
            flops=2 * count * rows * rows * width,
            bytes_accessed=2 * count * rows * (4 * width + rows),
            transcendentals=0,
        ),
    )(
        spans,
        slots,
        order,
        *[array for arrays in sets for array in arrays],
        *master_pieces,
        master,
    )


class Grid:
    def __init__(self, count):
        self.count = count
        self.me = lax.axis_index("dp")
        self.x_pairs = [(d, d ^ 1) for d in range(count)]
        self.y_pairs = [(d, d ^ 2) for d in range(count)]

    def over_x(self, value):
        return lax.ppermute(value, "dp", self.x_pairs)

    def over_y(self, value):
        return lax.ppermute(value, "dp", self.y_pairs)

    def over_z(self, value, shift):
        pairs = [(d, (d // 4 + shift) % LINE * 4 + d % 4) for d in range(self.count)]
        return lax.ppermute(value, "dp", pairs)


def place(me, dx, dy, dz):
    z = ((me >> 2) + dz) & (LINE - 1)
    return z * 4 + ((me & 3) ^ (2 * dy + dx))


def after(value, *others):
    return lax.optimization_barrier((value, *others))[0]


def added(*values):
    return sum(value.astype(jnp.float32) for value in values)


class MasterGather:
    def __init__(self, grid, master):
        self.grid = grid
        self.lines = [[z * 4 + corner for z in range(LINE)] for corner in range(4)]
        self.planes = [[z * 4 + corner for corner in range(4)] for z in range(LINE)]
        matrices, *shape = master.shape
        self.split = matrices // 2
        self.shape = [4 * LINE, -1, *shape]
        self.own = half(master)
        self.low = self.gather(self.own[: self.split], self.planes)
        self.high = self.gather(self.own[self.split :], self.lines)
        self.matrices = matrices

    def gather(self, value, groups):
        return lax.all_gather(value, "dp", axis_index_groups=groups)

    def over_planes(self, *ties):
        self.high = self.gather(after(self.high, *ties), self.planes).reshape(self.shape)

    def along_lines(self, *ties):
        self.low = self.gather(after(self.low, *ties), self.lines).reshape(self.shape)

    def masters(self):
        by_line = [z * 4 + corner for z in range(LINE) for corner in range(4)]
        by_plane = [corner * LINE + z for z in range(LINE) for corner in range(4)]
        return [(0, self.split, by_line), (self.split, self.matrices, by_plane)]

    def spans(self):
        corner_mine, z_mine = self.grid.me & 3, self.grid.me >> 2
        spans = []
        for z in range(LINE):
            for corner in range(4):
                apart = corner ^ corner_mine
                dx, dy = apart & 1, apart >> 1
                spans.append((dx * 2 + dy) * 4 + ((z - z_mine) & (LINE - 1)))
        return jnp.stack(spans).astype(jnp.int32)


def reduce_scatter(grid, terms, row_count, master_gather):
    def term(me, dx, dy, dz):
        start = place(me, dx, dy, dz) * row_count
        return lax.dynamic_slice_in_dim(terms, start, row_count, axis=1)

    me = grid.me
    raw_far1, raw_far2 = term(me, 1, 1, 1), term(me, 1, 1, 2)
    me = after(grid.me, raw_far1, raw_far2, master_gather.own)
    raw_x1, raw_far3, raw_y2 = term(me, 1, 0, 1), term(me, 1, 1, 3), term(me, 0, 1, 2)
    raw_y3, raw_far0, raw_x0 = term(me, 0, 1, 3), term(me, 1, 1, 0), term(me, 1, 0, 0)
    far1 = grid.over_x(raw_far1)
    far2 = grid.over_y(raw_far2)
    along_x1 = grid.over_x(raw_x1)
    far3 = grid.over_y(raw_far3)
    along_y2 = grid.over_y(raw_y2)

    me = after(grid.me, far1, far2, raw_y3)
    sent_x2 = half(added(term(me, 1, 0, 2), far2))
    sent_y1 = half(added(term(me, 0, 1, 1), far1))
    along_x2 = grid.over_x(sent_x2)
    along_y1 = grid.over_y(sent_y1)

    me = after(grid.me, far3, along_x1, sent_x2, sent_y1)
    sent_x3 = half(added(term(me, 1, 0, 3), far3))
    along_x3 = grid.over_x(sent_x3)
    along_y3 = grid.over_y(after(raw_y3, far3, along_x1))

    me = after(grid.me, along_y2, along_x2, sent_x3)
    near2 = half(added(term(me, 0, 0, 2), along_x2, along_y2))
    line2 = grid.over_z(near2, 2)
    far0 = grid.over_x(after(raw_far0, along_x2))

    me = after(grid.me, along_x1, along_y1, along_x3, near2)
    near1 = half(added(term(me, 0, 0, 1), along_x1, along_y1))
    line1 = grid.over_z(near1, 1)
    along_x0 = grid.over_x(after(raw_x0, along_x3))

    me = after(grid.me, along_x3, along_y3, far0, near1, master_gather.low, master_gather.high)
    near3 = half(added(term(me, 0, 0, 3), along_x3, along_y3))
    sent_y0 = half(added(term(me, 0, 1, 0), far0))
    line3 = grid.over_z(near3, 3)
    master_gather.over_planes(near3, sent_y0)
    along_y0 = grid.over_y(sent_y0)
    me = after(grid.me, near3, sent_y0, line2)
    return added(term(me, 0, 0, 0), along_x0, along_y0, line1, line2, line3)


def all_gather(grid, own, *ties):
    x0, y0 = grid.over_x(own), grid.over_y(own)
    z1, z3 = grid.over_z(own, LINE - 1), grid.over_z(own, 1)
    far0 = grid.over_x(y0)
    x1, y1 = grid.over_x(z1), grid.over_y(z1)
    x3, y3 = grid.over_x(z3), grid.over_y(z3)
    z2 = grid.over_z(after(own, z1, z3, *ties), 2)
    far3 = grid.over_y(x3)
    x2, y2 = grid.over_x(z2), grid.over_y(z2)
    far1 = grid.over_x(y1)
    far2 = grid.over_y(x2)
    return [own, z1, z2, z3, y0, y1, y2, y3, x0, x1, x2, x3, far0, far1, far2, far3]


def updated(summed, momentum):
    new_momentum = momentum_decay * momentum + summed
    return new_momentum, half(summed + momentum_decay * new_momentum)


def per_device(gradients, momentum, master, owners):
    me = lax.axis_index("dp")
    dp_count = lax.axis_size("dp")
    matrices, row_count, width = momentum.shape
    terms = gradients[0]
    held = owners == me
    index = jnp.arange(matrices)
    rank = jnp.sum(held[None, :] & (index[None, :] < index[:, None]), axis=1)
    slots = jnp.where(held, rank, -1).astype(jnp.int32)

    in_pieces = dp_count == 4 * LINE and row_count % 32 == 0
    if in_pieces:
        grid = Grid(dp_count)
        rows = master
        master_gather = MasterGather(grid, master)
        spans = master_gather.spans()
        summed = reduce_scatter(grid, terms, row_count, master_gather)
        new_momentum, own = updated(summed, momentum)
        pieces = all_gather(grid, own, master_gather.high)
        master_gather.along_lines(*pieces[1:4])
        master_pieces, masters = [master_gather.low, master_gather.high], master_gather.masters()
    else:
        spans = jnp.zeros((1,), jnp.int32)
        rows = jnp.zeros((matrices, terms.shape[1], width), jnp.float32)
        rows = lax.dynamic_update_slice_in_dim(rows, master, me * row_count, axis=1)
        summed = lax.psum_scatter(terms, "dp", scatter_dimension=1, tiled=True)
        new_momentum, own = updated(summed.astype(jnp.float32), momentum)
        master_pieces = [lax.all_gather(half(master), "dp", axis=1, tiled=True)[None]]
        masters = [(0, matrices, [0])]
        pieces = [lax.all_gather(own, "dp", axis=1, tiled=True)]

    order = jnp.arange(matrices, dtype=jnp.int32)
    if lax.axis_size("col") == 2 and matrices % 2 == 0:
        size = matrices // 2
        order = (order + lax.axis_index("col") * size) % matrices
        mine, theirs = order[:size], order[size:]
        their_update, their_gram = grams(pieces, theirs)
        swap = [(0, 1), (1, 0)]
        other_part = lax.ppermute(their_gram, "col", swap)
        my_update, my_gram = grams(pieces, mine)
        chain, squares = chains([my_gram, other_part])
        other = [lax.ppermute(chain, "col", swap), lax.ppermute(squares, "col", swap)]
        sets = [[chain, squares, my_update], [*other, their_update]]
    else:
        update, gram = grams(pieces, order)
        sets = [[*chains([lax.psum(gram, "col")]), update]]
    new_weights, new_master, owned_updates, rms = applied(
        spans, slots, order, sets, master_pieces, masters, rows
    )
    if not in_pieces:
        new_master = lax.dynamic_slice_in_dim(new_master, me * row_count, row_count, axis=1)
    return (new_weights, new_master, new_momentum, owned_updates[None], rms)


def solution(mesh):
    return jax.shard_map(
        per_device,
        mesh=mesh,
        in_specs=(P("dp", None, None, "col"), P(None, "dp", "col"), P(None, "dp", "col"), P()),
        out_specs=(
            P(None, None, "col"),
            P(None, "dp", "col"),
            P(None, "dp", "col"),
            P("dp", None, None, "col"),
            P("dp", None),
        ),
        check_vma=False,
    )
```

```python
import functools
import math

import jax
import jax.numpy as jnp
from jax import lax
from jax.experimental import pallas as pl
from jax.experimental.pallas import tpu as pltpu
from jax.sharding import PartitionSpec as P

KV = 512
D = 2048
MOST = 2

quintic_first = 3.4445
quintic_second = -4.775
quintic_third = 2.0315
momentum_decay = 0.95
learn_rate = 0.3
weight_decay = 0.1
epsilon = 1e-07
factor = 0.2 * math.sqrt(max(KV, D))

VMEM_LIMIT = 56 * 1024 * 1024
LINE = 4


def dot(left, right):
    return jnp.dot(left, right, preferred_element_type=jnp.float32)


def half(value):
    return value.astype(jnp.bfloat16)


def gram_kernel(order_ref, *refs):
    piece_refs, (update_ref, gram_ref) = refs[:-2], refs[-2:]
    start = 0
    for ref in piece_refs:
        rows = ref.shape[1]
        update_ref[0, start : start + rows] = ref[0]
        start += rows
    block = update_ref[0]
    gram = lax.dot_general(
        block, block, (((1,), (1,)), ((), ())), preferred_element_type=jnp.float32
    )
    gram_ref[0] = half(gram)


def grams(pieces, order):
    width = pieces[0].shape[2]
    count = order.shape[0]
    rows = sum(piece.shape[1] for piece in pieces)

    def spec(minor):
        return pl.BlockSpec((1, rows, minor), lambda i, order: (i, 0, 0))

    return pl.pallas_call(
        gram_kernel,
        grid_spec=pltpu.PrefetchScalarGridSpec(
            num_scalar_prefetch=1,
            grid=(count,),
            in_specs=[
                pl.BlockSpec((1, *piece.shape[1:]), lambda i, order: (order[i], 0, 0))
                for piece in pieces
            ],
            out_specs=[spec(width), spec(rows)],
        ),
        out_shape=[
            jax.ShapeDtypeStruct((count, rows, width), jnp.bfloat16),
            jax.ShapeDtypeStruct((count, rows, rows), jnp.bfloat16),
        ],
        compiler_params=pltpu.CompilerParams(vmem_limit_bytes=VMEM_LIMIT),
        cost_estimate=pl.CostEstimate(
            flops=2 * count * rows * rows * width,
            bytes_accessed=2 * count * rows * (2 * width + rows),
            transcendentals=0,
        ),
    )(order, *pieces)


def mixers(grams_now):
    return [
        quintic_second * gram + quintic_third * dot(half(gram), half(gram)) for gram in grams_now
    ]


def next_grams(grams_now, mixes):
    lefts = [
        quintic_first * gram + dot(half(mix), half(gram)) for gram, mix in zip(grams_now, mixes)
    ]
    return [quintic_first * left + dot(half(left), half(mix)) for left, mix in zip(lefts, mixes)]


def chain_kernel(parts, *refs):
    gram_refs = refs[:parts]
    chain_ref, squares_ref = refs[parts:]
    count, rows, _ = chain_ref.shape
    on_diagonal = lax.broadcasted_iota(jnp.int32, (rows, rows), 0) == lax.broadcasted_iota(
        jnp.int32, (rows, rows), 1
    )
    grams_now = []
    inverses = []
    for index in range(count):
        gram = gram_refs[0][index].astype(jnp.float32)
        for ref in gram_refs[1:]:
            gram = gram + ref[index].astype(jnp.float32)
        diagonal = jnp.where(on_diagonal, gram, 0.0)
        squares = jnp.sum(jnp.sum(diagonal, axis=0, keepdims=True), axis=1, keepdims=True)
        squares_ref[index] = jnp.broadcast_to(squares, squares_ref.shape[1:])
        inverse = 1.0 / (jnp.sqrt(squares) + epsilon)
        grams_now.append(gram * inverse * inverse)
        inverses.append(inverse)
    first = mixers(grams_now)
    grams_now = next_grams(grams_now, first)
    second = mixers(grams_now)
    grams_now = next_grams(grams_now, second)
    third = mixers(grams_now)
    pairs = [
        quintic_first * (m0 + m1) + dot(half(m1), half(m0)) for m0, m1 in zip(first, second)
    ]
    cubed = jnp.where(on_diagonal, quintic_first**3, 0.0)
    for index, (pair, m2) in enumerate(zip(pairs, third)):
        whole = quintic_first * pair + quintic_first**2 * m2 + dot(half(m2), half(pair))
        chain_ref[index] = half((cubed + whole) * (factor * inverses[index]))


def chains(gram_parts):
    count, rows, _ = gram_parts[0].shape
    step = 3 if count % 3 == 0 else 1
    parts = len(gram_parts)
    spec = pl.BlockSpec((step, rows, rows), lambda i: (i, 0, 0))
    return pl.pallas_call(
        functools.partial(chain_kernel, parts),
        grid=(count // step,),
        in_specs=[spec] * parts,
        out_specs=[spec, pl.BlockSpec((step, 8, 128), lambda i: (i, 0, 0))],
        out_shape=[
            jax.ShapeDtypeStruct((count, rows, rows), jnp.bfloat16),
            jax.ShapeDtypeStruct((count, 8, 128), jnp.float32),
        ],
        compiler_params=pltpu.CompilerParams(vmem_limit_bytes=VMEM_LIMIT),
        cost_estimate=pl.CostEstimate(
            flops=18 * count * rows * rows * rows,
            bytes_accessed=2 * count * rows * rows * (parts + 1),
            transcendentals=0,
        ),
    )(*gram_parts)


def apply_kernel(sets, first_count, masters, places_ref, spans_ref, slots_ref, order_ref, *refs):
    set_refs = [refs[3 * at : 3 * at + 3] for at in range(sets)]
    master_refs = refs[3 * sets : -6]
    rows_ref, weights_ref, new_rows_ref, owned_ref, rms_ref, scaled_ref = refs[-6:]
    blocks = spans_ref.shape[0]
    height = scaled_ref.shape[0] // blocks
    at = pl.program_id(0)
    matrix = order_ref[at]
    slot = slots_ref[matrix]

    @pl.when(at == 0)
    def _():
        owned_ref[...] = jnp.zeros_like(owned_ref)
        rms_ref[...] = jnp.zeros_like(rms_ref)

    def target(block_at):
        return pl.ds(pl.multiple_of(places_ref[block_at] * height, height), height)

    def span(block_at):
        return pl.ds(pl.multiple_of(spans_ref[block_at] * height, height), height)

    lane = lax.broadcasted_iota(jnp.int32, rms_ref.shape, 1)

    def make(chain_ref, squares_ref, update_ref):
        rms = jnp.sqrt(squares_ref[0, :1, :1] / float(KV * D))
        rms_ref[...] = jnp.where(lane == slot, rms, rms_ref[...])
        scaled_ref[...] = half(dot(chain_ref[0], update_ref[0]))

    for index, chosen in enumerate(set_refs):
        pl.when((at >= first_count) == (index == 1))(functools.partial(make, *chosen))

    decayed = rows_ref[0] * (1.0 - learn_rate * weight_decay)
    new_rows_ref[0] = decayed - learn_rate * scaled_ref[:height].astype(jnp.float32)
    def write(lies):
        for block_at, (piece, where) in enumerate(lies):
            decayed = master_refs[piece][where, 0].astype(jnp.float32) * (
                1.0 - learn_rate * weight_decay
            )
            weights_ref[0, target(block_at)] = half(
                decayed - learn_rate * scaled_ref[span(block_at)].astype(jnp.float32)
            )

    for start, stop, lies in masters:
        pl.when((matrix >= start) & (matrix < stop))(functools.partial(write, lies))

    @pl.when(slot >= 0)
    def _():
        for block_at in range(blocks):
            owned_ref[jnp.maximum(slot, 0), target(block_at)] = scaled_ref[span(block_at)]


def applied(places, spans, slots, order, sets, master_pieces, masters, master):
    _, rows, width = sets[0][2].shape
    count, row_count, _ = master.shape
    first_count = sets[0][0].shape[0]

    def by_matrix(height, minor):
        def index(i, places, spans, slots, order):
            return (order[i], 0, 0)

        return pl.BlockSpec((1, height, minor), index)

    def by_piece(piece, start, depth):
        def index(i, places, spans, slots, order):
            return (0, jnp.clip(order[i] - start, 0, piece.shape[1] - 1), 0, 0)

        return pl.BlockSpec((depth, 1, *piece.shape[2:]), index)

    def by_step(array, start):
        last = array.shape[0] - 1

        def index(i, *_):
            return (jnp.clip(i - start, 0, last), 0, 0)

        return pl.BlockSpec((1, *array.shape[1:]), index)

    owned = (MOST, rows, width)
    return pl.pallas_call(
        functools.partial(apply_kernel, len(sets), first_count, masters),
        grid_spec=pltpu.PrefetchScalarGridSpec(
            num_scalar_prefetch=4,
            grid=(count,),
            in_specs=[
                by_step(array, at * first_count) for at, arrays in enumerate(sets) for array in arrays
            ]
            + [by_piece(*piece) for piece in master_pieces]
            + [by_matrix(row_count, width)],
            out_specs=[
                by_matrix(rows, width),
                by_matrix(row_count, width),
                pl.BlockSpec(owned, lambda i, *_: (0, 0, 0)),
                pl.BlockSpec((1, MOST), lambda i, *_: (0, 0)),
            ],
            scratch_shapes=[pltpu.VMEM((rows, width), jnp.bfloat16)],
        ),
        out_shape=[
            jax.ShapeDtypeStruct((count, rows, width), jnp.bfloat16),
            jax.ShapeDtypeStruct(master.shape, jnp.float32),
            jax.ShapeDtypeStruct(owned, jnp.bfloat16),
            jax.ShapeDtypeStruct((1, MOST), jnp.float32),
        ],
        compiler_params=pltpu.CompilerParams(vmem_limit_bytes=VMEM_LIMIT),
        cost_estimate=pl.CostEstimate(
            flops=2 * count * rows * rows * width,
            bytes_accessed=2 * count * rows * (4 * width + rows),
            transcendentals=0,
        ),
    )(
        places,
        spans,
        slots,
        order,
        *[array for arrays in sets for array in arrays],
        *[piece[0] for piece in master_pieces],
        master,
    )


class Grid:
    def __init__(self, count):
        self.count = count
        self.me = lax.axis_index("dp")
        self.x_pairs = [(d, d ^ 1) for d in range(count)]
        self.y_pairs = [(d, d ^ 2) for d in range(count)]

    def over_x(self, value):
        return lax.ppermute(value, "dp", self.x_pairs)

    def over_y(self, value):
        return lax.ppermute(value, "dp", self.y_pairs)

    def over_z(self, value, shift):
        pairs = [(d, (d // 4 + shift) % LINE * 4 + d % 4) for d in range(self.count)]
        return lax.ppermute(value, "dp", pairs)


def place(me, dx, dy, dz):
    z = ((me >> 2) + dz) & (LINE - 1)
    return z * 4 + ((me & 3) ^ (2 * dy + dx))


def after(value, *others):
    return lax.optimization_barrier((value, *others))[0]


def added(*values):
    return sum(value.astype(jnp.float32) for value in values)


class MasterGather:
    def __init__(self, grid, master):
        self.grid = grid
        self.lines = [[z * 4 + corner for z in range(LINE)] for corner in range(4)]
        self.split = master.shape[0] // 2
        self.own = half(master)
        self.line = lax.all_gather(self.own, "dp", axis_index_groups=self.lines)

    def near(self, *ties):
        line = after(self.line, *ties)
        self.high = line[:, self.split :]
        sent = jnp.concatenate([self.high, self.own[None, : self.split]])
        self.near_x = self.grid.over_x(sent)
        self.near_y = self.grid.over_y(sent)

    def low_plane(self):
        low_x, low_y = self.near_x[LINE], self.near_y[LINE]
        self.plane = jnp.stack([self.own[: self.split], low_y, low_x, self.grid.over_x(low_y)])

    def low_lines(self, *ties):
        low = lax.all_gather(after(self.plane, *ties), "dp", axis_index_groups=self.lines)
        self.low = low.reshape(4 * LINE, *low.shape[2:])

    def high_corners(self, *ties):
        near_y = after(self.near_y, *ties)
        near_x = after(self.near_x, *ties)
        self.far_x = self.grid.over_x(near_y[: LINE // 2])
        self.far_y = self.grid.over_y(near_x[LINE // 2 : LINE])

    def pieces(self):
        high = [self.high, self.near_y, self.near_x, self.far_x, self.far_y]
        depths = [LINE, LINE, LINE, LINE // 2, LINE // 2]
        return [(self.low, 0, 4 * LINE)] + [
            (piece, self.split, depth) for piece, depth in zip(high, depths)
        ]

    def masters(self, matrices):
        low = [(0, z * 4 + at) for at in range(4) for z in range(LINE)]
        high = [(piece, z) for piece in (1, 2, 3) for z in range(LINE)]
        high += [(4 + z // 2, z % 2) for z in range(LINE)]
        return [(0, self.split, low), (self.split, matrices, high)]

    def places(self):
        corner, z_mine = self.grid.me & 3, self.grid.me >> 2
        places = [
            z * 4 + (corner ^ (2 * dy + dx)) for dx in range(2) for dy in range(2) for z in range(LINE)
        ]
        spans = [at * 4 + ((z - z_mine) & (LINE - 1)) for at in range(4) for z in range(LINE)]
        return jnp.stack(places).astype(jnp.int32), jnp.stack(spans).astype(jnp.int32)


def reduce_scatter(grid, terms, row_count, master_gather):
    def term(me, dx, dy, dz):
        start = place(me, dx, dy, dz) * row_count
        return lax.dynamic_slice_in_dim(terms, start, row_count, axis=1)

    me = grid.me
    raw_far1, raw_far2 = term(me, 1, 1, 1), term(me, 1, 1, 2)
    me = after(grid.me, raw_far1, raw_far2, master_gather.own)
    raw_x1, raw_far3, raw_y2 = term(me, 1, 0, 1), term(me, 1, 1, 3), term(me, 0, 1, 2)
    raw_y3, raw_far0, raw_x0 = term(me, 0, 1, 3), term(me, 1, 1, 0), term(me, 1, 0, 0)
    far1 = grid.over_x(raw_far1)
    far2 = grid.over_y(raw_far2)
    along_x1 = grid.over_x(raw_x1)
    far3 = grid.over_y(raw_far3)
    along_y2 = grid.over_y(raw_y2)

    me = after(grid.me, far1, far2, raw_y3)
    sent_x2 = half(added(term(me, 1, 0, 2), far2))
    sent_y1 = half(added(term(me, 0, 1, 1), far1))
    along_x2 = grid.over_x(sent_x2)
    along_y1 = grid.over_y(sent_y1)

    me = after(grid.me, far3, along_x1, sent_x2, sent_y1)
    sent_x3 = half(added(term(me, 1, 0, 3), far3))
    along_x3 = grid.over_x(sent_x3)
    along_y3 = grid.over_y(after(raw_y3, far3, along_x1))

    me = after(grid.me, along_y2, along_x2, sent_x3)
    near2 = half(added(term(me, 0, 0, 2), along_x2, along_y2))
    line2 = grid.over_z(near2, 2)
    far0 = grid.over_x(after(raw_far0, along_x2))

    me = after(grid.me, along_x1, along_y1, along_x3, near2)
    near1 = half(added(term(me, 0, 0, 1), along_x1, along_y1))
    line1 = grid.over_z(near1, 1)
    along_x0 = grid.over_x(after(raw_x0, along_x3))

    me = after(grid.me, along_x3, along_y3, far0, near1)
    near3 = half(added(term(me, 0, 0, 3), along_x3, along_y3))
    sent_y0 = half(added(term(me, 0, 1, 0), far0))
    line3 = grid.over_z(near3, 3)
    master_gather.near(near3, sent_y0)
    along_y0 = grid.over_y(sent_y0)
    me = after(grid.me, near3, sent_y0, line2)
    return added(term(me, 0, 0, 0), along_x0, along_y0, line1, line2, line3)


def all_gather(grid, own, before_z2, before_x2):
    x0, y0 = grid.over_x(own), grid.over_y(own)
    z1, z3 = grid.over_z(own, LINE - 1), grid.over_z(own, 1)
    far0 = grid.over_x(y0)
    x1, y1 = grid.over_x(z1), grid.over_y(z1)
    x3, y3 = grid.over_x(z3), grid.over_y(z3)
    z2 = grid.over_z(after(own, z1, z3, *before_z2), 2)
    far3 = grid.over_y(x3)
    sent = after(z2, before_x2)
    x2, y2 = grid.over_x(sent), grid.over_y(sent)
    far1 = grid.over_x(y1)
    far2 = grid.over_y(x2)
    return [own, z1, z2, z3, y0, y1, y2, y3, x0, x1, x2, x3, far0, far1, far2, far3]


def updated(summed, momentum):
    new_momentum = momentum_decay * momentum + summed
    return new_momentum, half(summed + momentum_decay * new_momentum)


def per_device(gradients, momentum, master, owners):
    me = lax.axis_index("dp")
    dp_count = lax.axis_size("dp")
    matrices, row_count, width = momentum.shape
    terms = gradients[0]
    held = owners == me
    index = jnp.arange(matrices)
    rank = jnp.sum(held[None, :] & (index[None, :] < index[:, None]), axis=1)
    slots = jnp.where(held, rank, -1).astype(jnp.int32)

    in_pieces = dp_count == 4 * LINE and row_count % 32 == 0
    if in_pieces:
        grid = Grid(dp_count)
        rows = master
        master_gather = MasterGather(grid, master)
        places, spans = master_gather.places()
        summed = reduce_scatter(grid, terms, row_count, master_gather)
        new_momentum, own = updated(summed, momentum)
        master_gather.low_plane()
        pieces = all_gather(
            grid, own, (master_gather.near_x, master_gather.near_y), master_gather.plane
        )
        master_gather.low_lines(*pieces[1:4])
        master_gather.high_corners(*pieces[1:])
        master_pieces, masters = master_gather.pieces(), master_gather.masters(matrices)
    else:
        places = spans = jnp.zeros((1,), jnp.int32)
        rows = jnp.zeros((matrices, terms.shape[1], width), jnp.float32)
        rows = lax.dynamic_update_slice_in_dim(rows, master, me * row_count, axis=1)
        summed = lax.psum_scatter(terms, "dp", scatter_dimension=1, tiled=True)
        new_momentum, own = updated(summed.astype(jnp.float32), momentum)
        master_pieces = [(lax.all_gather(half(master), "dp", axis=1, tiled=True)[None], 0, 1)]
        masters = [(0, matrices, [(0, 0)])]
        pieces = [lax.all_gather(own, "dp", axis=1, tiled=True)]

    order = jnp.arange(matrices, dtype=jnp.int32)
    if lax.axis_size("col") == 2 and matrices % 2 == 0:
        size = matrices // 2
        order = (order + lax.axis_index("col") * size) % matrices
        mine, theirs = order[:size], order[size:]
        their_update, their_gram = grams(pieces, theirs)
        swap = [(0, 1), (1, 0)]
        other_part = lax.ppermute(their_gram, "col", swap)
        my_update, my_gram = grams(pieces, mine)
        chain, squares = chains([my_gram, other_part])
        sent = chain
        if in_pieces:
            sent = after(chain, master_gather.far_x, master_gather.far_y)
        other = [lax.ppermute(sent, "col", swap), lax.ppermute(squares, "col", swap)]
        sets = [[chain, squares, my_update], [*other, their_update]]
    else:
        update, gram = grams(pieces, order)
        sets = [[*chains([lax.psum(gram, "col")]), update]]
    new_weights, new_master, owned_updates, rms = applied(
        places, spans, slots, order, sets, master_pieces, masters, rows
    )
    if not in_pieces:
        new_master = lax.dynamic_slice_in_dim(new_master, me * row_count, row_count, axis=1)
    return (new_weights, new_master, new_momentum, owned_updates[None], rms)


def solution(mesh):
    return jax.shard_map(
        per_device,
        mesh=mesh,
        in_specs=(P("dp", None, None, "col"), P(None, "dp", "col"), P(None, "dp", "col"), P()),
        out_specs=(
            P(None, None, "col"),
            P(None, "dp", "col"),
            P(None, "dp", "col"),
            P("dp", None, None, "col"),
            P("dp", None),
        ),
        check_vma=False,
    )
```

```python
import functools
import math

import jax
import jax.numpy as jnp
from jax import lax
from jax.experimental import pallas as pl
from jax.experimental.pallas import tpu as pltpu
from jax.sharding import PartitionSpec as P

KV = 512
D = 2048
MOST = 2

quintic_first = 3.4445
quintic_second = -4.775
quintic_third = 2.0315
momentum_decay = 0.95
learn_rate = 0.3
weight_decay = 0.1
epsilon = 1e-07
factor = 0.2 * math.sqrt(max(KV, D))

VMEM_LIMIT = 56 * 1024 * 1024
LINE = 4


def dot(left, right):
    return jnp.dot(left, right, preferred_element_type=jnp.float32)


def half(value):
    return value.astype(jnp.bfloat16)


def gram_kernel(order_ref, *refs):
    piece_refs, (update_ref, gram_ref) = refs[:-2], refs[-2:]
    start = 0
    for ref in piece_refs:
        rows = ref.shape[1]
        update_ref[0, start : start + rows] = ref[0]
        start += rows
    block = update_ref[0]
    gram = lax.dot_general(
        block, block, (((1,), (1,)), ((), ())), preferred_element_type=jnp.float32
    )
    gram_ref[0] = half(gram)


def grams(pieces, order):
    width = pieces[0].shape[2]
    count = order.shape[0]
    rows = sum(piece.shape[1] for piece in pieces)

    def spec(minor):
        return pl.BlockSpec((1, rows, minor), lambda i, order: (i, 0, 0))

    return pl.pallas_call(
        gram_kernel,
        grid_spec=pltpu.PrefetchScalarGridSpec(
            num_scalar_prefetch=1,
            grid=(count,),
            in_specs=[
                pl.BlockSpec((1, *piece.shape[1:]), lambda i, order: (order[i], 0, 0))
                for piece in pieces
            ],
            out_specs=[spec(width), spec(rows)],
        ),
        out_shape=[
            jax.ShapeDtypeStruct((count, rows, width), jnp.bfloat16),
            jax.ShapeDtypeStruct((count, rows, rows), jnp.bfloat16),
        ],
        compiler_params=pltpu.CompilerParams(vmem_limit_bytes=VMEM_LIMIT),
        cost_estimate=pl.CostEstimate(
            flops=2 * count * rows * rows * width,
            bytes_accessed=2 * count * rows * (2 * width + rows),
            transcendentals=0,
        ),
    )(order, *pieces)


def mixers(grams_now):
    return [
        quintic_second * gram + quintic_third * dot(half(gram), half(gram)) for gram in grams_now
    ]


def next_grams(grams_now, mixes):
    lefts = [
        quintic_first * gram + dot(half(mix), half(gram)) for gram, mix in zip(grams_now, mixes)
    ]
    return [quintic_first * left + dot(half(left), half(mix)) for left, mix in zip(lefts, mixes)]


def chain_kernel(parts, *refs):
    gram_refs = refs[:parts]
    chain_ref, squares_ref = refs[parts:]
    count, rows, _ = chain_ref.shape
    on_diagonal = lax.broadcasted_iota(jnp.int32, (rows, rows), 0) == lax.broadcasted_iota(
        jnp.int32, (rows, rows), 1
    )
    grams_now = []
    inverses = []
    for index in range(count):
        gram = gram_refs[0][index].astype(jnp.float32)
        for ref in gram_refs[1:]:
            gram = gram + ref[index].astype(jnp.float32)
        diagonal = jnp.where(on_diagonal, gram, 0.0)
        squares = jnp.sum(jnp.sum(diagonal, axis=0, keepdims=True), axis=1, keepdims=True)
        squares_ref[index] = jnp.broadcast_to(squares, squares_ref.shape[1:])
        inverse = 1.0 / (jnp.sqrt(squares) + epsilon)
        grams_now.append(gram * inverse * inverse)
        inverses.append(inverse)
    first = mixers(grams_now)
    grams_now = next_grams(grams_now, first)
    second = mixers(grams_now)
    grams_now = next_grams(grams_now, second)
    third = mixers(grams_now)
    pairs = [
        quintic_first * (m0 + m1) + dot(half(m1), half(m0)) for m0, m1 in zip(first, second)
    ]
    cubed = jnp.where(on_diagonal, quintic_first**3, 0.0)
    for index, (pair, m2) in enumerate(zip(pairs, third)):
        whole = quintic_first * pair + quintic_first**2 * m2 + dot(half(m2), half(pair))
        chain_ref[index] = half((cubed + whole) * (factor * inverses[index]))


def chains(gram_parts):
    count, rows, _ = gram_parts[0].shape
    step = 3 if count % 3 == 0 else 1
    parts = len(gram_parts)
    spec = pl.BlockSpec((step, rows, rows), lambda i: (i, 0, 0))
    return pl.pallas_call(
        functools.partial(chain_kernel, parts),
        grid=(count // step,),
        in_specs=[spec] * parts,
        out_specs=[spec, pl.BlockSpec((step, 8, 128), lambda i: (i, 0, 0))],
        out_shape=[
            jax.ShapeDtypeStruct((count, rows, rows), jnp.bfloat16),
            jax.ShapeDtypeStruct((count, 8, 128), jnp.float32),
        ],
        compiler_params=pltpu.CompilerParams(vmem_limit_bytes=VMEM_LIMIT),
        cost_estimate=pl.CostEstimate(
            flops=18 * count * rows * rows * rows,
            bytes_accessed=2 * count * rows * rows * (parts + 1),
            transcendentals=0,
        ),
    )(*gram_parts)


def apply_kernel(sets, first_count, masters, places_ref, spans_ref, slots_ref, order_ref, *refs):
    set_refs = [refs[3 * at : 3 * at + 3] for at in range(sets)]
    master_refs = refs[3 * sets : -6]
    rows_ref, weights_ref, new_rows_ref, owned_ref, rms_ref, scaled_ref = refs[-6:]
    blocks = spans_ref.shape[0]
    height = scaled_ref.shape[0] // blocks
    at = pl.program_id(0)
    matrix = order_ref[at]
    slot = slots_ref[matrix]

    @pl.when(at == 0)
    def _():
        owned_ref[...] = jnp.zeros_like(owned_ref)
        rms_ref[...] = jnp.zeros_like(rms_ref)

    def target(block_at):
        return pl.ds(pl.multiple_of(places_ref[block_at] * height, height), height)

    def span(block_at):
        return pl.ds(pl.multiple_of(spans_ref[block_at] * height, height), height)

    lane = lax.broadcasted_iota(jnp.int32, rms_ref.shape, 1)

    def make(chain_ref, squares_ref, update_ref):
        rms = jnp.sqrt(squares_ref[0, :1, :1] / float(KV * D))
        rms_ref[...] = jnp.where(lane == slot, rms, rms_ref[...])
        scaled_ref[...] = half(dot(chain_ref[0], update_ref[0]))

    for index, chosen in enumerate(set_refs):
        pl.when((at >= first_count) == (index == 1))(functools.partial(make, *chosen))

    decayed = rows_ref[0] * (1.0 - learn_rate * weight_decay)
    new_rows_ref[0] = decayed - learn_rate * scaled_ref[:height].astype(jnp.float32)
    def write(lies):
        for block_at, (piece, where) in enumerate(lies):
            decayed = master_refs[piece][where, 0].astype(jnp.float32) * (
                1.0 - learn_rate * weight_decay
            )
            weights_ref[0, target(block_at)] = half(
                decayed - learn_rate * scaled_ref[span(block_at)].astype(jnp.float32)
            )

    for start, stop, lies in masters:
        pl.when((matrix >= start) & (matrix < stop))(functools.partial(write, lies))

    @pl.when(slot >= 0)
    def _():
        for block_at in range(blocks):
            owned_ref[jnp.maximum(slot, 0), target(block_at)] = scaled_ref[span(block_at)]


def applied(places, spans, slots, order, sets, master_pieces, masters, master):
    _, rows, width = sets[0][2].shape
    count, row_count, _ = master.shape
    first_count = sets[0][0].shape[0]

    def by_matrix(height, minor):
        def index(i, places, spans, slots, order):
            return (order[i], 0, 0)

        return pl.BlockSpec((1, height, minor), index)

    def by_piece(piece, start, depth):
        def index(i, places, spans, slots, order):
            return (0, jnp.clip(order[i] - start, 0, piece.shape[1] - 1), 0, 0)

        return pl.BlockSpec((depth, 1, *piece.shape[2:]), index)

    def by_step(array, start):
        last = array.shape[0] - 1

        def index(i, *_):
            return (jnp.clip(i - start, 0, last), 0, 0)

        return pl.BlockSpec((1, *array.shape[1:]), index)

    owned = (MOST, rows, width)
    return pl.pallas_call(
        functools.partial(apply_kernel, len(sets), first_count, masters),
        grid_spec=pltpu.PrefetchScalarGridSpec(
            num_scalar_prefetch=4,
            grid=(count,),
            in_specs=[
                by_step(array, at * first_count) for at, arrays in enumerate(sets) for array in arrays
            ]
            + [by_piece(*piece) for piece in master_pieces]
            + [by_matrix(row_count, width)],
            out_specs=[
                by_matrix(rows, width),
                by_matrix(row_count, width),
                pl.BlockSpec(owned, lambda i, *_: (0, 0, 0)),
                pl.BlockSpec((1, MOST), lambda i, *_: (0, 0)),
            ],
            scratch_shapes=[pltpu.VMEM((rows, width), jnp.bfloat16)],
        ),
        out_shape=[
            jax.ShapeDtypeStruct((count, rows, width), jnp.bfloat16),
            jax.ShapeDtypeStruct(master.shape, jnp.float32),
            jax.ShapeDtypeStruct(owned, jnp.bfloat16),
            jax.ShapeDtypeStruct((1, MOST), jnp.float32),
        ],
        compiler_params=pltpu.CompilerParams(vmem_limit_bytes=VMEM_LIMIT),
        cost_estimate=pl.CostEstimate(
            flops=2 * count * rows * rows * width,
            bytes_accessed=2 * count * rows * (4 * width + rows),
            transcendentals=0,
        ),
    )(
        places,
        spans,
        slots,
        order,
        *[array for arrays in sets for array in arrays],
        *[piece[0] for piece in master_pieces],
        master,
    )


class Grid:
    def __init__(self, count):
        self.count = count
        self.me = lax.axis_index("dp")
        self.x_pairs = [(d, d ^ 1) for d in range(count)]
        self.y_pairs = [(d, d ^ 2) for d in range(count)]

    def over_x(self, value):
        return lax.ppermute(value, "dp", self.x_pairs)

    def over_y(self, value):
        return lax.ppermute(value, "dp", self.y_pairs)

    def over_z(self, value, shift):
        pairs = [(d, (d // 4 + shift) % LINE * 4 + d % 4) for d in range(self.count)]
        return lax.ppermute(value, "dp", pairs)


def place(me, dx, dy, dz):
    z = ((me >> 2) + dz) & (LINE - 1)
    return z * 4 + ((me & 3) ^ (2 * dy + dx))


def after(value, *others):
    return lax.optimization_barrier((value, *others))[0]


def added(*values):
    return sum(value.astype(jnp.float32) for value in values)


class MasterGather:
    def __init__(self, grid, master):
        self.grid = grid
        self.lines = [[z * 4 + corner for z in range(LINE)] for corner in range(4)]
        self.split = master.shape[0] // 2
        self.own = half(master)
        self.line = lax.all_gather(self.own, "dp", axis_index_groups=self.lines)

    def near(self, *ties):
        line = after(self.line, *ties)
        self.high = line[:, self.split :]
        sent = jnp.concatenate([self.high, self.own[None, : self.split]])
        self.near_x = self.grid.over_x(sent)
        self.near_y = self.grid.over_y(sent)

    def low_plane(self):
        low_x, low_y = self.near_x[LINE], self.near_y[LINE]
        self.plane = jnp.stack([self.own[: self.split], low_y, low_x, self.grid.over_x(low_y)])

    def low_lines(self, *ties):
        low = lax.all_gather(after(self.plane, *ties), "dp", axis_index_groups=self.lines)
        self.low = low.reshape(4 * LINE, *low.shape[2:])

    def high_corners(self, *ties):
        near_y = after(self.near_y, *ties)
        near_x = after(self.near_x, *ties)
        self.far_x = self.grid.over_x(near_y[: LINE // 2])
        self.far_y = self.grid.over_y(near_x[LINE // 2 : LINE])

    def pieces(self):
        high = [self.high, self.near_y, self.near_x, self.far_x, self.far_y]
        depths = [LINE, LINE, LINE, LINE // 2, LINE // 2]
        return [(self.low, 0, 4 * LINE)] + [
            (piece, self.split, depth) for piece, depth in zip(high, depths)
        ]

    def masters(self, matrices):
        low = [(0, z * 4 + at) for at in range(4) for z in range(LINE)]
        high = [(piece, z) for piece in (1, 2, 3) for z in range(LINE)]
        high += [(4 + z // 2, z % 2) for z in range(LINE)]
        return [(0, self.split, low), (self.split, matrices, high)]

    def places(self):
        corner, z_mine = self.grid.me & 3, self.grid.me >> 2
        places = [
            z * 4 + (corner ^ (2 * dy + dx)) for dx in range(2) for dy in range(2) for z in range(LINE)
        ]
        spans = [at * 4 + ((z - z_mine) & (LINE - 1)) for at in range(4) for z in range(LINE)]
        return jnp.stack(places).astype(jnp.int32), jnp.stack(spans).astype(jnp.int32)


def reduce_scatter(grid, terms, row_count, master_gather):
    def term(me, dx, dy, dz):
        start = place(me, dx, dy, dz) * row_count
        return lax.dynamic_slice_in_dim(terms, start, row_count, axis=1)

    raw_far1, raw_far2 = term(grid.me, 1, 1, 1), term(grid.me, 1, 1, 2)
    me = after(grid.me, raw_far1, raw_far2, master_gather.own)
    raw = {
        where: term(me, *where)
        for where in [(1, 0, 1), (1, 1, 3), (0, 1, 2), (0, 1, 3), (1, 1, 0), (1, 0, 0)]
    }
    far1 = grid.over_x(raw_far1)
    far2 = grid.over_y(raw_far2)
    along_x1 = grid.over_x(raw[1, 0, 1])
    far3 = grid.over_y(raw[1, 1, 3])
    along_y2 = grid.over_y(raw[0, 1, 2])
    me = after(grid.me, *raw.values())
    rest = [(1, 0, 2), (0, 1, 1), (1, 0, 3), (0, 1, 0)] + [(0, 0, dz) for dz in range(LINE)]
    raw.update(zip(rest, lax.optimization_barrier([term(me, *where) for where in rest])))

    far1, far2, here = lax.optimization_barrier((far1, far2, [raw[where] for where in rest]))
    raw.update(zip(rest, here))
    sent_x2 = half(added(raw[1, 0, 2], far2))
    sent_y1 = half(added(raw[0, 1, 1], far1))
    along_x2 = grid.over_x(sent_x2)
    along_y1 = grid.over_y(sent_y1)

    far0 = grid.over_x(after(raw[1, 1, 0], along_x1, sent_x2, sent_y1))

    mine2, mine3 = after((raw[0, 0, 2], raw[1, 0, 3]), along_x2, along_y2)
    near2 = half(added(mine2, along_x2, along_y2))
    sent_x3 = half(added(mine3, far3))
    line2 = grid.over_z(near2, 2)
    along_x3 = grid.over_x(sent_x3)
    along_y3 = grid.over_y(after(raw[0, 1, 3], along_y2, far3))

    near1 = half(added(after(raw[0, 0, 1], near2, sent_x3), along_x1, along_y1))
    line1 = grid.over_z(near1, 1)
    along_x0 = grid.over_x(after(raw[1, 0, 0], near1))

    sent_y0 = half(added(after(raw[0, 1, 0], near1), far0))
    near3 = half(added(after(raw[0, 0, 3], sent_y0, line2), along_x3, along_y3))
    line3 = grid.over_z(near3, 3)
    master_gather.near(near3, sent_y0)
    along_y0 = grid.over_y(sent_y0)
    mine = after(raw[0, 0, 0], near3, sent_y0, line2)
    return added(mine, along_x0, along_y0, line1, line2, line3)


def all_gather(grid, own, before_z2, before_x2):
    x0, y0 = grid.over_x(own), grid.over_y(own)
    z1, z3 = grid.over_z(own, LINE - 1), grid.over_z(own, 1)
    far0 = grid.over_x(y0)
    x1, y1 = grid.over_x(z1), grid.over_y(z1)
    x3, y3 = grid.over_x(z3), grid.over_y(z3)
    z2 = grid.over_z(after(own, z1, z3, *before_z2), 2)
    far3 = grid.over_y(x3)
    sent = after(z2, before_x2)
    x2, y2 = grid.over_x(sent), grid.over_y(sent)
    far1 = grid.over_x(y1)
    far2 = grid.over_y(x2)
    return [own, z1, z2, z3, y0, y1, y2, y3, x0, x1, x2, x3, far0, far1, far2, far3]


def updated(summed, momentum):
    new_momentum = momentum_decay * momentum + summed
    return new_momentum, half(summed + momentum_decay * new_momentum)


def per_device(gradients, momentum, master, owners):
    me = lax.axis_index("dp")
    dp_count = lax.axis_size("dp")
    matrices, row_count, width = momentum.shape
    terms = gradients[0]
    held = owners == me
    index = jnp.arange(matrices)
    rank = jnp.sum(held[None, :] & (index[None, :] < index[:, None]), axis=1)
    slots = jnp.where(held, rank, -1).astype(jnp.int32)

    in_pieces = dp_count == 4 * LINE and row_count % 32 == 0
    if in_pieces:
        grid = Grid(dp_count)
        rows = master
        master_gather = MasterGather(grid, master)
        places, spans = master_gather.places()
        summed = reduce_scatter(grid, terms, row_count, master_gather)
        new_momentum, own = updated(summed, momentum)
        master_gather.low_plane()
        pieces = all_gather(
            grid, own, (master_gather.near_x, master_gather.near_y), master_gather.plane
        )
        master_gather.low_lines(*pieces[1:4])
        master_gather.high_corners(*pieces[1:])
        master_pieces, masters = master_gather.pieces(), master_gather.masters(matrices)
    else:
        places = spans = jnp.zeros((1,), jnp.int32)
        rows = jnp.zeros((matrices, terms.shape[1], width), jnp.float32)
        rows = lax.dynamic_update_slice_in_dim(rows, master, me * row_count, axis=1)
        summed = lax.psum_scatter(terms, "dp", scatter_dimension=1, tiled=True)
        new_momentum, own = updated(summed.astype(jnp.float32), momentum)
        master_pieces = [(lax.all_gather(half(master), "dp", axis=1, tiled=True)[None], 0, 1)]
        masters = [(0, matrices, [(0, 0)])]
        pieces = [lax.all_gather(own, "dp", axis=1, tiled=True)]

    order = jnp.arange(matrices, dtype=jnp.int32)
    if lax.axis_size("col") == 2 and matrices % 2 == 0:
        size = matrices // 2
        order = (order + lax.axis_index("col") * size) % matrices
        mine, theirs = order[:size], order[size:]
        their_update, their_gram = grams(pieces, theirs)
        swap = [(0, 1), (1, 0)]
        other_part = lax.ppermute(their_gram, "col", swap)
        my_update, my_gram = grams(pieces, mine)
        chain, squares = chains([my_gram, other_part])
        sent = chain
        if in_pieces:
            sent = after(chain, master_gather.far_x, master_gather.far_y)
        other = [lax.ppermute(sent, "col", swap), lax.ppermute(squares, "col", swap)]
        sets = [[chain, squares, my_update], [*other, their_update]]
    else:
        update, gram = grams(pieces, order)
        sets = [[*chains([lax.psum(gram, "col")]), update]]
    new_weights, new_master, owned_updates, rms = applied(
        places, spans, slots, order, sets, master_pieces, masters, rows
    )
    if not in_pieces:
        new_master = lax.dynamic_slice_in_dim(new_master, me * row_count, row_count, axis=1)
    return (new_weights, new_master, new_momentum, owned_updates[None], rms)


def solution(mesh):
    return jax.shard_map(
        per_device,
        mesh=mesh,
        in_specs=(P("dp", None, None, "col"), P(None, "dp", "col"), P(None, "dp", "col"), P()),
        out_specs=(
            P(None, None, "col"),
            P(None, "dp", "col"),
            P(None, "dp", "col"),
            P("dp", None, None, "col"),
            P("dp", None),
        ),
        check_vma=False,
    )
```

```python
import functools
import math

import jax
import jax.numpy as jnp
from jax import lax
from jax.experimental import pallas as pl
from jax.experimental.pallas import tpu as pltpu
from jax.sharding import PartitionSpec as P

KV = 512
D = 2048
MOST = 2

quintic_first = 3.4445
quintic_second = -4.775
quintic_third = 2.0315
momentum_decay = 0.95
learn_rate = 0.3
weight_decay = 0.1
epsilon = 1e-07
factor = 0.2 * math.sqrt(max(KV, D))

MIB = 1024 * 1024
LINE = 4


def dot(left, right):
    return jnp.dot(left, right, preferred_element_type=jnp.float32)


def half(value):
    return value.astype(jnp.bfloat16)


def gram_kernel(order_ref, *refs):
    piece_refs, (update_ref, gram_ref) = refs[:-2], refs[-2:]
    start = 0
    for ref in piece_refs:
        rows = ref.shape[1]
        update_ref[0, start : start + rows] = ref[0]
        start += rows
    block = update_ref[0]
    gram = lax.dot_general(
        block, block, (((1,), (1,)), ((), ())), preferred_element_type=jnp.float32
    )
    gram_ref[0] = half(gram)


def grams(pieces, order):
    width = pieces[0].shape[2]
    count = order.shape[0]
    rows = sum(piece.shape[1] for piece in pieces)

    def spec(minor):
        return pl.BlockSpec((1, rows, minor), lambda i, order: (i, 0, 0))

    return pl.pallas_call(
        gram_kernel,
        grid_spec=pltpu.PrefetchScalarGridSpec(
            num_scalar_prefetch=1,
            grid=(count,),
            in_specs=[
                pl.BlockSpec((1, *piece.shape[1:]), lambda i, order: (order[i], 0, 0))
                for piece in pieces
            ],
            out_specs=[spec(width), spec(rows)],
        ),
        out_shape=[
            jax.ShapeDtypeStruct((count, rows, width), jnp.bfloat16),
            jax.ShapeDtypeStruct((count, rows, rows), jnp.bfloat16),
        ],
        compiler_params=pltpu.CompilerParams(vmem_limit_bytes=9 * MIB),
        cost_estimate=pl.CostEstimate(
            flops=2 * count * rows * rows * width,
            bytes_accessed=2 * count * rows * (2 * width + rows),
            transcendentals=0,
        ),
    )(order, *pieces)


def mixers(grams_now):
    return [
        quintic_second * gram + quintic_third * dot(half(gram), half(gram)) for gram in grams_now
    ]


def next_grams(grams_now, mixes):
    lefts = [
        quintic_first * gram + dot(half(mix), half(gram)) for gram, mix in zip(grams_now, mixes)
    ]
    return [quintic_first * left + dot(half(left), half(mix)) for left, mix in zip(lefts, mixes)]


def chain_kernel(parts, *refs):
    gram_refs = refs[:parts]
    chain_ref, squares_ref = refs[parts:]
    count, rows, _ = chain_ref.shape
    on_diagonal = lax.broadcasted_iota(jnp.int32, (rows, rows), 0) == lax.broadcasted_iota(
        jnp.int32, (rows, rows), 1
    )
    grams_now = []
    inverses = []
    for index in range(count):
        gram = gram_refs[0][index].astype(jnp.float32)
        for ref in gram_refs[1:]:
            gram = gram + ref[index].astype(jnp.float32)
        diagonal = jnp.where(on_diagonal, gram, 0.0)
        squares = jnp.sum(jnp.sum(diagonal, axis=0, keepdims=True), axis=1, keepdims=True)
        squares_ref[index] = jnp.broadcast_to(squares, squares_ref.shape[1:])
        inverse = 1.0 / (jnp.sqrt(squares) + epsilon)
        grams_now.append(gram * inverse * inverse)
        inverses.append(inverse)
    first = mixers(grams_now)
    grams_now = next_grams(grams_now, first)
    second = mixers(grams_now)
    grams_now = next_grams(grams_now, second)
    third = mixers(grams_now)
    pairs = [
        quintic_first * (m0 + m1) + dot(half(m1), half(m0)) for m0, m1 in zip(first, second)
    ]
    cubed = jnp.where(on_diagonal, quintic_first**3, 0.0)
    for index, (pair, m2) in enumerate(zip(pairs, third)):
        whole = quintic_first * pair + quintic_first**2 * m2 + dot(half(m2), half(pair))
        chain_ref[index] = half((cubed + whole) * (factor * inverses[index]))


def chains(gram_parts):
    count, rows, _ = gram_parts[0].shape
    step = 3 if count % 3 == 0 else 1
    parts = len(gram_parts)
    spec = pl.BlockSpec((step, rows, rows), lambda i: (i, 0, 0))
    return pl.pallas_call(
        functools.partial(chain_kernel, parts),
        grid=(count // step,),
        in_specs=[spec] * parts,
        out_specs=[spec, pl.BlockSpec((step, 8, 128), lambda i: (i, 0, 0))],
        out_shape=[
            jax.ShapeDtypeStruct((count, rows, rows), jnp.bfloat16),
            jax.ShapeDtypeStruct((count, 8, 128), jnp.float32),
        ],
        compiler_params=pltpu.CompilerParams(vmem_limit_bytes=20 * MIB),
        cost_estimate=pl.CostEstimate(
            flops=18 * count * rows * rows * rows,
            bytes_accessed=2 * count * rows * rows * (parts + 1),
            transcendentals=0,
        ),
    )(*gram_parts)


def apply_kernel(sets, first_count, masters, places_ref, spans_ref, slots_ref, order_ref, *refs):
    set_refs = [refs[3 * at : 3 * at + 3] for at in range(sets)]
    master_refs = refs[3 * sets : -6]
    rows_ref, weights_ref, new_rows_ref, owned_ref, rms_ref, scaled_ref = refs[-6:]
    blocks = spans_ref.shape[0]
    height = scaled_ref.shape[0] // blocks
    at = pl.program_id(0)
    matrix = order_ref[at]
    slot = slots_ref[matrix]

    @pl.when(at == 0)
    def _():
        owned_ref[...] = jnp.zeros_like(owned_ref)
        rms_ref[...] = jnp.zeros_like(rms_ref)

    def target(block_at):
        return pl.ds(pl.multiple_of(places_ref[block_at] * height, height), height)

    def span(block_at):
        return pl.ds(pl.multiple_of(spans_ref[block_at] * height, height), height)

    lane = lax.broadcasted_iota(jnp.int32, rms_ref.shape, 1)

    def make(chain_ref, squares_ref, update_ref):
        rms = jnp.sqrt(squares_ref[0, :1, :1] / float(KV * D))
        rms_ref[...] = jnp.where(lane == slot, rms, rms_ref[...])
        scaled_ref[...] = half(dot(chain_ref[0], update_ref[0]))

    for index, chosen in enumerate(set_refs):
        pl.when((at >= first_count) == (index == 1))(functools.partial(make, *chosen))

    decayed = rows_ref[0] * (1.0 - learn_rate * weight_decay)
    new_rows_ref[0] = decayed - learn_rate * scaled_ref[:height].astype(jnp.float32)
    def write(lies):
        for block_at, (piece, where) in enumerate(lies):
            decayed = master_refs[piece][where, 0].astype(jnp.float32) * (
                1.0 - learn_rate * weight_decay
            )
            weights_ref[0, target(block_at)] = half(
                decayed - learn_rate * scaled_ref[span(block_at)].astype(jnp.float32)
            )

    for start, stop, lies in masters:
        pl.when((matrix >= start) & (matrix < stop))(functools.partial(write, lies))

    @pl.when(slot >= 0)
    def _():
        for block_at in range(blocks):
            owned_ref[jnp.maximum(slot, 0), target(block_at)] = scaled_ref[span(block_at)]


def applied(places, spans, slots, order, sets, master_pieces, masters, master):
    _, rows, width = sets[0][2].shape
    count, row_count, _ = master.shape
    first_count = sets[0][0].shape[0]

    def by_matrix(height, minor):
        def index(i, places, spans, slots, order):
            return (order[i], 0, 0)

        return pl.BlockSpec((1, height, minor), index)

    def by_piece(piece, start, depth):
        def index(i, places, spans, slots, order):
            return (0, jnp.clip(order[i] - start, 0, piece.shape[1] - 1), 0, 0)

        return pl.BlockSpec((depth, 1, *piece.shape[2:]), index)

    def by_step(array, start):
        last = array.shape[0] - 1

        def index(i, *_):
            return (jnp.clip(i - start, 0, last), 0, 0)

        return pl.BlockSpec((1, *array.shape[1:]), index)

    owned = (MOST, rows, width)
    return pl.pallas_call(
        functools.partial(apply_kernel, len(sets), first_count, masters),
        grid_spec=pltpu.PrefetchScalarGridSpec(
            num_scalar_prefetch=4,
            grid=(count,),
            in_specs=[
                by_step(array, at * first_count) for at, arrays in enumerate(sets) for array in arrays
            ]
            + [by_piece(*piece) for piece in master_pieces]
            + [by_matrix(row_count, width)],
            out_specs=[
                by_matrix(rows, width),
                by_matrix(row_count, width),
                pl.BlockSpec(owned, lambda i, *_: (0, 0, 0)),
                pl.BlockSpec((1, MOST), lambda i, *_: (0, 0)),
            ],
            scratch_shapes=[pltpu.VMEM((rows, width), jnp.bfloat16)],
        ),
        out_shape=[
            jax.ShapeDtypeStruct((count, rows, width), jnp.bfloat16),
            jax.ShapeDtypeStruct(master.shape, jnp.float32),
            jax.ShapeDtypeStruct(owned, jnp.bfloat16),
            jax.ShapeDtypeStruct((1, MOST), jnp.float32),
        ],
        compiler_params=pltpu.CompilerParams(vmem_limit_bytes=20 * MIB),
        cost_estimate=pl.CostEstimate(
            flops=2 * count * rows * rows * width,
            bytes_accessed=2 * count * rows * (4 * width + rows),
            transcendentals=0,
        ),
    )(
        places,
        spans,
        slots,
        order,
        *[array for arrays in sets for array in arrays],
        *[piece[0] for piece in master_pieces],
        master,
    )


class Grid:
    def __init__(self, count):
        self.count = count
        self.me = lax.axis_index("dp")
        self.x_pairs = [(d, d ^ 1) for d in range(count)]
        self.y_pairs = [(d, d ^ 2) for d in range(count)]

    def over_x(self, value):
        return lax.ppermute(value, "dp", self.x_pairs)

    def over_y(self, value):
        return lax.ppermute(value, "dp", self.y_pairs)

    def over_z(self, value, shift):
        pairs = [(d, (d // 4 + shift) % LINE * 4 + d % 4) for d in range(self.count)]
        return lax.ppermute(value, "dp", pairs)


def place(me, dx, dy, dz):
    z = ((me >> 2) + dz) & (LINE - 1)
    return z * 4 + ((me & 3) ^ (2 * dy + dx))


def after(value, *others):
    return lax.optimization_barrier((value, *others))[0]


def added(*values):
    return sum(value.astype(jnp.float32) for value in values)


class MasterGather:
    def __init__(self, grid, master):
        self.grid = grid
        self.lines = [[z * 4 + corner for z in range(LINE)] for corner in range(4)]
        self.split = master.shape[0] // 2
        self.own = half(master)
        self.line = lax.all_gather(self.own, "dp", axis_index_groups=self.lines)

    def near(self, *ties):
        line = after(self.line, *ties)
        self.high = line[:, self.split :]
        sent = jnp.concatenate([self.high, self.own[None, : self.split]])
        self.near_x = self.grid.over_x(sent)
        self.near_y = self.grid.over_y(sent)

    def low_plane(self):
        low_x, low_y = self.near_x[LINE], self.near_y[LINE]
        self.plane = jnp.stack([self.own[: self.split], low_y, low_x, self.grid.over_x(low_y)])

    def low_lines(self, *ties):
        low = lax.all_gather(after(self.plane, *ties), "dp", axis_index_groups=self.lines)
        self.low = low.reshape(4 * LINE, *low.shape[2:])

    def high_corners(self, *ties):
        near_y = after(self.near_y, *ties)
        near_x = after(self.near_x, *ties)
        self.far_x = self.grid.over_x(near_y[: LINE // 2])
        self.far_y = self.grid.over_y(near_x[LINE // 2 : LINE])

    def pieces(self):
        high = [self.high, self.near_y, self.near_x, self.far_x, self.far_y]
        depths = [LINE, LINE, LINE, LINE // 2, LINE // 2]
        return [(self.low, 0, 4 * LINE)] + [
            (piece, self.split, depth) for piece, depth in zip(high, depths)
        ]

    def masters(self, matrices):
        low = [(0, z * 4 + at) for at in range(4) for z in range(LINE)]
        high = [(piece, z) for piece in (1, 2, 3) for z in range(LINE)]
        high += [(4 + z // 2, z % 2) for z in range(LINE)]
        return [(0, self.split, low), (self.split, matrices, high)]

    def places(self):
        corner, z_mine = self.grid.me & 3, self.grid.me >> 2
        places = [
            z * 4 + (corner ^ (2 * dy + dx)) for dx in range(2) for dy in range(2) for z in range(LINE)
        ]
        spans = [at * 4 + ((z - z_mine) & (LINE - 1)) for at in range(4) for z in range(LINE)]
        return jnp.stack(places).astype(jnp.int32), jnp.stack(spans).astype(jnp.int32)


def reduce_scatter(grid, terms, row_count, master_gather):
    def term(me, dx, dy, dz):
        start = place(me, dx, dy, dz) * row_count
        return lax.dynamic_slice_in_dim(terms, start, row_count, axis=1)

    me = grid.me
    raw_far1, raw_far2 = term(me, 1, 1, 1), term(me, 1, 1, 2)
    me = after(grid.me, raw_far1, raw_far2, master_gather.own)
    raw_x1, raw_far3, raw_y2 = term(me, 1, 0, 1), term(me, 1, 1, 3), term(me, 0, 1, 2)
    raw_y3, raw_far0, raw_x0 = term(me, 0, 1, 3), term(me, 1, 1, 0), term(me, 1, 0, 0)
    far1 = grid.over_x(raw_far1)
    far2 = grid.over_y(raw_far2)
    along_x1 = grid.over_x(raw_x1)
    far3 = grid.over_y(raw_far3)
    along_y2 = grid.over_y(raw_y2)

    me = after(grid.me, far1, far2, raw_y3)
    sent_x2 = half(added(term(me, 1, 0, 2), far2))
    sent_y1 = half(added(term(me, 0, 1, 1), far1))
    along_x2 = grid.over_x(sent_x2)
    along_y1 = grid.over_y(sent_y1)

    me = after(grid.me, far3, along_x1, sent_x2, sent_y1)
    sent_x3 = half(added(term(me, 1, 0, 3), far3))
    along_x3 = grid.over_x(sent_x3)
    along_y3 = grid.over_y(after(raw_y3, far3, along_x1))

    me = after(grid.me, along_y2, along_x2, sent_x3)
    near2 = half(added(term(me, 0, 0, 2), along_x2, along_y2))
    line2 = grid.over_z(near2, 2)
    far0 = grid.over_x(after(raw_far0, along_x2))

    me = after(grid.me, along_x1, along_y1, along_x3, near2)
    near1 = half(added(term(me, 0, 0, 1), along_x1, along_y1))
    line1 = grid.over_z(near1, 1)
    along_x0 = grid.over_x(after(raw_x0, along_x3))

    me = after(grid.me, along_x3, along_y3, far0, near1)
    near3 = half(added(term(me, 0, 0, 3), along_x3, along_y3))
    sent_y0 = half(added(term(me, 0, 1, 0), far0))
    line3 = grid.over_z(near3, 3)
    master_gather.near(near3, sent_y0)
    along_y0 = grid.over_y(sent_y0)
    me = after(grid.me, near3, sent_y0, line2)
    return added(term(me, 0, 0, 0), along_x0, along_y0, line1, line2, line3)


def all_gather(grid, own, before_z2, before_x2):
    x0, y0 = grid.over_x(own), grid.over_y(own)
    z1, z3 = grid.over_z(own, LINE - 1), grid.over_z(own, 1)
    far0 = grid.over_x(y0)
    x1, y1 = grid.over_x(z1), grid.over_y(z1)
    x3, y3 = grid.over_x(z3), grid.over_y(z3)
    z2 = grid.over_z(after(own, z1, z3, *before_z2), 2)
    far3 = grid.over_y(x3)
    sent = after(z2, before_x2)
    x2, y2 = grid.over_x(sent), grid.over_y(sent)
    far1 = grid.over_x(y1)
    far2 = grid.over_y(x2)
    return [own, z1, z2, z3, y0, y1, y2, y3, x0, x1, x2, x3, far0, far1, far2, far3]


def updated(summed, momentum):
    new_momentum = momentum_decay * momentum + summed
    return new_momentum, half(summed + momentum_decay * new_momentum)


def per_device(gradients, momentum, master, owners):
    me = lax.axis_index("dp")
    dp_count = lax.axis_size("dp")
    matrices, row_count, width = momentum.shape
    terms = gradients[0]
    held = owners == me
    index = jnp.arange(matrices)
    rank = jnp.sum(held[None, :] & (index[None, :] < index[:, None]), axis=1)
    slots = jnp.where(held, rank, -1).astype(jnp.int32)

    in_pieces = dp_count == 4 * LINE and row_count % 32 == 0
    if in_pieces:
        grid = Grid(dp_count)
        rows = master
        master_gather = MasterGather(grid, master)
        places, spans = master_gather.places()
        summed = reduce_scatter(grid, terms, row_count, master_gather)
        new_momentum, own = updated(summed, momentum)
        master_gather.low_plane()
        pieces = all_gather(
            grid, own, (master_gather.near_x, master_gather.near_y), master_gather.plane
        )
        master_gather.low_lines(*pieces[1:4])
        master_gather.high_corners(*pieces[1:])
        master_pieces, masters = master_gather.pieces(), master_gather.masters(matrices)
    else:
        places = spans = jnp.zeros((1,), jnp.int32)
        rows = jnp.zeros((matrices, terms.shape[1], width), jnp.float32)
        rows = lax.dynamic_update_slice_in_dim(rows, master, me * row_count, axis=1)
        summed = lax.psum_scatter(terms, "dp", scatter_dimension=1, tiled=True)
        new_momentum, own = updated(summed.astype(jnp.float32), momentum)
        master_pieces = [(lax.all_gather(half(master), "dp", axis=1, tiled=True)[None], 0, 1)]
        masters = [(0, matrices, [(0, 0)])]
        pieces = [lax.all_gather(own, "dp", axis=1, tiled=True)]

    order = jnp.arange(matrices, dtype=jnp.int32)
    if lax.axis_size("col") == 2 and matrices % 2 == 0:
        size = matrices // 2
        order = (order + lax.axis_index("col") * size) % matrices
        mine, theirs = order[:size], order[size:]
        their_update, their_gram = grams(pieces, theirs)
        swap = [(0, 1), (1, 0)]
        other_part = lax.ppermute(their_gram, "col", swap)
        my_update, my_gram = grams(pieces, mine)
        chain, squares = chains([my_gram, other_part])
        sent = chain
        if in_pieces:
            sent = after(chain, master_gather.far_x, master_gather.far_y)
        other = [lax.ppermute(sent, "col", swap), lax.ppermute(squares, "col", swap)]
        sets = [[chain, squares, my_update], [*other, their_update]]
    else:
        update, gram = grams(pieces, order)
        sets = [[*chains([lax.psum(gram, "col")]), update]]
    new_weights, new_master, owned_updates, rms = applied(
        places, spans, slots, order, sets, master_pieces, masters, rows
    )
    if not in_pieces:
        new_master = lax.dynamic_slice_in_dim(new_master, me * row_count, row_count, axis=1)
    return (new_weights, new_master, new_momentum, owned_updates[None], rms)


def solution(mesh):
    return jax.shard_map(
        per_device,
        mesh=mesh,
        in_specs=(P("dp", None, None, "col"), P(None, "dp", "col"), P(None, "dp", "col"), P()),
        out_specs=(
            P(None, None, "col"),
            P(None, "dp", "col"),
            P(None, "dp", "col"),
            P("dp", None, None, "col"),
            P("dp", None),
        ),
        check_vma=False,
    )
```

```python
import functools
import math

import jax
import jax.numpy as jnp
from jax import lax
from jax.experimental import pallas as pl
from jax.experimental.pallas import tpu as pltpu
from jax.sharding import PartitionSpec as P

KV = 512
D = 2048
MOST = 2

quintic_first = 3.4445
quintic_second = -4.775
quintic_third = 2.0315
momentum_decay = 0.95
learn_rate = 0.3
weight_decay = 0.1
epsilon = 1e-07
factor = 0.2 * math.sqrt(max(KV, D))

MIB = 1024 * 1024
LINE = 4


def dot(left, right):
    return jnp.dot(left, right, preferred_element_type=jnp.float32)


def half(value):
    return value.astype(jnp.bfloat16)


def gram_kernel(order_ref, *refs):
    piece_refs, (update_ref, gram_ref) = refs[:-2], refs[-2:]
    start = 0
    for ref in piece_refs:
        rows = ref.shape[1]
        update_ref[0, start : start + rows] = ref[0]
        start += rows
    block = update_ref[0]
    gram = lax.dot_general(
        block, block, (((1,), (1,)), ((), ())), preferred_element_type=jnp.float32
    )
    gram_ref[0] = half(gram)


def grams(pieces, order):
    width = pieces[0].shape[2]
    count = order.shape[0]
    rows = sum(piece.shape[1] for piece in pieces)

    def spec(minor):
        return pl.BlockSpec((1, rows, minor), lambda i, order: (i, 0, 0))

    return pl.pallas_call(
        gram_kernel,
        grid_spec=pltpu.PrefetchScalarGridSpec(
            num_scalar_prefetch=1,
            grid=(count,),
            in_specs=[
                pl.BlockSpec((1, *piece.shape[1:]), lambda i, order: (order[i], 0, 0))
                for piece in pieces
            ],
            out_specs=[spec(width), spec(rows)],
        ),
        out_shape=[
            jax.ShapeDtypeStruct((count, rows, width), jnp.bfloat16),
            jax.ShapeDtypeStruct((count, rows, rows), jnp.bfloat16),
        ],
        compiler_params=pltpu.CompilerParams(vmem_limit_bytes=56 * MIB),
        cost_estimate=pl.CostEstimate(
            flops=2 * count * rows * rows * width,
            bytes_accessed=2 * count * rows * (2 * width + rows),
            transcendentals=0,
        ),
    )(order, *pieces)


def mixers(grams_now):
    return [
        quintic_second * gram + quintic_third * dot(half(gram), half(gram)) for gram in grams_now
    ]


def next_grams(grams_now, mixes):
    lefts = [
        quintic_first * gram + dot(half(mix), half(gram)) for gram, mix in zip(grams_now, mixes)
    ]
    return [quintic_first * left + dot(half(left), half(mix)) for left, mix in zip(lefts, mixes)]


def chain_kernel(parts, *refs):
    gram_refs = refs[:parts]
    chain_ref, squares_ref = refs[parts:]
    count, rows, _ = chain_ref.shape
    on_diagonal = lax.broadcasted_iota(jnp.int32, (rows, rows), 0) == lax.broadcasted_iota(
        jnp.int32, (rows, rows), 1
    )
    grams_now = []
    inverses = []
    for index in range(count):
        gram = gram_refs[0][index].astype(jnp.float32)
        for ref in gram_refs[1:]:
            gram = gram + ref[index].astype(jnp.float32)
        diagonal = jnp.where(on_diagonal, gram, 0.0)
        squares = jnp.sum(jnp.sum(diagonal, axis=0, keepdims=True), axis=1, keepdims=True)
        squares_ref[index] = jnp.broadcast_to(squares, squares_ref.shape[1:])
        inverse = 1.0 / (jnp.sqrt(squares) + epsilon)
        grams_now.append(gram * inverse * inverse)
        inverses.append(inverse)
    first = mixers(grams_now)
    grams_now = next_grams(grams_now, first)
    second = mixers(grams_now)
    grams_now = next_grams(grams_now, second)
    third = mixers(grams_now)
    pairs = [
        quintic_first * (m0 + m1) + dot(half(m1), half(m0)) for m0, m1 in zip(first, second)
    ]
    cubed = jnp.where(on_diagonal, quintic_first**3, 0.0)
    for index, (pair, m2) in enumerate(zip(pairs, third)):
        whole = quintic_first * pair + quintic_first**2 * m2 + dot(half(m2), half(pair))
        chain_ref[index] = half((cubed + whole) * (factor * inverses[index]))


def chains(gram_parts):
    count, rows, _ = gram_parts[0].shape
    step = 3 if count % 3 == 0 else 1
    parts = len(gram_parts)
    spec = pl.BlockSpec((step, rows, rows), lambda i: (i, 0, 0))
    return pl.pallas_call(
        functools.partial(chain_kernel, parts),
        grid=(count // step,),
        in_specs=[spec] * parts,
        out_specs=[spec, pl.BlockSpec((step, 8, 128), lambda i: (i, 0, 0))],
        out_shape=[
            jax.ShapeDtypeStruct((count, rows, rows), jnp.bfloat16),
            jax.ShapeDtypeStruct((count, 8, 128), jnp.float32),
        ],
        compiler_params=pltpu.CompilerParams(vmem_limit_bytes=20 * MIB),
        cost_estimate=pl.CostEstimate(
            flops=18 * count * rows * rows * rows,
            bytes_accessed=2 * count * rows * rows * (parts + 1),
            transcendentals=0,
        ),
    )(*gram_parts)


def apply_kernel(sets, first_count, masters, places_ref, spans_ref, slots_ref, order_ref, *refs):
    set_refs = [refs[3 * at : 3 * at + 3] for at in range(sets)]
    master_refs = refs[3 * sets : -6]
    rows_ref, weights_ref, new_rows_ref, owned_ref, rms_ref, scaled_ref = refs[-6:]
    blocks = spans_ref.shape[0]
    height = scaled_ref.shape[0] // blocks
    at = pl.program_id(0)
    matrix = order_ref[at]
    slot = slots_ref[matrix]

    @pl.when(at == 0)
    def _():
        owned_ref[...] = jnp.zeros_like(owned_ref)
        rms_ref[...] = jnp.zeros_like(rms_ref)

    def target(block_at):
        return pl.ds(pl.multiple_of(places_ref[block_at] * height, height), height)

    def span(block_at):
        return pl.ds(pl.multiple_of(spans_ref[block_at] * height, height), height)

    lane = lax.broadcasted_iota(jnp.int32, rms_ref.shape, 1)

    def make(chain_ref, squares_ref, update_ref):
        rms = jnp.sqrt(squares_ref[0, :1, :1] / float(KV * D))
        rms_ref[...] = jnp.where(lane == slot, rms, rms_ref[...])
        scaled_ref[...] = half(dot(chain_ref[0], update_ref[0]))

    for index, chosen in enumerate(set_refs):
        pl.when((at >= first_count) == (index == 1))(functools.partial(make, *chosen))

    decayed = rows_ref[0] * (1.0 - learn_rate * weight_decay)
    new_rows_ref[0] = decayed - learn_rate * scaled_ref[:height].astype(jnp.float32)
    def write(lies):
        for block_at, (piece, where) in enumerate(lies):
            decayed = master_refs[piece][where, 0].astype(jnp.float32) * (
                1.0 - learn_rate * weight_decay
            )
            weights_ref[0, target(block_at)] = half(
                decayed - learn_rate * scaled_ref[span(block_at)].astype(jnp.float32)
            )

    for start, stop, lies in masters:
        pl.when((matrix >= start) & (matrix < stop))(functools.partial(write, lies))

    @pl.when(slot >= 0)
    def _():
        for block_at in range(blocks):
            owned_ref[jnp.maximum(slot, 0), target(block_at)] = scaled_ref[span(block_at)]


def applied(places, spans, slots, order, sets, master_pieces, masters, master):
    _, rows, width = sets[0][2].shape
    count, row_count, _ = master.shape
    first_count = sets[0][0].shape[0]

    def by_matrix(height, minor):
        def index(i, places, spans, slots, order):
            return (order[i], 0, 0)

        return pl.BlockSpec((1, height, minor), index)

    def by_piece(piece, start, depth):
        def index(i, places, spans, slots, order):
            return (0, jnp.clip(order[i] - start, 0, piece.shape[1] - 1), 0, 0)

        return pl.BlockSpec((depth, 1, *piece.shape[2:]), index)

    def by_step(array, start):
        last = array.shape[0] - 1

        def index(i, *_):
            return (jnp.clip(i - start, 0, last), 0, 0)

        return pl.BlockSpec((1, *array.shape[1:]), index)

    owned = (MOST, rows, width)
    return pl.pallas_call(
        functools.partial(apply_kernel, len(sets), first_count, masters),
        grid_spec=pltpu.PrefetchScalarGridSpec(
            num_scalar_prefetch=4,
            grid=(count,),
            in_specs=[
                by_step(array, at * first_count) for at, arrays in enumerate(sets) for array in arrays
            ]
            + [by_piece(*piece) for piece in master_pieces]
            + [by_matrix(row_count, width)],
            out_specs=[
                by_matrix(rows, width),
                by_matrix(row_count, width),
                pl.BlockSpec(owned, lambda i, *_: (0, 0, 0)),
                pl.BlockSpec((1, MOST), lambda i, *_: (0, 0)),
            ],
            scratch_shapes=[pltpu.VMEM((rows, width), jnp.bfloat16)],
        ),
        out_shape=[
            jax.ShapeDtypeStruct((count, rows, width), jnp.bfloat16),
            jax.ShapeDtypeStruct(master.shape, jnp.float32),
            jax.ShapeDtypeStruct(owned, jnp.bfloat16),
            jax.ShapeDtypeStruct((1, MOST), jnp.float32),
        ],
        compiler_params=pltpu.CompilerParams(vmem_limit_bytes=56 * MIB),
        cost_estimate=pl.CostEstimate(
            flops=2 * count * rows * rows * width,
            bytes_accessed=2 * count * rows * (4 * width + rows),
            transcendentals=0,
        ),
    )(
        places,
        spans,
        slots,
        order,
        *[array for arrays in sets for array in arrays],
        *[piece[0] for piece in master_pieces],
        master,
    )


class Grid:
    def __init__(self, count):
        self.count = count
        self.me = lax.axis_index("dp")
        self.x_pairs = [(d, d ^ 1) for d in range(count)]
        self.y_pairs = [(d, d ^ 2) for d in range(count)]

    def over_x(self, value):
        return lax.ppermute(value, "dp", self.x_pairs)

    def over_y(self, value):
        return lax.ppermute(value, "dp", self.y_pairs)

    def over_z(self, value, shift):
        pairs = [(d, (d // 4 + shift) % LINE * 4 + d % 4) for d in range(self.count)]
        return lax.ppermute(value, "dp", pairs)


def place(me, dx, dy, dz):
    z = ((me >> 2) + dz) & (LINE - 1)
    return z * 4 + ((me & 3) ^ (2 * dy + dx))


def after(value, *others):
    return lax.optimization_barrier((value, *others))[0]


def added(*values):
    return sum(value.astype(jnp.float32) for value in values)


class MasterGather:
    def __init__(self, grid, master):
        self.grid = grid
        self.lines = [[z * 4 + corner for z in range(LINE)] for corner in range(4)]
        self.split = master.shape[0] // 2
        self.own = half(master)
        self.line = lax.all_gather(self.own, "dp", axis_index_groups=self.lines)

    def near(self, *ties):
        line = after(self.line, *ties)
        self.high = line[:, self.split :]
        sent = jnp.concatenate([self.high, self.own[None, : self.split]])
        self.near_x = self.grid.over_x(sent)
        self.near_y = self.grid.over_y(sent)

    def low_plane(self):
        low_x, low_y = self.near_x[LINE], self.near_y[LINE]
        self.plane = jnp.stack([self.own[: self.split], low_y, low_x, self.grid.over_x(low_y)])

    def low_lines(self, *ties):
        low = lax.all_gather(after(self.plane, *ties), "dp", axis_index_groups=self.lines)
        self.low = low.reshape(4 * LINE, *low.shape[2:])

    def high_corners(self, *ties):
        self.far = self.grid.over_x(after(self.near_y, *ties)[:LINE])

    def pieces(self):
        high = [self.high, self.near_y, self.near_x, self.far]
        return [(self.low, 0, 4 * LINE)] + [(piece, self.split, LINE) for piece in high]

    def masters(self, matrices):
        low = [(0, z * 4 + at) for at in range(4) for z in range(LINE)]
        high = [(piece, z) for piece in (1, 2, 3, 4) for z in range(LINE)]
        return [(0, self.split, low), (self.split, matrices, high)]

    def places(self):
        corner, z_mine = self.grid.me & 3, self.grid.me >> 2
        places = [
            z * 4 + (corner ^ (2 * dy + dx)) for dx in range(2) for dy in range(2) for z in range(LINE)
        ]
        spans = [at * 4 + ((z - z_mine) & (LINE - 1)) for at in range(4) for z in range(LINE)]
        return jnp.stack(places).astype(jnp.int32), jnp.stack(spans).astype(jnp.int32)


def reduce_scatter(grid, terms, row_count, master_gather):
    def term(me, dx, dy, dz):
        start = place(me, dx, dy, dz) * row_count
        return lax.dynamic_slice_in_dim(terms, start, row_count, axis=1)

    me = grid.me
    raw_far1, raw_far2 = term(me, 1, 1, 1), term(me, 1, 1, 2)
    me = after(grid.me, raw_far1, raw_far2, master_gather.own)
    raw_x1, raw_far3, raw_y2 = term(me, 1, 0, 1), term(me, 1, 1, 3), term(me, 0, 1, 2)
    raw_y3, raw_far0, raw_x0 = term(me, 0, 1, 3), term(me, 1, 1, 0), term(me, 1, 0, 0)
    far1 = grid.over_x(raw_far1)
    far2 = grid.over_y(raw_far2)
    along_x1 = grid.over_x(raw_x1)
    far3 = grid.over_y(raw_far3)
    along_y2 = grid.over_y(raw_y2)

    me = after(grid.me, far1, far2, raw_y3)
    sent_x2 = half(added(term(me, 1, 0, 2), far2))
    sent_y1 = half(added(term(me, 0, 1, 1), far1))
    along_x2 = grid.over_x(sent_x2)
    along_y1 = grid.over_y(sent_y1)

    me = after(grid.me, far3, along_x1, sent_x2, sent_y1)
    sent_x3 = half(added(term(me, 1, 0, 3), far3))
    along_x3 = grid.over_x(sent_x3)
    along_y3 = grid.over_y(after(raw_y3, far3, along_x1))

    me = after(grid.me, along_y2, along_x2, sent_x3)
    near2 = half(added(term(me, 0, 0, 2), along_x2, along_y2))
    line2 = grid.over_z(near2, 2)
    far0 = grid.over_x(after(raw_far0, along_x2))

    me = after(grid.me, along_x1, along_y1, along_x3, near2)
    near1 = half(added(term(me, 0, 0, 1), along_x1, along_y1))
    line1 = grid.over_z(near1, 1)
    along_x0 = grid.over_x(after(raw_x0, along_x3))

    me = after(grid.me, along_x3, along_y3, far0, near1)
    near3 = half(added(term(me, 0, 0, 3), along_x3, along_y3))
    sent_y0 = half(added(term(me, 0, 1, 0), far0))
    line3 = grid.over_z(near3, 3)
    master_gather.near(near3, sent_y0)
    along_y0 = grid.over_y(sent_y0)
    me = after(grid.me, near3, sent_y0, line2)
    return added(term(me, 0, 0, 0), along_x0, along_y0, line1, line2, line3)


def all_gather(grid, own, before_z2, before_x2):
    x0, y0 = grid.over_x(own), grid.over_y(own)
    z1, z3 = grid.over_z(own, LINE - 1), grid.over_z(own, 1)
    far0 = grid.over_x(y0)
    x1, y1 = grid.over_x(z1), grid.over_y(z1)
    x3, y3 = grid.over_x(z3), grid.over_y(z3)
    z2 = grid.over_z(after(own, z1, z3, *before_z2), 2)
    far3 = grid.over_y(x3)
    sent = after(z2, before_x2)
    x2, y2 = grid.over_x(sent), grid.over_y(sent)
    far1 = grid.over_x(y1)
    far2 = grid.over_y(x2)
    return [own, z1, z2, z3, y0, y1, y2, y3, x0, x1, x2, x3, far0, far1, far2, far3]


def updated(summed, momentum):
    new_momentum = momentum_decay * momentum + summed
    return new_momentum, half(summed + momentum_decay * new_momentum)


def per_device(gradients, momentum, master, owners):
    me = lax.axis_index("dp")
    dp_count = lax.axis_size("dp")
    matrices, row_count, width = momentum.shape
    terms = gradients[0]
    held = owners == me
    index = jnp.arange(matrices)
    rank = jnp.sum(held[None, :] & (index[None, :] < index[:, None]), axis=1)
    slots = jnp.where(held, rank, -1).astype(jnp.int32)

    in_pieces = dp_count == 4 * LINE and row_count % 32 == 0
    if in_pieces:
        grid = Grid(dp_count)
        rows = master
        master_gather = MasterGather(grid, master)
        places, spans = master_gather.places()
        summed = reduce_scatter(grid, terms, row_count, master_gather)
        new_momentum, own = updated(summed, momentum)
        master_gather.low_plane()
        pieces = all_gather(
            grid, own, (master_gather.near_x, master_gather.near_y), master_gather.plane
        )
        master_gather.low_lines(*pieces[1:4])
        master_gather.high_corners(*pieces[1:])
        master_pieces, masters = master_gather.pieces(), master_gather.masters(matrices)
    else:
        places = spans = jnp.zeros((1,), jnp.int32)
        rows = jnp.zeros((matrices, terms.shape[1], width), jnp.float32)
        rows = lax.dynamic_update_slice_in_dim(rows, master, me * row_count, axis=1)
        summed = lax.psum_scatter(terms, "dp", scatter_dimension=1, tiled=True)
        new_momentum, own = updated(summed.astype(jnp.float32), momentum)
        master_pieces = [(lax.all_gather(half(master), "dp", axis=1, tiled=True)[None], 0, 1)]
        masters = [(0, matrices, [(0, 0)])]
        pieces = [lax.all_gather(own, "dp", axis=1, tiled=True)]

    order = jnp.arange(matrices, dtype=jnp.int32)
    if lax.axis_size("col") == 2 and matrices % 2 == 0:
        size = matrices // 2
        order = (order + lax.axis_index("col") * size) % matrices
        mine, theirs = order[:size], order[size:]
        their_update, their_gram = grams(pieces, theirs)
        swap = [(0, 1), (1, 0)]
        other_part = lax.ppermute(their_gram, "col", swap)
        my_update, my_gram = grams(pieces, mine)
        chain, squares = chains([my_gram, other_part])
        sent = chain
        if in_pieces:
            sent = after(chain, master_gather.far)
        other = [lax.ppermute(sent, "col", swap), lax.ppermute(squares, "col", swap)]
        sets = [[chain, squares, my_update], [*other, their_update]]
    else:
        update, gram = grams(pieces, order)
        sets = [[*chains([lax.psum(gram, "col")]), update]]
    new_weights, new_master, owned_updates, rms = applied(
        places, spans, slots, order, sets, master_pieces, masters, rows
    )
    if not in_pieces:
        new_master = lax.dynamic_slice_in_dim(new_master, me * row_count, row_count, axis=1)
    return (new_weights, new_master, new_momentum, owned_updates[None], rms)


def solution(mesh):
    return jax.shard_map(
        per_device,
        mesh=mesh,
        in_specs=(P("dp", None, None, "col"), P(None, "dp", "col"), P(None, "dp", "col"), P()),
        out_specs=(
            P(None, None, "col"),
            P(None, "dp", "col"),
            P(None, "dp", "col"),
            P("dp", None, None, "col"),
            P("dp", None),
        ),
        check_vma=False,
    )
```

```python
import functools
import math

import jax
import jax.numpy as jnp
from jax import lax
from jax.experimental import pallas as pl
from jax.experimental.pallas import tpu as pltpu
from jax.sharding import PartitionSpec as P

KV = 512
D = 2048
MOST = 2

quintic_first = 3.4445
quintic_second = -4.775
quintic_third = 2.0315
momentum_decay = 0.95
learn_rate = 0.3
weight_decay = 0.1
epsilon = 1e-07
factor = 0.2 * math.sqrt(max(KV, D))

MIB = 1024 * 1024
LINE = 4


def dot(left, right):
    return jnp.dot(left, right, preferred_element_type=jnp.float32)


def half(value):
    return value.astype(jnp.bfloat16)


def gram_kernel(order_ref, *refs):
    piece_refs, (update_ref, gram_ref) = refs[:-2], refs[-2:]
    start = 0
    for ref in piece_refs:
        rows = ref.shape[1]
        update_ref[0, start : start + rows] = ref[0]
        start += rows
    block = update_ref[0]
    gram = lax.dot_general(
        block, block, (((1,), (1,)), ((), ())), preferred_element_type=jnp.float32
    )
    gram_ref[0] = half(gram)


def grams(pieces, order):
    width = pieces[0].shape[2]
    count = order.shape[0]
    rows = sum(piece.shape[1] for piece in pieces)

    def spec(minor):
        return pl.BlockSpec((1, rows, minor), lambda i, order: (i, 0, 0))

    return pl.pallas_call(
        gram_kernel,
        grid_spec=pltpu.PrefetchScalarGridSpec(
            num_scalar_prefetch=1,
            grid=(count,),
            in_specs=[
                pl.BlockSpec((1, *piece.shape[1:]), lambda i, order: (order[i], 0, 0))
                for piece in pieces
            ],
            out_specs=[spec(width), spec(rows)],
        ),
        out_shape=[
            jax.ShapeDtypeStruct((count, rows, width), jnp.bfloat16),
            jax.ShapeDtypeStruct((count, rows, rows), jnp.bfloat16),
        ],
        compiler_params=pltpu.CompilerParams(vmem_limit_bytes=56 * MIB),
        cost_estimate=pl.CostEstimate(
            flops=2 * count * rows * rows * width,
            bytes_accessed=2 * count * rows * (2 * width + rows),
            transcendentals=0,
        ),
    )(order, *pieces)


def mixers(grams_now):
    return [
        quintic_second * gram + quintic_third * dot(half(gram), half(gram)) for gram in grams_now
    ]


def next_grams(grams_now, mixes):
    lefts = [
        quintic_first * gram + dot(half(mix), half(gram)) for gram, mix in zip(grams_now, mixes)
    ]
    return [quintic_first * left + dot(half(left), half(mix)) for left, mix in zip(lefts, mixes)]


def chain_kernel(parts, *refs):
    gram_refs = refs[:parts]
    chain_ref, squares_ref = refs[parts:]
    count, rows, _ = chain_ref.shape
    on_diagonal = lax.broadcasted_iota(jnp.int32, (rows, rows), 0) == lax.broadcasted_iota(
        jnp.int32, (rows, rows), 1
    )
    grams_now = []
    inverses = []
    for index in range(count):
        gram = gram_refs[0][index].astype(jnp.float32)
        for ref in gram_refs[1:]:
            gram = gram + ref[index].astype(jnp.float32)
        diagonal = jnp.where(on_diagonal, gram, 0.0)
        squares = jnp.sum(jnp.sum(diagonal, axis=0, keepdims=True), axis=1, keepdims=True)
        squares_ref[index] = jnp.broadcast_to(squares, squares_ref.shape[1:])
        inverse = 1.0 / (jnp.sqrt(squares) + epsilon)
        grams_now.append(gram * inverse * inverse)
        inverses.append(inverse)
    first = mixers(grams_now)
    grams_now = next_grams(grams_now, first)
    second = mixers(grams_now)
    grams_now = next_grams(grams_now, second)
    third = mixers(grams_now)
    pairs = [
        quintic_first * (m0 + m1) + dot(half(m1), half(m0)) for m0, m1 in zip(first, second)
    ]
    cubed = jnp.where(on_diagonal, quintic_first**3, 0.0)
    for index, (pair, m2) in enumerate(zip(pairs, third)):
        whole = quintic_first * pair + quintic_first**2 * m2 + dot(half(m2), half(pair))
        chain_ref[index] = half((cubed + whole) * (factor * inverses[index]))


def chains(gram_parts):
    count, rows, _ = gram_parts[0].shape
    step = 3 if count % 3 == 0 else 1
    parts = len(gram_parts)
    spec = pl.BlockSpec((step, rows, rows), lambda i: (i, 0, 0))
    return pl.pallas_call(
        functools.partial(chain_kernel, parts),
        grid=(count // step,),
        in_specs=[spec] * parts,
        out_specs=[spec, pl.BlockSpec((step, 8, 128), lambda i: (i, 0, 0))],
        out_shape=[
            jax.ShapeDtypeStruct((count, rows, rows), jnp.bfloat16),
            jax.ShapeDtypeStruct((count, 8, 128), jnp.float32),
        ],
        compiler_params=pltpu.CompilerParams(vmem_limit_bytes=20 * MIB),
        cost_estimate=pl.CostEstimate(
            flops=18 * count * rows * rows * rows,
            bytes_accessed=2 * count * rows * rows * (parts + 1),
            transcendentals=0,
        ),
    )(*gram_parts)


def apply_kernel(sets, first_count, masters, places_ref, spans_ref, slots_ref, order_ref, *refs):
    set_refs = [refs[3 * at : 3 * at + 3] for at in range(sets)]
    master_refs = refs[3 * sets : -6]
    rows_ref, weights_ref, new_rows_ref, owned_ref, rms_ref, scaled_ref = refs[-6:]
    blocks = spans_ref.shape[0]
    height = scaled_ref.shape[0] // blocks
    at = pl.program_id(0)
    matrix = order_ref[at]
    slot = slots_ref[matrix]

    @pl.when(at == 0)
    def _():
        owned_ref[...] = jnp.zeros_like(owned_ref)
        rms_ref[...] = jnp.zeros_like(rms_ref)

    def target(block_at):
        return pl.ds(pl.multiple_of(places_ref[block_at] * height, height), height)

    def span(block_at):
        return pl.ds(pl.multiple_of(spans_ref[block_at] * height, height), height)

    lane = lax.broadcasted_iota(jnp.int32, rms_ref.shape, 1)

    def make(chain_ref, squares_ref, update_ref):
        rms = jnp.sqrt(squares_ref[0, :1, :1] / float(KV * D))
        rms_ref[...] = jnp.where(lane == slot, rms, rms_ref[...])
        scaled_ref[...] = half(dot(chain_ref[0], update_ref[0]))

    for index, chosen in enumerate(set_refs):
        pl.when((at >= first_count) == (index == 1))(functools.partial(make, *chosen))

    decayed = rows_ref[0] * (1.0 - learn_rate * weight_decay)
    new_rows_ref[0] = decayed - learn_rate * scaled_ref[:height].astype(jnp.float32)
    def write(lies):
        for block_at, (piece, where) in enumerate(lies):
            decayed = master_refs[piece][where, 0].astype(jnp.float32) * (
                1.0 - learn_rate * weight_decay
            )
            weights_ref[0, target(block_at)] = half(
                decayed - learn_rate * scaled_ref[span(block_at)].astype(jnp.float32)
            )

    for start, stop, lies in masters:
        pl.when((matrix >= start) & (matrix < stop))(functools.partial(write, lies))

    @pl.when(slot >= 0)
    def _():
        for block_at in range(blocks):
            owned_ref[jnp.maximum(slot, 0), target(block_at)] = scaled_ref[span(block_at)]


def applied(places, spans, slots, order, sets, master_pieces, masters, master):
    _, rows, width = sets[0][2].shape
    count, row_count, _ = master.shape
    first_count = sets[0][0].shape[0]

    def by_matrix(height, minor):
        def index(i, places, spans, slots, order):
            return (order[i], 0, 0)

        return pl.BlockSpec((1, height, minor), index)

    def by_piece(piece, start, depth):
        def index(i, places, spans, slots, order):
            return (0, jnp.clip(order[i] - start, 0, piece.shape[1] - 1), 0, 0)

        return pl.BlockSpec((depth, 1, *piece.shape[2:]), index)

    def by_step(array, start):
        last = array.shape[0] - 1

        def index(i, *_):
            return (jnp.clip(i - start, 0, last), 0, 0)

        return pl.BlockSpec((1, *array.shape[1:]), index)

    owned = (MOST, rows, width)
    return pl.pallas_call(
        functools.partial(apply_kernel, len(sets), first_count, masters),
        grid_spec=pltpu.PrefetchScalarGridSpec(
            num_scalar_prefetch=4,
            grid=(count,),
            in_specs=[
                by_step(array, at * first_count) for at, arrays in enumerate(sets) for array in arrays
            ]
            + [by_piece(*piece) for piece in master_pieces]
            + [by_matrix(row_count, width)],
            out_specs=[
                by_matrix(rows, width),
                by_matrix(row_count, width),
                pl.BlockSpec(owned, lambda i, *_: (0, 0, 0)),
                pl.BlockSpec((1, MOST), lambda i, *_: (0, 0)),
            ],
            scratch_shapes=[pltpu.VMEM((rows, width), jnp.bfloat16)],
        ),
        out_shape=[
            jax.ShapeDtypeStruct((count, rows, width), jnp.bfloat16),
            jax.ShapeDtypeStruct(master.shape, jnp.float32),
            jax.ShapeDtypeStruct(owned, jnp.bfloat16),
            jax.ShapeDtypeStruct((1, MOST), jnp.float32),
        ],
        compiler_params=pltpu.CompilerParams(vmem_limit_bytes=56 * MIB),
        cost_estimate=pl.CostEstimate(
            flops=2 * count * rows * rows * width,
            bytes_accessed=2 * count * rows * (4 * width + rows),
            transcendentals=0,
        ),
    )(
        places,
        spans,
        slots,
        order,
        *[array for arrays in sets for array in arrays],
        *[piece[0] for piece in master_pieces],
        master,
    )


class Grid:
    def __init__(self, count):
        self.count = count
        self.me = lax.axis_index("dp")
        self.x_pairs = [(d, d ^ 1) for d in range(count)]
        self.y_pairs = [(d, d ^ 2) for d in range(count)]

    def over_x(self, value):
        return lax.ppermute(value, "dp", self.x_pairs)

    def over_y(self, value):
        return lax.ppermute(value, "dp", self.y_pairs)

    def over_z(self, value, shift):
        pairs = [(d, (d // 4 + shift) % LINE * 4 + d % 4) for d in range(self.count)]
        return lax.ppermute(value, "dp", pairs)


def place(me, dx, dy, dz):
    z = ((me >> 2) + dz) & (LINE - 1)
    return z * 4 + ((me & 3) ^ (2 * dy + dx))


def after(value, *others):
    return lax.optimization_barrier((value, *others))[0]


def added(*values):
    return sum(value.astype(jnp.float32) for value in values)


class MasterGather:
    def __init__(self, grid, master):
        self.grid = grid
        self.lines = [[z * 4 + corner for z in range(LINE)] for corner in range(4)]
        self.split = master.shape[0] // 2
        self.own = half(master)
        self.line = lax.all_gather(self.own, "dp", axis_index_groups=self.lines)

    def near(self, *ties):
        middle = LINE // 2
        line = after(self.line, *ties)
        self.high = line[:, self.split :]
        low = self.own[None, : self.split]
        self.near_x = self.grid.over_x(jnp.concatenate([self.high[:middle], low]))
        self.near_y = self.grid.over_y(jnp.concatenate([self.high[middle:], low]))

    def low_plane(self):
        low_x, low_y = self.near_x[-1], self.near_y[-1]
        self.plane = jnp.stack([self.own[: self.split], low_y, low_x, self.grid.over_x(low_y)])

    def low_lines(self, *ties):
        low = lax.all_gather(after(self.plane, *ties), "dp", axis_index_groups=self.lines)
        self.low = low.reshape(4 * LINE, *low.shape[2:])

    def high_rest(self):
        middle = LINE // 2
        near_x, near_y = self.near_x[:middle], self.near_y[:middle]
        self.sent_x = jnp.concatenate([self.high[middle:], near_y])
        self.sent_y = jnp.concatenate([self.high[:middle], near_x])

    def send_rest(self, *ties):
        self.rest_x = self.grid.over_x(after(self.sent_x, *ties))
        self.rest_y = self.grid.over_y(after(self.sent_y, *ties))

    def pieces(self):
        high = [self.high, self.near_x, self.near_y, self.rest_x, self.rest_y]
        depths = [LINE, LINE // 2, LINE // 2, LINE, LINE]
        return [(self.low, 0, 4 * LINE)] + [
            (piece, self.split, depth) for piece, depth in zip(high, depths)
        ]

    def masters(self, matrices):
        low = [(0, z * 4 + at) for at in range(4) for z in range(LINE)]
        middle = LINE // 2
        halves = range(middle)
        high = [(1, z) for z in range(LINE)]
        high += [(5, z) for z in halves] + [(3, z) for z in halves]
        high += [(2, z) for z in halves] + [(4, z) for z in halves]
        high += [(5, middle + z) for z in halves] + [(4, middle + z) for z in halves]
        return [(0, self.split, low), (self.split, matrices, high)]

    def places(self):
        corner, z_mine = self.grid.me & 3, self.grid.me >> 2
        places = [
            z * 4 + (corner ^ (2 * dy + dx)) for dx in range(2) for dy in range(2) for z in range(LINE)
        ]
        spans = [at * 4 + ((z - z_mine) & (LINE - 1)) for at in range(4) for z in range(LINE)]
        return jnp.stack(places).astype(jnp.int32), jnp.stack(spans).astype(jnp.int32)


def reduce_scatter(grid, terms, row_count, master_gather):
    def term(me, dx, dy, dz):
        start = place(me, dx, dy, dz) * row_count
        return lax.dynamic_slice_in_dim(terms, start, row_count, axis=1)

    me = grid.me
    raw_far1, raw_far2 = term(me, 1, 1, 1), term(me, 1, 1, 2)
    me = after(grid.me, raw_far1, raw_far2, master_gather.own)
    raw_x1, raw_far3, raw_y2 = term(me, 1, 0, 1), term(me, 1, 1, 3), term(me, 0, 1, 2)
    raw_y3, raw_far0, raw_x0 = term(me, 0, 1, 3), term(me, 1, 1, 0), term(me, 1, 0, 0)
    far1 = grid.over_x(raw_far1)
    far2 = grid.over_y(raw_far2)
    along_x1 = grid.over_x(raw_x1)
    far3 = grid.over_y(raw_far3)
    along_y2 = grid.over_y(raw_y2)

    me = after(grid.me, far1, far2, raw_y3)
    sent_x2 = half(added(term(me, 1, 0, 2), far2))
    sent_y1 = half(added(term(me, 0, 1, 1), far1))
    along_x2 = grid.over_x(sent_x2)
    along_y1 = grid.over_y(sent_y1)

    me = after(grid.me, far3, along_x1, sent_x2, sent_y1)
    sent_x3 = half(added(term(me, 1, 0, 3), far3))
    along_x3 = grid.over_x(sent_x3)
    along_y3 = grid.over_y(after(raw_y3, far3, along_x1))

    me = after(grid.me, along_y2, along_x2, sent_x3)
    near2 = half(added(term(me, 0, 0, 2), along_x2, along_y2))
    line2 = grid.over_z(near2, 2)
    far0 = grid.over_x(after(raw_far0, along_x2))

    me = after(grid.me, along_x1, along_y1, along_x3, near2)
    near1 = half(added(term(me, 0, 0, 1), along_x1, along_y1))
    line1 = grid.over_z(near1, 1)
    along_x0 = grid.over_x(after(raw_x0, along_x3))

    me = after(grid.me, along_x3, along_y3, far0, near1)
    near3 = half(added(term(me, 0, 0, 3), along_x3, along_y3))
    sent_y0 = half(added(term(me, 0, 1, 0), far0))
    line3 = grid.over_z(near3, 3)
    master_gather.near(near3, sent_y0)
    along_y0 = grid.over_y(sent_y0)
    me = after(grid.me, near3, sent_y0, line2)
    return added(term(me, 0, 0, 0), along_x0, along_y0, line1, line2, line3)


def all_gather(grid, own, before_z2, before_x2):
    x0, y0 = grid.over_x(own), grid.over_y(own)
    z1, z3 = grid.over_z(own, LINE - 1), grid.over_z(own, 1)
    far0 = grid.over_x(y0)
    x1, y1 = grid.over_x(z1), grid.over_y(z1)
    x3, y3 = grid.over_x(z3), grid.over_y(z3)
    z2 = grid.over_z(after(own, z1, z3, *before_z2), 2)
    far3 = grid.over_y(x3)
    sent = after(z2, *before_x2)
    x2, y2 = grid.over_x(sent), grid.over_y(sent)
    far1 = grid.over_x(y1)
    far2 = grid.over_y(x2)
    return [own, z1, z2, z3, y0, y1, y2, y3, x0, x1, x2, x3, far0, far1, far2, far3]


def updated(summed, momentum):
    new_momentum = momentum_decay * momentum + summed
    return new_momentum, half(summed + momentum_decay * new_momentum)


def per_device(gradients, momentum, master, owners):
    me = lax.axis_index("dp")
    dp_count = lax.axis_size("dp")
    matrices, row_count, width = momentum.shape
    terms = gradients[0]
    held = owners == me
    index = jnp.arange(matrices)
    rank = jnp.sum(held[None, :] & (index[None, :] < index[:, None]), axis=1)
    slots = jnp.where(held, rank, -1).astype(jnp.int32)

    in_pieces = dp_count == 4 * LINE and row_count % 32 == 0
    if in_pieces:
        grid = Grid(dp_count)
        rows = master
        master_gather = MasterGather(grid, master)
        places, spans = master_gather.places()
        summed = reduce_scatter(grid, terms, row_count, master_gather)
        new_momentum, own = updated(summed, momentum)
        master_gather.low_plane()
        master_gather.high_rest()
        before_x2 = [master_gather.plane, master_gather.sent_x, master_gather.sent_y]
        pieces = all_gather(grid, own, [master_gather.near_x, master_gather.near_y], before_x2)
        master_gather.low_lines(*pieces[1:4])
        master_gather.send_rest(*pieces[1:])
        master_pieces, masters = master_gather.pieces(), master_gather.masters(matrices)
    else:
        places = spans = jnp.zeros((1,), jnp.int32)
        rows = jnp.zeros((matrices, terms.shape[1], width), jnp.float32)
        rows = lax.dynamic_update_slice_in_dim(rows, master, me * row_count, axis=1)
        summed = lax.psum_scatter(terms, "dp", scatter_dimension=1, tiled=True)
        new_momentum, own = updated(summed.astype(jnp.float32), momentum)
        master_pieces = [(lax.all_gather(half(master), "dp", axis=1, tiled=True)[None], 0, 1)]
        masters = [(0, matrices, [(0, 0)])]
        pieces = [lax.all_gather(own, "dp", axis=1, tiled=True)]

    order = jnp.arange(matrices, dtype=jnp.int32)
    if lax.axis_size("col") == 2 and matrices % 2 == 0:
        size = matrices // 2
        order = (order + lax.axis_index("col") * size) % matrices
        mine, theirs = order[:size], order[size:]
        their_update, their_gram = grams(pieces, theirs)
        swap = [(0, 1), (1, 0)]
        other_part = lax.ppermute(their_gram, "col", swap)
        my_update, my_gram = grams(pieces, mine)
        chain, squares = chains([my_gram, other_part])
        sent = chain
        if in_pieces:
            sent = after(chain, master_gather.rest_x, master_gather.rest_y)
        other = [lax.ppermute(sent, "col", swap), lax.ppermute(squares, "col", swap)]
        sets = [[chain, squares, my_update], [*other, their_update]]
    else:
        update, gram = grams(pieces, order)
        sets = [[*chains([lax.psum(gram, "col")]), update]]
    new_weights, new_master, owned_updates, rms = applied(
        places, spans, slots, order, sets, master_pieces, masters, rows
    )
    if not in_pieces:
        new_master = lax.dynamic_slice_in_dim(new_master, me * row_count, row_count, axis=1)
    return (new_weights, new_master, new_momentum, owned_updates[None], rms)


def solution(mesh):
    return jax.shard_map(
        per_device,
        mesh=mesh,
        in_specs=(P("dp", None, None, "col"), P(None, "dp", "col"), P(None, "dp", "col"), P()),
        out_specs=(
            P(None, None, "col"),
            P(None, "dp", "col"),
            P(None, "dp", "col"),
            P("dp", None, None, "col"),
            P("dp", None),
        ),
        check_vma=False,
    )
```

```python
import functools
import math

import jax
import jax.numpy as jnp
from jax import lax
from jax.experimental import pallas as pl
from jax.experimental.pallas import tpu as pltpu
from jax.sharding import PartitionSpec as P

KV = 512
D = 2048
MOST = 2

quintic_first = 3.4445
quintic_second = -4.775
quintic_third = 2.0315
momentum_decay = 0.95
learn_rate = 0.3
weight_decay = 0.1
epsilon = 1e-07
factor = 0.2 * math.sqrt(max(KV, D))

MIB = 1024 * 1024
LINE = 4


def dot(left, right):
    return jnp.dot(left, right, preferred_element_type=jnp.float32)


def half(value):
    return value.astype(jnp.bfloat16)


def gram_kernel(order_ref, *refs):
    piece_refs, (update_ref, gram_ref) = refs[:-2], refs[-2:]
    start = 0
    for ref in piece_refs:
        rows = ref.shape[1]
        update_ref[0, start : start + rows] = ref[0]
        start += rows
    block = update_ref[0]
    gram = lax.dot_general(
        block, block, (((1,), (1,)), ((), ())), preferred_element_type=jnp.float32
    )
    gram_ref[0] = half(gram)


def grams(pieces, order):
    width = pieces[0].shape[2]
    count = order.shape[0]
    rows = sum(piece.shape[1] for piece in pieces)

    def spec(minor):
        return pl.BlockSpec((1, rows, minor), lambda i, order: (i, 0, 0))

    return pl.pallas_call(
        gram_kernel,
        grid_spec=pltpu.PrefetchScalarGridSpec(
            num_scalar_prefetch=1,
            grid=(count,),
            in_specs=[
                pl.BlockSpec((1, *piece.shape[1:]), lambda i, order: (order[i], 0, 0))
                for piece in pieces
            ],
            out_specs=[spec(width), spec(rows)],
        ),
        out_shape=[
            jax.ShapeDtypeStruct((count, rows, width), jnp.bfloat16),
            jax.ShapeDtypeStruct((count, rows, rows), jnp.bfloat16),
        ],
        compiler_params=pltpu.CompilerParams(vmem_limit_bytes=56 * MIB),
        cost_estimate=pl.CostEstimate(
            flops=2 * count * rows * rows * width,
            bytes_accessed=2 * count * rows * (2 * width + rows),
            transcendentals=0,
        ),
    )(order, *pieces)


def mixers(grams_now):
    return [
        quintic_second * gram + quintic_third * dot(half(gram), half(gram)) for gram in grams_now
    ]


def next_grams(grams_now, mixes):
    lefts = [
        quintic_first * gram + dot(half(mix), half(gram)) for gram, mix in zip(grams_now, mixes)
    ]
    return [quintic_first * left + dot(half(left), half(mix)) for left, mix in zip(lefts, mixes)]


def chain_kernel(parts, *refs):
    gram_refs = refs[:parts]
    chain_ref, squares_ref = refs[parts:]
    count, rows, _ = chain_ref.shape
    on_diagonal = lax.broadcasted_iota(jnp.int32, (rows, rows), 0) == lax.broadcasted_iota(
        jnp.int32, (rows, rows), 1
    )
    grams_now = []
    inverses = []
    for index in range(count):
        gram = gram_refs[0][index].astype(jnp.float32)
        for ref in gram_refs[1:]:
            gram = gram + ref[index].astype(jnp.float32)
        diagonal = jnp.where(on_diagonal, gram, 0.0)
        squares = jnp.sum(jnp.sum(diagonal, axis=0, keepdims=True), axis=1, keepdims=True)
        squares_ref[index] = jnp.broadcast_to(squares, squares_ref.shape[1:])
        inverse = 1.0 / (jnp.sqrt(squares) + epsilon)
        grams_now.append(gram * inverse * inverse)
        inverses.append(inverse)
    first = mixers(grams_now)
    grams_now = next_grams(grams_now, first)
    second = mixers(grams_now)
    grams_now = next_grams(grams_now, second)
    third = mixers(grams_now)
    pairs = [
        quintic_first * (m0 + m1) + dot(half(m1), half(m0)) for m0, m1 in zip(first, second)
    ]
    cubed = jnp.where(on_diagonal, quintic_first**3, 0.0)
    for index, (pair, m2) in enumerate(zip(pairs, third)):
        whole = quintic_first * pair + quintic_first**2 * m2 + dot(half(m2), half(pair))
        chain_ref[index] = half((cubed + whole) * (factor * inverses[index]))


def chains(gram_parts):
    count, rows, _ = gram_parts[0].shape
    step = 3 if count % 3 == 0 else 1
    parts = len(gram_parts)
    spec = pl.BlockSpec((step, rows, rows), lambda i: (i, 0, 0))
    return pl.pallas_call(
        functools.partial(chain_kernel, parts),
        grid=(count // step,),
        in_specs=[spec] * parts,
        out_specs=[spec, pl.BlockSpec((step, 8, 128), lambda i: (i, 0, 0))],
        out_shape=[
            jax.ShapeDtypeStruct((count, rows, rows), jnp.bfloat16),
            jax.ShapeDtypeStruct((count, 8, 128), jnp.float32),
        ],
        compiler_params=pltpu.CompilerParams(vmem_limit_bytes=20 * MIB),
        cost_estimate=pl.CostEstimate(
            flops=18 * count * rows * rows * rows,
            bytes_accessed=2 * count * rows * rows * (parts + 1),
            transcendentals=0,
        ),
    )(*gram_parts)


def apply_kernel(sets, first_count, masters, places_ref, spans_ref, slots_ref, order_ref, *refs):
    set_refs = [refs[3 * at : 3 * at + 3] for at in range(sets)]
    master_refs = refs[3 * sets : -6]
    rows_ref, weights_ref, new_rows_ref, owned_ref, rms_ref, scaled_ref = refs[-6:]
    blocks = spans_ref.shape[0]
    height = scaled_ref.shape[0] // blocks
    at = pl.program_id(0)
    matrix = order_ref[at]
    slot = slots_ref[matrix]

    @pl.when(at == 0)
    def _():
        owned_ref[...] = jnp.zeros_like(owned_ref)
        rms_ref[...] = jnp.zeros_like(rms_ref)

    def target(block_at):
        return pl.ds(pl.multiple_of(places_ref[block_at] * height, height), height)

    def span(block_at):
        return pl.ds(pl.multiple_of(spans_ref[block_at] * height, height), height)

    lane = lax.broadcasted_iota(jnp.int32, rms_ref.shape, 1)

    def make(chain_ref, squares_ref, update_ref):
        rms = jnp.sqrt(squares_ref[0, :1, :1] / float(KV * D))
        rms_ref[...] = jnp.where(lane == slot, rms, rms_ref[...])
        scaled_ref[...] = half(dot(chain_ref[0], update_ref[0]))

    for index, chosen in enumerate(set_refs):
        pl.when((at >= first_count) == (index == 1))(functools.partial(make, *chosen))

    decayed = rows_ref[0] * (1.0 - learn_rate * weight_decay)
    new_rows_ref[0] = decayed - learn_rate * scaled_ref[:height].astype(jnp.float32)
    def write(lies):
        for block_at, (piece, where) in enumerate(lies):
            decayed = master_refs[piece][where, 0].astype(jnp.float32) * (
                1.0 - learn_rate * weight_decay
            )
            weights_ref[0, target(block_at)] = half(
                decayed - learn_rate * scaled_ref[span(block_at)].astype(jnp.float32)
            )

    for start, stop, lies in masters:
        pl.when((matrix >= start) & (matrix < stop))(functools.partial(write, lies))

    @pl.when(slot >= 0)
    def _():
        for block_at in range(blocks):
            owned_ref[jnp.maximum(slot, 0), target(block_at)] = scaled_ref[span(block_at)]


def applied(places, spans, slots, order, sets, master_pieces, masters, master):
    _, rows, width = sets[0][2].shape
    count, row_count, _ = master.shape
    first_count = sets[0][0].shape[0]

    def by_matrix(height, minor):
        def index(i, places, spans, slots, order):
            return (order[i], 0, 0)

        return pl.BlockSpec((1, height, minor), index)

    def by_piece(piece, start, depth):
        def index(i, places, spans, slots, order):
            return (0, jnp.clip(order[i] - start, 0, piece.shape[1] - 1), 0, 0)

        return pl.BlockSpec((depth, 1, *piece.shape[2:]), index)

    def by_step(array, start):
        last = array.shape[0] - 1

        def index(i, *_):
            return (jnp.clip(i - start, 0, last), 0, 0)

        return pl.BlockSpec((1, *array.shape[1:]), index)

    owned = (MOST, rows, width)
    return pl.pallas_call(
        functools.partial(apply_kernel, len(sets), first_count, masters),
        grid_spec=pltpu.PrefetchScalarGridSpec(
            num_scalar_prefetch=4,
            grid=(count,),
            in_specs=[
                by_step(array, at * first_count) for at, arrays in enumerate(sets) for array in arrays
            ]
            + [by_piece(*piece) for piece in master_pieces]
            + [by_matrix(row_count, width)],
            out_specs=[
                by_matrix(rows, width),
                by_matrix(row_count, width),
                pl.BlockSpec(owned, lambda i, *_: (0, 0, 0)),
                pl.BlockSpec((1, MOST), lambda i, *_: (0, 0)),
            ],
            scratch_shapes=[pltpu.VMEM((rows, width), jnp.bfloat16)],
        ),
        out_shape=[
            jax.ShapeDtypeStruct((count, rows, width), jnp.bfloat16),
            jax.ShapeDtypeStruct(master.shape, jnp.float32),
            jax.ShapeDtypeStruct(owned, jnp.bfloat16),
            jax.ShapeDtypeStruct((1, MOST), jnp.float32),
        ],
        compiler_params=pltpu.CompilerParams(vmem_limit_bytes=56 * MIB),
        cost_estimate=pl.CostEstimate(
            flops=2 * count * rows * rows * width,
            bytes_accessed=2 * count * rows * (4 * width + rows),
            transcendentals=0,
        ),
    )(
        places,
        spans,
        slots,
        order,
        *[array for arrays in sets for array in arrays],
        *[piece[0] for piece in master_pieces],
        master,
    )


class Grid:
    def __init__(self, count):
        self.count = count
        self.me = lax.axis_index("dp")
        self.x_pairs = [(d, d ^ 1) for d in range(count)]
        self.y_pairs = [(d, d ^ 2) for d in range(count)]

    def over_x(self, value):
        return lax.ppermute(value, "dp", self.x_pairs)

    def over_y(self, value):
        return lax.ppermute(value, "dp", self.y_pairs)

    def over_z(self, value, shift):
        pairs = [(d, (d // 4 + shift) % LINE * 4 + d % 4) for d in range(self.count)]
        return lax.ppermute(value, "dp", pairs)


def place(me, dx, dy, dz):
    z = ((me >> 2) + dz) & (LINE - 1)
    return z * 4 + ((me & 3) ^ (2 * dy + dx))


def after(value, *others):
    return lax.optimization_barrier((value, *others))[0]


def added(*values):
    return sum(value.astype(jnp.float32) for value in values)


class MasterGather:
    def __init__(self, grid, master):
        self.grid = grid
        self.lines = [[z * 4 + corner for z in range(LINE)] for corner in range(4)]
        self.split = master.shape[0] // 2
        self.own = half(master)
        self.line = lax.all_gather(self.own, "dp", axis_index_groups=self.lines)

    def near(self, *ties):
        line = after(self.line, *ties)
        self.high = line[:, self.split :]
        sent = jnp.concatenate([self.high, self.own[None, : self.split]])
        self.near_x = self.grid.over_x(sent)
        self.near_y = self.grid.over_y(sent)

    def low_plane(self):
        low_x, low_y = self.near_x[LINE], self.near_y[LINE]
        self.plane = jnp.stack([self.own[: self.split], low_y, low_x, self.grid.over_x(low_y)])

    def low_lines(self, *ties):
        low = lax.all_gather(after(self.plane, *ties), "dp", axis_index_groups=self.lines)
        self.low = low.reshape(4 * LINE, *low.shape[2:])

    def high_corners(self, *ties):
        self.far = self.grid.over_x(after(self.near_y, *ties)[:LINE])

    def pieces(self):
        high = [self.high, self.near_y, self.near_x, self.far]
        return [(self.low, 0, 4 * LINE)] + [(piece, self.split, LINE) for piece in high]

    def masters(self, matrices):
        low = [(0, z * 4 + at) for at in range(4) for z in range(LINE)]
        high = [(piece, z) for piece in (1, 2, 3, 4) for z in range(LINE)]
        return [(0, self.split, low), (self.split, matrices, high)]

    def places(self):
        corner, z_mine = self.grid.me & 3, self.grid.me >> 2
        places = [
            z * 4 + (corner ^ (2 * dy + dx)) for dx in range(2) for dy in range(2) for z in range(LINE)
        ]
        spans = [at * 4 + ((z - z_mine) & (LINE - 1)) for at in range(4) for z in range(LINE)]
        return jnp.stack(places).astype(jnp.int32), jnp.stack(spans).astype(jnp.int32)


def reduce_scatter(grid, terms, row_count, master_gather):
    def term(me, dx, dy, dz):
        start = place(me, dx, dy, dz) * row_count
        return lax.dynamic_slice_in_dim(terms, start, row_count, axis=1)

    me = grid.me
    raw_far1, raw_far2 = term(me, 1, 1, 1), term(me, 1, 1, 2)
    me = after(grid.me, raw_far1, raw_far2, master_gather.own)
    raw_x1, raw_far3, raw_y2 = term(me, 1, 0, 1), term(me, 1, 1, 3), term(me, 0, 1, 2)
    raw_y3, raw_far0, raw_x0 = term(me, 0, 1, 3), term(me, 1, 1, 0), term(me, 1, 0, 0)
    far1 = grid.over_x(raw_far1)
    far2 = grid.over_y(raw_far2)
    along_x1 = grid.over_x(raw_x1)
    far3 = grid.over_y(raw_far3)
    along_y2 = grid.over_y(raw_y2)

    me = after(grid.me, far1, far2, raw_y3)
    sent_x2 = half(added(term(me, 1, 0, 2), far2))
    sent_y1 = half(added(term(me, 0, 1, 1), far1))
    along_x2 = grid.over_x(sent_x2)
    along_y1 = grid.over_y(sent_y1)

    me = after(grid.me, far3, along_x1, sent_x2, sent_y1)
    sent_x3 = half(added(term(me, 1, 0, 3), far3))
    along_x3 = grid.over_x(sent_x3)
    along_y3 = grid.over_y(after(raw_y3, far3, along_x1))

    me = after(grid.me, along_y2, along_x2, sent_x3)
    near2 = half(added(term(me, 0, 0, 2), along_x2, along_y2))
    line2 = grid.over_z(near2, 2)
    far0 = grid.over_x(after(raw_far0, along_x2))

    me = after(grid.me, along_x1, along_y1, along_x3, near2)
    near1 = half(added(term(me, 0, 0, 1), along_x1, along_y1))
    line1 = grid.over_z(near1, 1)
    along_x0 = grid.over_x(after(raw_x0, along_x3))

    me = after(grid.me, along_x3, along_y3, far0, near1)
    near3 = half(added(term(me, 0, 0, 3), along_x3, along_y3))
    sent_y0 = half(added(term(me, 0, 1, 0), far0))
    line3 = grid.over_z(near3, 3)
    master_gather.near(near3, sent_y0)
    along_y0 = grid.over_y(sent_y0)
    me = after(grid.me, near3, sent_y0, line2)
    return added(term(me, 0, 0, 0), along_x0, along_y0, line1, line2, line3)


def all_gather(grid, own, before_x0, before_x2):
    z1, z3 = grid.over_z(own, LINE - 1), grid.over_z(own, 1)
    z2 = grid.over_z(own, 2)
    sent = after(own, *before_x0)
    x0, y0 = grid.over_x(sent), grid.over_y(sent)
    far0 = grid.over_x(y0)
    x1, y1 = grid.over_x(z1), grid.over_y(z1)
    x3, y3 = grid.over_x(z3), grid.over_y(z3)
    far3 = grid.over_y(x3)
    sent = after(z2, before_x2)
    x2, y2 = grid.over_x(sent), grid.over_y(sent)
    far1 = grid.over_x(y1)
    far2 = grid.over_y(x2)
    return [own, z1, z2, z3, y0, y1, y2, y3, x0, x1, x2, x3, far0, far1, far2, far3]


def updated(summed, momentum):
    new_momentum = momentum_decay * momentum + summed
    return new_momentum, half(summed + momentum_decay * new_momentum)


def per_device(gradients, momentum, master, owners):
    me = lax.axis_index("dp")
    dp_count = lax.axis_size("dp")
    matrices, row_count, width = momentum.shape
    terms = gradients[0]
    held = owners == me
    index = jnp.arange(matrices)
    rank = jnp.sum(held[None, :] & (index[None, :] < index[:, None]), axis=1)
    slots = jnp.where(held, rank, -1).astype(jnp.int32)

    in_pieces = dp_count == 4 * LINE and row_count % 32 == 0
    if in_pieces:
        grid = Grid(dp_count)
        rows = master
        master_gather = MasterGather(grid, master)
        places, spans = master_gather.places()
        summed = reduce_scatter(grid, terms, row_count, master_gather)
        new_momentum, own = updated(summed, momentum)
        master_gather.low_plane()
        pieces = all_gather(
            grid, own, (master_gather.near_x, master_gather.near_y), master_gather.plane
        )
        master_gather.low_lines(*pieces[1:4])
        master_gather.high_corners(*pieces[1:])
        master_pieces, masters = master_gather.pieces(), master_gather.masters(matrices)
    else:
        places = spans = jnp.zeros((1,), jnp.int32)
        rows = jnp.zeros((matrices, terms.shape[1], width), jnp.float32)
        rows = lax.dynamic_update_slice_in_dim(rows, master, me * row_count, axis=1)
        summed = lax.psum_scatter(terms, "dp", scatter_dimension=1, tiled=True)
        new_momentum, own = updated(summed.astype(jnp.float32), momentum)
        master_pieces = [(lax.all_gather(half(master), "dp", axis=1, tiled=True)[None], 0, 1)]
        masters = [(0, matrices, [(0, 0)])]
        pieces = [lax.all_gather(own, "dp", axis=1, tiled=True)]

    order = jnp.arange(matrices, dtype=jnp.int32)
    if lax.axis_size("col") == 2 and matrices % 2 == 0:
        size = matrices // 2
        order = (order + lax.axis_index("col") * size) % matrices
        mine, theirs = order[:size], order[size:]
        their_update, their_gram = grams(pieces, theirs)
        swap = [(0, 1), (1, 0)]
        other_part = lax.ppermute(their_gram, "col", swap)
        my_update, my_gram = grams(pieces, mine)
        chain, squares = chains([my_gram, other_part])
        sent = chain
        if in_pieces:
            sent = after(chain, master_gather.far)
        other = [lax.ppermute(sent, "col", swap), lax.ppermute(squares, "col", swap)]
        sets = [[chain, squares, my_update], [*other, their_update]]
    else:
        update, gram = grams(pieces, order)
        sets = [[*chains([lax.psum(gram, "col")]), update]]
    new_weights, new_master, owned_updates, rms = applied(
        places, spans, slots, order, sets, master_pieces, masters, rows
    )
    if not in_pieces:
        new_master = lax.dynamic_slice_in_dim(new_master, me * row_count, row_count, axis=1)
    return (new_weights, new_master, new_momentum, owned_updates[None], rms)


def solution(mesh):
    return jax.shard_map(
        per_device,
        mesh=mesh,
        in_specs=(P("dp", None, None, "col"), P(None, "dp", "col"), P(None, "dp", "col"), P()),
        out_specs=(
            P(None, None, "col"),
            P(None, "dp", "col"),
            P(None, "dp", "col"),
            P("dp", None, None, "col"),
            P("dp", None),
        ),
        check_vma=False,
    )
```

```python
import functools
import math

import jax
import jax.numpy as jnp
from jax import lax
from jax.experimental import pallas as pl
from jax.experimental.pallas import tpu as pltpu
from jax.sharding import PartitionSpec as P

KV = 512
D = 2048
MOST = 2

quintic_first = 3.4445
quintic_second = -4.775
quintic_third = 2.0315
momentum_decay = 0.95
learn_rate = 0.3
weight_decay = 0.1
epsilon = 1e-07
factor = 0.2 * math.sqrt(max(KV, D))

MIB = 1024 * 1024
LINE = 4


def dot(left, right):
    return jnp.dot(left, right, preferred_element_type=jnp.float32)


def half(value):
    return value.astype(jnp.bfloat16)


def gram_kernel(order_ref, *refs):
    piece_refs, (update_ref, gram_ref) = refs[:-2], refs[-2:]
    start = 0
    for ref in piece_refs:
        rows = ref.shape[1]
        update_ref[0, start : start + rows] = ref[0]
        start += rows
    block = update_ref[0]
    gram = lax.dot_general(
        block, block, (((1,), (1,)), ((), ())), preferred_element_type=jnp.float32
    )
    gram_ref[0] = half(gram)


def grams(pieces, order):
    width = pieces[0].shape[2]
    count = order.shape[0]
    rows = sum(piece.shape[1] for piece in pieces)

    def spec(minor):
        return pl.BlockSpec((1, rows, minor), lambda i, order: (i, 0, 0))

    return pl.pallas_call(
        gram_kernel,
        grid_spec=pltpu.PrefetchScalarGridSpec(
            num_scalar_prefetch=1,
            grid=(count,),
            in_specs=[
                pl.BlockSpec((1, *piece.shape[1:]), lambda i, order: (order[i], 0, 0))
                for piece in pieces
            ],
            out_specs=[spec(width), spec(rows)],
        ),
        out_shape=[
            jax.ShapeDtypeStruct((count, rows, width), jnp.bfloat16),
            jax.ShapeDtypeStruct((count, rows, rows), jnp.bfloat16),
        ],
        compiler_params=pltpu.CompilerParams(vmem_limit_bytes=56 * MIB),
        cost_estimate=pl.CostEstimate(
            flops=2 * count * rows * rows * width,
            bytes_accessed=2 * count * rows * (2 * width + rows),
            transcendentals=0,
        ),
    )(order, *pieces)


def mixers(grams_now):
    return [
        quintic_second * gram + quintic_third * dot(half(gram), half(gram)) for gram in grams_now
    ]


def next_grams(grams_now, mixes):
    lefts = [
        quintic_first * gram + dot(half(mix), half(gram)) for gram, mix in zip(grams_now, mixes)
    ]
    return [quintic_first * left + dot(half(left), half(mix)) for left, mix in zip(lefts, mixes)]


def chain_kernel(parts, *refs):
    gram_refs = refs[:parts]
    chain_ref, squares_ref = refs[parts:]
    count, rows, _ = chain_ref.shape
    on_diagonal = lax.broadcasted_iota(jnp.int32, (rows, rows), 0) == lax.broadcasted_iota(
        jnp.int32, (rows, rows), 1
    )
    grams_now = []
    inverses = []
    for index in range(count):
        gram = gram_refs[0][index].astype(jnp.float32)
        for ref in gram_refs[1:]:
            gram = gram + ref[index].astype(jnp.float32)
        diagonal = jnp.where(on_diagonal, gram, 0.0)
        squares = jnp.sum(jnp.sum(diagonal, axis=0, keepdims=True), axis=1, keepdims=True)
        squares_ref[index] = jnp.broadcast_to(squares, squares_ref.shape[1:])
        inverse = 1.0 / (jnp.sqrt(squares) + epsilon)
        grams_now.append(gram * inverse * inverse)
        inverses.append(inverse)
    first = mixers(grams_now)
    grams_now = next_grams(grams_now, first)
    second = mixers(grams_now)
    grams_now = next_grams(grams_now, second)
    third = mixers(grams_now)
    pairs = [
        quintic_first * (m0 + m1) + dot(half(m1), half(m0)) for m0, m1 in zip(first, second)
    ]
    cubed = jnp.where(on_diagonal, quintic_first**3, 0.0)
    for index, (pair, m2) in enumerate(zip(pairs, third)):
        whole = quintic_first * pair + quintic_first**2 * m2 + dot(half(m2), half(pair))
        chain_ref[index] = half((cubed + whole) * (factor * inverses[index]))


def chains(gram_parts):
    count, rows, _ = gram_parts[0].shape
    step = 3 if count % 3 == 0 else 1
    parts = len(gram_parts)
    spec = pl.BlockSpec((step, rows, rows), lambda i: (i, 0, 0))
    return pl.pallas_call(
        functools.partial(chain_kernel, parts),
        grid=(count // step,),
        in_specs=[spec] * parts,
        out_specs=[spec, pl.BlockSpec((step, 8, 128), lambda i: (i, 0, 0))],
        out_shape=[
            jax.ShapeDtypeStruct((count, rows, rows), jnp.bfloat16),
            jax.ShapeDtypeStruct((count, 8, 128), jnp.float32),
        ],
        compiler_params=pltpu.CompilerParams(vmem_limit_bytes=20 * MIB),
        cost_estimate=pl.CostEstimate(
            flops=18 * count * rows * rows * rows,
            bytes_accessed=2 * count * rows * rows * (parts + 1),
            transcendentals=0,
        ),
    )(*gram_parts)


def apply_kernel(sets, first_count, masters, places_ref, spans_ref, slots_ref, order_ref, *refs):
    set_refs = [refs[3 * at : 3 * at + 3] for at in range(sets)]
    master_refs = refs[3 * sets : -6]
    rows_ref, weights_ref, new_rows_ref, owned_ref, rms_ref, scaled_ref = refs[-6:]
    blocks = spans_ref.shape[0]
    height = scaled_ref.shape[0] // blocks
    at = pl.program_id(0)
    matrix = order_ref[at]
    slot = slots_ref[matrix]

    @pl.when(at == 0)
    def _():
        owned_ref[...] = jnp.zeros_like(owned_ref)
        rms_ref[...] = jnp.zeros_like(rms_ref)

    def target(block_at):
        return pl.ds(pl.multiple_of(places_ref[block_at] * height, height), height)

    def span(block_at):
        return pl.ds(pl.multiple_of(spans_ref[block_at] * height, height), height)

    lane = lax.broadcasted_iota(jnp.int32, rms_ref.shape, 1)

    def make(chain_ref, squares_ref, update_ref):
        rms = jnp.sqrt(squares_ref[0, :1, :1] / float(KV * D))
        rms_ref[...] = jnp.where(lane == slot, rms, rms_ref[...])
        scaled_ref[...] = half(dot(chain_ref[0], update_ref[0]))

    for index, chosen in enumerate(set_refs):
        pl.when((at >= first_count) == (index == 1))(functools.partial(make, *chosen))

    decayed = rows_ref[0] * (1.0 - learn_rate * weight_decay)
    new_rows_ref[0] = decayed - learn_rate * scaled_ref[:height].astype(jnp.float32)
    def write(lies):
        for block_at, (piece, where) in enumerate(lies):
            decayed = master_refs[piece][where, 0].astype(jnp.float32) * (
                1.0 - learn_rate * weight_decay
            )
            weights_ref[0, target(block_at)] = half(
                decayed - learn_rate * scaled_ref[span(block_at)].astype(jnp.float32)
            )

    for start, stop, lies in masters:
        pl.when((matrix >= start) & (matrix < stop))(functools.partial(write, lies))

    @pl.when(slot >= 0)
    def _():
        for block_at in range(blocks):
            owned_ref[jnp.maximum(slot, 0), target(block_at)] = scaled_ref[span(block_at)]


def applied(places, spans, slots, order, sets, master_pieces, masters, master):
    _, rows, width = sets[0][2].shape
    count, row_count, _ = master.shape
    first_count = sets[0][0].shape[0]

    def by_matrix(height, minor):
        def index(i, places, spans, slots, order):
            return (order[i], 0, 0)

        return pl.BlockSpec((1, height, minor), index)

    def by_piece(piece, start, depth):
        def index(i, places, spans, slots, order):
            return (0, jnp.clip(order[i] - start, 0, piece.shape[1] - 1), 0, 0)

        return pl.BlockSpec((depth, 1, *piece.shape[2:]), index)

    def by_step(array, start):
        last = array.shape[0] - 1

        def index(i, *_):
            return (jnp.clip(i - start, 0, last), 0, 0)

        return pl.BlockSpec((1, *array.shape[1:]), index)

    owned = (MOST, rows, width)
    return pl.pallas_call(
        functools.partial(apply_kernel, len(sets), first_count, masters),
        grid_spec=pltpu.PrefetchScalarGridSpec(
            num_scalar_prefetch=4,
            grid=(count,),
            in_specs=[
                by_step(array, at * first_count) for at, arrays in enumerate(sets) for array in arrays
            ]
            + [by_piece(*piece) for piece in master_pieces]
            + [by_matrix(row_count, width)],
            out_specs=[
                by_matrix(rows, width),
                by_matrix(row_count, width),
                pl.BlockSpec(owned, lambda i, *_: (0, 0, 0)),
                pl.BlockSpec((1, MOST), lambda i, *_: (0, 0)),
            ],
            scratch_shapes=[pltpu.VMEM((rows, width), jnp.bfloat16)],
        ),
        out_shape=[
            jax.ShapeDtypeStruct((count, rows, width), jnp.bfloat16),
            jax.ShapeDtypeStruct(master.shape, jnp.float32),
            jax.ShapeDtypeStruct(owned, jnp.bfloat16),
            jax.ShapeDtypeStruct((1, MOST), jnp.float32),
        ],
        compiler_params=pltpu.CompilerParams(vmem_limit_bytes=56 * MIB),
        cost_estimate=pl.CostEstimate(
            flops=2 * count * rows * rows * width,
            bytes_accessed=2 * count * rows * (4 * width + rows),
            transcendentals=0,
        ),
    )(
        places,
        spans,
        slots,
        order,
        *[array for arrays in sets for array in arrays],
        *[piece[0] for piece in master_pieces],
        master,
    )


class Grid:
    def __init__(self, count):
        self.count = count
        self.me = lax.axis_index("dp")
        self.x_pairs = [(d, d ^ 1) for d in range(count)]
        self.y_pairs = [(d, d ^ 2) for d in range(count)]

    def over_x(self, value):
        return lax.ppermute(value, "dp", self.x_pairs)

    def over_y(self, value):
        return lax.ppermute(value, "dp", self.y_pairs)

    def over_z(self, value, shift):
        pairs = [(d, (d // 4 + shift) % LINE * 4 + d % 4) for d in range(self.count)]
        return lax.ppermute(value, "dp", pairs)


def place(me, dx, dy, dz):
    z = ((me >> 2) + dz) & (LINE - 1)
    return z * 4 + ((me & 3) ^ (2 * dy + dx))


def after(value, *others):
    return lax.optimization_barrier((value, *others))[0]


def added(*values):
    return sum(value.astype(jnp.float32) for value in values)


class MasterGather:
    def __init__(self, grid, master):
        self.grid = grid
        self.lines = [[z * 4 + corner for z in range(LINE)] for corner in range(4)]
        self.split = master.shape[0] // 2
        self.own = half(master)
        self.line = lax.all_gather(self.own, "dp", axis_index_groups=self.lines)

    def near(self, *ties):
        line = after(self.line, *ties)
        self.high = line[:, self.split :]
        sent = jnp.concatenate([self.high, self.own[None, : self.split]])
        self.near_x = self.grid.over_x(sent)
        self.near_y = self.grid.over_y(sent)

    def low_plane(self):
        low_x, low_y = self.near_x[LINE], self.near_y[LINE]
        self.plane = jnp.stack([self.own[: self.split], low_y, low_x, self.grid.over_x(low_y)])

    def low_lines(self, *ties):
        low = lax.all_gather(after(self.plane, *ties), "dp", axis_index_groups=self.lines)
        self.low = low.reshape(4 * LINE, *low.shape[2:])

    def high_corners(self, *ties):
        self.far = self.grid.over_x(after(self.near_y, *ties)[:LINE])

    def pieces(self):
        high = [self.high, self.near_y, self.near_x, self.far]
        return [(self.low, 0, 4 * LINE)] + [(piece, self.split, LINE) for piece in high]

    def masters(self, matrices):
        low = [(0, z * 4 + at) for at in range(4) for z in range(LINE)]
        high = [(piece, z) for piece in (1, 2, 3, 4) for z in range(LINE)]
        return [(0, self.split, low), (self.split, matrices, high)]

    def places(self):
        corner, z_mine = self.grid.me & 3, self.grid.me >> 2
        places = [
            z * 4 + (corner ^ (2 * dy + dx)) for dx in range(2) for dy in range(2) for z in range(LINE)
        ]
        spans = [at * 4 + ((z - z_mine) & (LINE - 1)) for at in range(4) for z in range(LINE)]
        return jnp.stack(places).astype(jnp.int32), jnp.stack(spans).astype(jnp.int32)


def reduce_scatter(grid, terms, row_count, master_gather):
    def term(me, dx, dy, dz):
        start = place(me, dx, dy, dz) * row_count
        return lax.dynamic_slice_in_dim(terms, start, row_count, axis=1)

    me = grid.me
    raw_far1, raw_far2 = term(me, 1, 1, 1), term(me, 1, 1, 2)
    me = after(grid.me, raw_far1, raw_far2, master_gather.own)
    raw_x1, raw_far3, raw_y2 = term(me, 1, 0, 1), term(me, 1, 1, 3), term(me, 0, 1, 2)
    raw_y3, raw_far0, raw_x0 = term(me, 0, 1, 3), term(me, 1, 1, 0), term(me, 1, 0, 0)
    far1 = grid.over_x(raw_far1)
    far2 = grid.over_y(raw_far2)
    along_x1 = grid.over_x(raw_x1)
    far3 = grid.over_y(raw_far3)
    along_y2 = grid.over_y(raw_y2)

    ahead_at = [(1, 0, 2), (0, 1, 1), (1, 0, 3), (0, 0, 2), (0, 0, 1), (0, 0, 3), (0, 1, 0), (0, 0, 0)]
    me = after(grid.me, raw_y3)
    ahead = dict(zip(ahead_at, lax.optimization_barrier([term(me, *at) for at in ahead_at])))

    def ready(ties, *at):
        return after(ahead[at], *ties)

    ties = [far1, far2]
    sent_x2 = half(added(ready(ties, 1, 0, 2), far2))
    sent_y1 = half(added(ready(ties, 0, 1, 1), far1))
    along_x2 = grid.over_x(sent_x2)
    along_y1 = grid.over_y(sent_y1)

    ties = [far3, along_x1, sent_x2, sent_y1]
    sent_x3 = half(added(ready(ties, 1, 0, 3), far3))
    along_x3 = grid.over_x(sent_x3)
    along_y3 = grid.over_y(after(raw_y3, far3, along_x1))

    ties = [along_y2, along_x2, sent_x3]
    near2 = half(added(ready(ties, 0, 0, 2), along_x2, along_y2))
    line2 = grid.over_z(near2, 2)
    far0 = grid.over_x(after(raw_far0, along_x2))

    ties = [along_x1, along_y1, along_x3, near2, sent_x3]
    near1 = half(added(ready(ties, 0, 0, 1), along_x1, along_y1))
    line1 = grid.over_z(near1, 1)
    along_x0 = grid.over_x(after(raw_x0, near1))

    ties = [along_x3, along_y3, far0, near1]
    near3 = half(added(ready(ties, 0, 0, 3), along_x3, along_y3))
    sent_y0 = half(added(ready(ties, 0, 1, 0), far0))
    line3 = grid.over_z(near3, 3)
    master_gather.near(near3, sent_y0)
    along_y0 = grid.over_y(sent_y0)
    ties = [near3, sent_y0, line2]
    return added(ready(ties, 0, 0, 0), along_x0, along_y0, line1, line2, line3)


def all_gather(grid, own, before_z2, before_x2):
    x0, y0 = grid.over_x(own), grid.over_y(own)
    z1, z3 = grid.over_z(own, LINE - 1), grid.over_z(own, 1)
    far0 = grid.over_x(y0)
    x1, y1 = grid.over_x(z1), grid.over_y(z1)
    x3, y3 = grid.over_x(z3), grid.over_y(z3)
    z2 = grid.over_z(after(own, z1, z3, *before_z2), 2)
    far3 = grid.over_y(x3)
    sent = after(z2, before_x2)
    x2, y2 = grid.over_x(sent), grid.over_y(sent)
    far1 = grid.over_x(y1)
    far2 = grid.over_y(x2)
    return [own, z1, z2, z3, y0, y1, y2, y3, x0, x1, x2, x3, far0, far1, far2, far3]


def updated(summed, momentum):
    new_momentum = momentum_decay * momentum + summed
    return new_momentum, half(summed + momentum_decay * new_momentum)


def per_device(gradients, momentum, master, owners):
    me = lax.axis_index("dp")
    dp_count = lax.axis_size("dp")
    matrices, row_count, width = momentum.shape
    terms = gradients[0]
    held = owners == me
    index = jnp.arange(matrices)
    rank = jnp.sum(held[None, :] & (index[None, :] < index[:, None]), axis=1)
    slots = jnp.where(held, rank, -1).astype(jnp.int32)

    in_pieces = dp_count == 4 * LINE and row_count % 32 == 0
    if in_pieces:
        grid = Grid(dp_count)
        rows = master
        master_gather = MasterGather(grid, master)
        places, spans = master_gather.places()
        summed = reduce_scatter(grid, terms, row_count, master_gather)
        new_momentum, own = updated(summed, momentum)
        master_gather.low_plane()
        pieces = all_gather(
            grid, own, (master_gather.near_x, master_gather.near_y), master_gather.plane
        )
        master_gather.low_lines(*pieces[1:4])
        master_gather.high_corners(*pieces[1:])
        master_pieces, masters = master_gather.pieces(), master_gather.masters(matrices)
    else:
        places = spans = jnp.zeros((1,), jnp.int32)
        rows = jnp.zeros((matrices, terms.shape[1], width), jnp.float32)
        rows = lax.dynamic_update_slice_in_dim(rows, master, me * row_count, axis=1)
        summed = lax.psum_scatter(terms, "dp", scatter_dimension=1, tiled=True)
        new_momentum, own = updated(summed.astype(jnp.float32), momentum)
        master_pieces = [(lax.all_gather(half(master), "dp", axis=1, tiled=True)[None], 0, 1)]
        masters = [(0, matrices, [(0, 0)])]
        pieces = [lax.all_gather(own, "dp", axis=1, tiled=True)]

    order = jnp.arange(matrices, dtype=jnp.int32)
    if lax.axis_size("col") == 2 and matrices % 2 == 0:
        size = matrices // 2
        order = (order + lax.axis_index("col") * size) % matrices
        mine, theirs = order[:size], order[size:]
        their_update, their_gram = grams(pieces, theirs)
        swap = [(0, 1), (1, 0)]
        other_part = lax.ppermute(their_gram, "col", swap)
        my_update, my_gram = grams(pieces, mine)
        chain, squares = chains([my_gram, other_part])
        sent = chain
        if in_pieces:
            sent = after(chain, master_gather.far)
        other = [lax.ppermute(sent, "col", swap), lax.ppermute(squares, "col", swap)]
        sets = [[chain, squares, my_update], [*other, their_update]]
    else:
        update, gram = grams(pieces, order)
        sets = [[*chains([lax.psum(gram, "col")]), update]]
    new_weights, new_master, owned_updates, rms = applied(
        places, spans, slots, order, sets, master_pieces, masters, rows
    )
    if not in_pieces:
        new_master = lax.dynamic_slice_in_dim(new_master, me * row_count, row_count, axis=1)
    return (new_weights, new_master, new_momentum, owned_updates[None], rms)


def solution(mesh):
    return jax.shard_map(
        per_device,
        mesh=mesh,
        in_specs=(P("dp", None, None, "col"), P(None, "dp", "col"), P(None, "dp", "col"), P()),
        out_specs=(
            P(None, None, "col"),
            P(None, "dp", "col"),
            P(None, "dp", "col"),
            P("dp", None, None, "col"),
            P("dp", None),
        ),
        check_vma=False,
    )
```

```python
import functools
import math

import jax
import jax.numpy as jnp
from jax import lax
from jax.experimental import pallas as pl
from jax.experimental.pallas import tpu as pltpu
from jax.sharding import PartitionSpec as P

KV = 512
D = 2048
MOST = 2

quintic_first = 3.4445
quintic_second = -4.775
quintic_third = 2.0315
momentum_decay = 0.95
learn_rate = 0.3
weight_decay = 0.1
epsilon = 1e-07
factor = 0.2 * math.sqrt(max(KV, D))

MIB = 1024 * 1024
LINE = 4


def dot(left, right):
    return jnp.dot(left, right, preferred_element_type=jnp.float32)


def half(value):
    return value.astype(jnp.bfloat16)


def gram_kernel(order_ref, *refs):
    piece_refs, (update_ref, gram_ref) = refs[:-2], refs[-2:]
    start = 0
    for ref in piece_refs:
        rows = ref.shape[1]
        update_ref[0, start : start + rows] = ref[0]
        start += rows
    block = update_ref[0]
    gram = lax.dot_general(
        block, block, (((1,), (1,)), ((), ())), preferred_element_type=jnp.float32
    )
    gram_ref[0] = half(gram)


def grams(pieces, order):
    width = pieces[0].shape[2]
    count = order.shape[0]
    rows = sum(piece.shape[1] for piece in pieces)

    def spec(minor):
        return pl.BlockSpec((1, rows, minor), lambda i, order: (i, 0, 0))

    return pl.pallas_call(
        gram_kernel,
        grid_spec=pltpu.PrefetchScalarGridSpec(
            num_scalar_prefetch=1,
            grid=(count,),
            in_specs=[
                pl.BlockSpec((1, *piece.shape[1:]), lambda i, order: (order[i], 0, 0))
                for piece in pieces
            ],
            out_specs=[spec(width), spec(rows)],
        ),
        out_shape=[
            jax.ShapeDtypeStruct((count, rows, width), jnp.bfloat16),
            jax.ShapeDtypeStruct((count, rows, rows), jnp.bfloat16),
        ],
        compiler_params=pltpu.CompilerParams(vmem_limit_bytes=56 * MIB),
        cost_estimate=pl.CostEstimate(
            flops=2 * count * rows * rows * width,
            bytes_accessed=2 * count * rows * (2 * width + rows),
            transcendentals=0,
        ),
    )(order, *pieces)


def mixers(grams_now):
    return [
        quintic_second * gram + quintic_third * dot(half(gram), half(gram)) for gram in grams_now
    ]


def next_grams(grams_now, mixes):
    lefts = [
        quintic_first * gram + dot(half(mix), half(gram)) for gram, mix in zip(grams_now, mixes)
    ]
    return [quintic_first * left + dot(half(left), half(mix)) for left, mix in zip(lefts, mixes)]


def chain_kernel(parts, *refs):
    gram_refs = refs[:parts]
    chain_ref, squares_ref = refs[parts:]
    count, rows, _ = chain_ref.shape
    on_diagonal = lax.broadcasted_iota(jnp.int32, (rows, rows), 0) == lax.broadcasted_iota(
        jnp.int32, (rows, rows), 1
    )
    grams_now = []
    inverses = []
    for index in range(count):
        gram = gram_refs[0][index].astype(jnp.float32)
        for ref in gram_refs[1:]:
            gram = gram + ref[index].astype(jnp.float32)
        diagonal = jnp.where(on_diagonal, gram, 0.0)
        squares = jnp.sum(jnp.sum(diagonal, axis=0, keepdims=True), axis=1, keepdims=True)
        squares_ref[index] = jnp.broadcast_to(squares, squares_ref.shape[1:])
        inverse = 1.0 / (jnp.sqrt(squares) + epsilon)
        grams_now.append(gram * inverse * inverse)
        inverses.append(inverse)
    first = mixers(grams_now)
    grams_now = next_grams(grams_now, first)
    second = mixers(grams_now)
    grams_now = next_grams(grams_now, second)
    third = mixers(grams_now)
    pairs = [
        quintic_first * (m0 + m1) + dot(half(m1), half(m0)) for m0, m1 in zip(first, second)
    ]
    cubed = jnp.where(on_diagonal, quintic_first**3, 0.0)
    for index, (pair, m2) in enumerate(zip(pairs, third)):
        whole = quintic_first * pair + quintic_first**2 * m2 + dot(half(m2), half(pair))
        chain_ref[index] = half((cubed + whole) * (factor * inverses[index]))


def chains(gram_parts):
    count, rows, _ = gram_parts[0].shape
    step = 3 if count % 3 == 0 else 1
    parts = len(gram_parts)
    spec = pl.BlockSpec((step, rows, rows), lambda i: (i, 0, 0))
    return pl.pallas_call(
        functools.partial(chain_kernel, parts),
        grid=(count // step,),
        in_specs=[spec] * parts,
        out_specs=[spec, pl.BlockSpec((step, 8, 128), lambda i: (i, 0, 0))],
        out_shape=[
            jax.ShapeDtypeStruct((count, rows, rows), jnp.bfloat16),
            jax.ShapeDtypeStruct((count, 8, 128), jnp.float32),
        ],
        compiler_params=pltpu.CompilerParams(vmem_limit_bytes=20 * MIB),
        cost_estimate=pl.CostEstimate(
            flops=18 * count * rows * rows * rows,
            bytes_accessed=2 * count * rows * rows * (parts + 1),
            transcendentals=0,
        ),
    )(*gram_parts)


def apply_kernel(sets, first_count, masters, places_ref, spans_ref, slots_ref, order_ref, *refs):
    set_refs = [refs[3 * at : 3 * at + 3] for at in range(sets)]
    master_refs = refs[3 * sets : -6]
    rows_ref, weights_ref, new_rows_ref, owned_ref, rms_ref, scaled_ref = refs[-6:]
    blocks = spans_ref.shape[0]
    height = scaled_ref.shape[0] // blocks
    at = pl.program_id(0)
    matrix = order_ref[at]
    slot = slots_ref[matrix]

    @pl.when(at == 0)
    def _():
        owned_ref[...] = jnp.zeros_like(owned_ref)
        rms_ref[...] = jnp.zeros_like(rms_ref)

    def target(block_at):
        return pl.ds(pl.multiple_of(places_ref[block_at] * height, height), height)

    def span(block_at):
        return pl.ds(pl.multiple_of(spans_ref[block_at] * height, height), height)

    lane = lax.broadcasted_iota(jnp.int32, rms_ref.shape, 1)

    def make(chain_ref, squares_ref, update_ref):
        rms = jnp.sqrt(squares_ref[0, :1, :1] / float(KV * D))
        rms_ref[...] = jnp.where(lane == slot, rms, rms_ref[...])
        scaled_ref[...] = half(dot(chain_ref[0], update_ref[0]))

    for index, chosen in enumerate(set_refs):
        pl.when((at >= first_count) == (index == 1))(functools.partial(make, *chosen))

    decayed = rows_ref[0] * (1.0 - learn_rate * weight_decay)
    new_rows_ref[0] = decayed - learn_rate * scaled_ref[:height].astype(jnp.float32)
    def write(lies):
        for block_at, (piece, where) in enumerate(lies):
            decayed = master_refs[piece][where, 0].astype(jnp.float32) * (
                1.0 - learn_rate * weight_decay
            )
            weights_ref[0, target(block_at)] = half(
                decayed - learn_rate * scaled_ref[span(block_at)].astype(jnp.float32)
            )

    for start, stop, lies in masters:
        pl.when((matrix >= start) & (matrix < stop))(functools.partial(write, lies))

    @pl.when(slot >= 0)
    def _():
        for block_at in range(blocks):
            owned_ref[jnp.maximum(slot, 0), target(block_at)] = scaled_ref[span(block_at)]


def applied(places, spans, slots, order, sets, master_pieces, masters, master):
    _, rows, width = sets[0][2].shape
    count, row_count, _ = master.shape
    first_count = sets[0][0].shape[0]

    def by_matrix(height, minor):
        def index(i, places, spans, slots, order):
            return (order[i], 0, 0)

        return pl.BlockSpec((1, height, minor), index)

    def by_piece(piece, start, depth):
        def index(i, places, spans, slots, order):
            return (0, jnp.clip(order[i] - start, 0, piece.shape[1] - 1), 0, 0)

        return pl.BlockSpec((depth, 1, *piece.shape[2:]), index)

    def by_step(array, start):
        last = array.shape[0] - 1

        def index(i, *_):
            return (jnp.clip(i - start, 0, last), 0, 0)

        return pl.BlockSpec((1, *array.shape[1:]), index)

    owned = (MOST, rows, width)
    return pl.pallas_call(
        functools.partial(apply_kernel, len(sets), first_count, masters),
        grid_spec=pltpu.PrefetchScalarGridSpec(
            num_scalar_prefetch=4,
            grid=(count,),
            in_specs=[
                by_step(array, at * first_count) for at, arrays in enumerate(sets) for array in arrays
            ]
            + [by_piece(*piece) for piece in master_pieces]
            + [by_matrix(row_count, width)],
            out_specs=[
                by_matrix(rows, width),
                by_matrix(row_count, width),
                pl.BlockSpec(owned, lambda i, *_: (0, 0, 0)),
                pl.BlockSpec((1, MOST), lambda i, *_: (0, 0)),
            ],
            scratch_shapes=[pltpu.VMEM((rows, width), jnp.bfloat16)],
        ),
        out_shape=[
            jax.ShapeDtypeStruct((count, rows, width), jnp.bfloat16),
            jax.ShapeDtypeStruct(master.shape, jnp.float32),
            jax.ShapeDtypeStruct(owned, jnp.bfloat16),
            jax.ShapeDtypeStruct((1, MOST), jnp.float32),
        ],
        compiler_params=pltpu.CompilerParams(vmem_limit_bytes=56 * MIB),
        cost_estimate=pl.CostEstimate(
            flops=2 * count * rows * rows * width,
            bytes_accessed=2 * count * rows * (4 * width + rows),
            transcendentals=0,
        ),
    )(
        places,
        spans,
        slots,
        order,
        *[array for arrays in sets for array in arrays],
        *[piece[0] for piece in master_pieces],
        master,
    )


class Grid:
    def __init__(self, count):
        self.count = count
        self.me = lax.axis_index("dp")
        self.x_pairs = [(d, d ^ 1) for d in range(count)]
        self.y_pairs = [(d, d ^ 2) for d in range(count)]

    def over_x(self, value):
        return lax.ppermute(value, "dp", self.x_pairs)

    def over_y(self, value):
        return lax.ppermute(value, "dp", self.y_pairs)

    def over_z(self, value, shift):
        pairs = [(d, (d // 4 + shift) % LINE * 4 + d % 4) for d in range(self.count)]
        return lax.ppermute(value, "dp", pairs)


def place(me, dx, dy, dz):
    z = ((me >> 2) + dz) & (LINE - 1)
    return z * 4 + ((me & 3) ^ (2 * dy + dx))


def after(value, *others):
    return lax.optimization_barrier((value, *others))[0]


def added(*values):
    return sum(value.astype(jnp.float32) for value in values)


class MasterGather:
    def __init__(self, grid, master):
        self.grid = grid
        self.lines = [[z * 4 + corner for z in range(LINE)] for corner in range(4)]
        self.split = master.shape[0] // 2
        self.own = half(master)
        self.line = lax.all_gather(self.own, "dp", axis_index_groups=self.lines)

    def near(self, *ties):
        line = after(self.line, *ties)
        self.high = line[:, self.split :]
        sent = jnp.concatenate([self.high, self.own[None, : self.split]])
        self.near_x = self.grid.over_x(sent)
        self.near_y = self.grid.over_y(sent)

    def low_plane(self):
        low_x, low_y = self.near_x[LINE], self.near_y[LINE]
        self.plane = jnp.stack([self.own[: self.split], low_y, low_x, self.grid.over_x(low_y)])

    def low_lines(self, *ties):
        low = lax.all_gather(after(self.plane, *ties), "dp", axis_index_groups=self.lines)
        self.low = low.reshape(4 * LINE, *low.shape[2:])

    def high_corners(self, *ties):
        self.far = self.grid.over_x(after(self.near_y, *ties)[:LINE])

    def pieces(self):
        high = [self.high, self.near_y, self.near_x, self.far]
        return [(self.low, 0, 4 * LINE)] + [(piece, self.split, LINE) for piece in high]

    def masters(self, matrices):
        low = [(0, z * 4 + at) for at in range(4) for z in range(LINE)]
        high = [(piece, z) for piece in (1, 2, 3, 4) for z in range(LINE)]
        return [(0, self.split, low), (self.split, matrices, high)]

    def places(self):
        corner, z_mine = self.grid.me & 3, self.grid.me >> 2
        places = [
            z * 4 + (corner ^ (2 * dy + dx)) for dx in range(2) for dy in range(2) for z in range(LINE)
        ]
        spans = [at * 4 + ((z - z_mine) & (LINE - 1)) for at in range(4) for z in range(LINE)]
        return jnp.stack(places).astype(jnp.int32), jnp.stack(spans).astype(jnp.int32)


def reduce_scatter(grid, terms, row_count, master_gather):
    def term(me, dx, dy, dz):
        start = place(me, dx, dy, dz) * row_count
        return lax.dynamic_slice_in_dim(terms, start, row_count, axis=1)

    own = after(master_gather.own, grid.me)
    terms = after(terms, own)
    me = grid.me
    raw_far1, raw_far2 = term(me, 1, 1, 1), term(me, 1, 1, 2)
    me = after(grid.me, raw_far1, raw_far2, master_gather.own)
    raw_x1, raw_far3, raw_y2 = term(me, 1, 0, 1), term(me, 1, 1, 3), term(me, 0, 1, 2)
    raw_y3, raw_far0, raw_x0 = term(me, 0, 1, 3), term(me, 1, 1, 0), term(me, 1, 0, 0)
    far1 = grid.over_x(raw_far1)
    far2 = grid.over_y(raw_far2)
    along_x1 = grid.over_x(raw_x1)
    far3 = grid.over_y(raw_far3)
    along_y2 = grid.over_y(raw_y2)

    ahead_at = [(1, 0, 2), (0, 1, 1), (1, 0, 3), (0, 0, 2), (0, 0, 1), (0, 0, 3), (0, 1, 0), (0, 0, 0)]
    me = after(grid.me, raw_y3)
    ahead = dict(zip(ahead_at, lax.optimization_barrier([term(me, *at) for at in ahead_at])))

    def ready(ties, *at):
        return after(ahead[at], *ties)

    ties = [far1, far2]
    sent_x2 = half(added(ready(ties, 1, 0, 2), far2))
    sent_y1 = half(added(ready(ties, 0, 1, 1), far1))
    along_x2 = grid.over_x(sent_x2)
    along_y1 = grid.over_y(sent_y1)

    ties = [far3, along_x1, sent_x2, sent_y1]
    sent_x3 = half(added(ready(ties, 1, 0, 3), far3))
    along_x3 = grid.over_x(sent_x3)
    along_y3 = grid.over_y(after(raw_y3, far3, along_x1))

    ties = [along_y2, along_x2, sent_x3]
    near2 = half(added(ready(ties, 0, 0, 2), along_x2, along_y2))
    line2 = grid.over_z(near2, 2)
    far0 = grid.over_x(after(raw_far0, along_x2))

    ties = [along_x1, along_y1, along_x3, near2, sent_x3]
    near1 = half(added(ready(ties, 0, 0, 1), along_x1, along_y1))
    line1 = grid.over_z(near1, 1)
    along_x0 = grid.over_x(after(raw_x0, near1))

    ties = [along_x3, along_y3, far0, near1]
    near3 = half(added(ready(ties, 0, 0, 3), along_x3, along_y3))
    sent_y0 = half(added(ready(ties, 0, 1, 0), far0))
    line3 = grid.over_z(near3, 3)
    master_gather.near(near3, sent_y0)
    along_y0 = grid.over_y(sent_y0)
    ties = [near3, sent_y0, line2]
    return added(ready(ties, 0, 0, 0), along_x0, along_y0, line1, line2, line3)


def all_gather(grid, own, before_z2, before_x2):
    x0, y0 = grid.over_x(own), grid.over_y(own)
    z1, z3 = grid.over_z(own, LINE - 1), grid.over_z(own, 1)
    far0 = grid.over_x(y0)
    x1, y1 = grid.over_x(z1), grid.over_y(z1)
    x3, y3 = grid.over_x(z3), grid.over_y(z3)
    z2 = grid.over_z(after(own, z1, z3, *before_z2), 2)
    far3 = grid.over_y(x3)
    sent = after(z2, before_x2)
    x2, y2 = grid.over_x(sent), grid.over_y(sent)
    far1 = grid.over_x(y1)
    far2 = grid.over_y(x2)
    return [own, z1, z2, z3, y0, y1, y2, y3, x0, x1, x2, x3, far0, far1, far2, far3]


def updated(summed, momentum):
    new_momentum = momentum_decay * momentum + summed
    return new_momentum, half(summed + momentum_decay * new_momentum)


def per_device(gradients, momentum, master, owners):
    me = lax.axis_index("dp")
    dp_count = lax.axis_size("dp")
    matrices, row_count, width = momentum.shape
    terms = gradients[0]
    held = owners == me
    index = jnp.arange(matrices)
    rank = jnp.sum(held[None, :] & (index[None, :] < index[:, None]), axis=1)
    slots = jnp.where(held, rank, -1).astype(jnp.int32)

    in_pieces = dp_count == 4 * LINE and row_count % 32 == 0
    if in_pieces:
        grid = Grid(dp_count)
        rows = master
        master_gather = MasterGather(grid, master)
        places, spans = master_gather.places()
        summed = reduce_scatter(grid, terms, row_count, master_gather)
        new_momentum, own = updated(summed, momentum)
        master_gather.low_plane()
        pieces = all_gather(
            grid, own, (master_gather.near_x, master_gather.near_y), master_gather.plane
        )
        master_gather.low_lines(*pieces[1:4])
        master_gather.high_corners(*pieces[1:])
        master_pieces, masters = master_gather.pieces(), master_gather.masters(matrices)
    else:
        places = spans = jnp.zeros((1,), jnp.int32)
        rows = jnp.zeros((matrices, terms.shape[1], width), jnp.float32)
        rows = lax.dynamic_update_slice_in_dim(rows, master, me * row_count, axis=1)
        summed = lax.psum_scatter(terms, "dp", scatter_dimension=1, tiled=True)
        new_momentum, own = updated(summed.astype(jnp.float32), momentum)
        master_pieces = [(lax.all_gather(half(master), "dp", axis=1, tiled=True)[None], 0, 1)]
        masters = [(0, matrices, [(0, 0)])]
        pieces = [lax.all_gather(own, "dp", axis=1, tiled=True)]

    order = jnp.arange(matrices, dtype=jnp.int32)
    if lax.axis_size("col") == 2 and matrices % 2 == 0:
        size = matrices // 2
        order = (order + lax.axis_index("col") * size) % matrices
        mine, theirs = order[:size], order[size:]
        their_update, their_gram = grams(pieces, theirs)
        swap = [(0, 1), (1, 0)]
        other_part = lax.ppermute(their_gram, "col", swap)
        my_update, my_gram = grams(pieces, mine)
        chain, squares = chains([my_gram, other_part])
        sent = chain
        if in_pieces:
            sent = after(chain, master_gather.far)
        other = [lax.ppermute(sent, "col", swap), lax.ppermute(squares, "col", swap)]
        sets = [[chain, squares, my_update], [*other, their_update]]
    else:
        update, gram = grams(pieces, order)
        sets = [[*chains([lax.psum(gram, "col")]), update]]
    new_weights, new_master, owned_updates, rms = applied(
        places, spans, slots, order, sets, master_pieces, masters, rows
    )
    if not in_pieces:
        new_master = lax.dynamic_slice_in_dim(new_master, me * row_count, row_count, axis=1)
    return (new_weights, new_master, new_momentum, owned_updates[None], rms)


def solution(mesh):
    return jax.shard_map(
        per_device,
        mesh=mesh,
        in_specs=(P("dp", None, None, "col"), P(None, "dp", "col"), P(None, "dp", "col"), P()),
        out_specs=(
            P(None, None, "col"),
            P(None, "dp", "col"),
            P(None, "dp", "col"),
            P("dp", None, None, "col"),
            P("dp", None),
        ),
        check_vma=False,
    )
```
